32 devices in a mesh: batch: 8 (over z, x), rows: 4 (over y, core).
Axes of the slice: x: 2, y: 2, z: 4, core: 2. Of those that a mesh axis runs over, the one named last changes fastest.
Arguments:
- features: float32 [8, 16, 40, 2048], P('batch', 'rows'), may hold values from -25 to 25
- reduce_weight: float32 [2048, 512], P('batch'), may hold values from -0.125 to 0.125
- reduce_norm: float32 [2, 512], P(None, 'batch'), may hold values from -1.5 to 1.5
- dilate_weight: float32 [4608, 512], P('batch'), may hold values from -0.09375 to 0.09375
- dilate_norm: float32 [2, 512], P(None, 'batch'), may hold values from -1.5 to 1.5
- expand_weight: float32 [512, 2048], P('batch'), may hold values from -0.25 to 0.25
- expand_norm: float32 [2, 2048], P(None, 'batch'), may hold values from -1.5 to 1.5
- depth_head: float32 [4608, 512], P('batch'), may hold values from -0.09375 to 0.09375
- segment_head: float32 [4608, 512], P('batch'), may hold values from -0.09375 to 0.09375
- normal_head: float32 [4608, 512], P('batch'), may hold values from -0.09375 to 0.09375
- contour_head: float32 [4608, 512], P('batch'), may hold values from -0.09375 to 0.09375
- depth_message: float32 [4608, 512], P('batch'), may hold values from -0.0625 to 0.0625
- segment_message: float32 [4608, 512], P('batch'), may hold values from -0.0625 to 0.0625
- normal_message: float32 [4608, 512], P('batch'), may hold values from -0.0625 to 0.0625
- contour_message: float32 [4608, 512], P('batch'), may hold values from -0.0625 to 0.0625
- depth_gate: float32 [512, 512], P('batch'), may hold values from -0.25 to 0.25
- segment_gate: float32 [512, 512], P('batch'), may hold values from -0.25 to 0.25
- classifier: float32 [512, 40], P('batch'), may hold values from -0.5 to 0.5
- depth_valid: int32 [8, 16, 40], P('batch', 'rows'), may hold values from 0 to 1, as said below
- labels: int32 [8, 16, 40], P('batch', 'rows'), may hold values from 0 to 39
- block_cotangent: float32 [8, 16, 40, 2048], P('batch', 'rows'), may hold values from -6 to 6
- depth_cotangent: float32 [8, 16, 40, 512], P('batch', 'rows'), may hold values from -1.75 to 1.75
Outputs:
- block_out: float32 [8, 16, 40, 2048], P('batch', 'rows')
- depth_stream: float32 [8, 16, 40, 512], P('batch', 'rows')
- segment_stream: float32 [8, 16, 40, 512], P('batch', 'rows')
- features_grad: float32 [8, 16, 40, 2048], P('batch', 'rows')
- reduce_weight_grad: float32 [2048, 512], P('batch')
- reduce_norm_grad: float32 [2, 512], P(None, 'batch')
- dilate_weight_grad: float32 [4608, 512], P('batch')
- dilate_norm_grad: float32 [2, 512], P(None, 'batch')
- expand_weight_grad: float32 [512, 2048], P('batch')
- expand_norm_grad: float32 [2, 2048], P(None, 'batch')
- depth_head_grad: float32 [4608, 512], P('batch')
- segment_head_grad: float32 [4608, 512], P('batch')
- normal_head_grad: float32 [4608, 512], P('batch')
- contour_head_grad: float32 [4608, 512], P('batch')
- depth_message_grad: float32 [4608, 512], P('batch')
- segment_message_grad: float32 [4608, 512], P('batch')
- normal_message_grad: float32 [4608, 512], P('batch')
- contour_message_grad: float32 [4608, 512], P('batch')
- depth_gate_grad: float32 [512, 512], P('batch')
- segment_gate_grad: float32 [512, 512], P('batch')
- classifier_grad: float32 [512, 40], P('batch')
The draws below stay inside these ranges and needn't reach their ends.
Inputs may be any that keep to these rules, and one draw needn't show every extreme that they name: `depth_valid`: every image has a valid pixel at its first row and first column.
All inputs are finite; a program needn't handle non-finite values.
Results may differ from the reference program's by a relative error of at most 0.0003.
Values sent between devices are 32-bit elements; how exact they have to be, the bound alone decides.
No kernel may reach another device: no remote copies, remote signals or barrier semaphores. Data moves between devices by JAX's collectives and lax.ppermute only.
A program may use at most 384 MiB of HBM per device.

```python
import math
import jax
import jax.numpy as jnp
from jax import lax

C_IN = 2048
C_MID = 512
CLASSES = 40
WIDTH = 40
IMAGES = 8
HEIGHT = 16


def affine_rows(key, breadth):
    gain_key, bias_key = jax.random.split(key)
    gains = jax.random.uniform(gain_key, (1, breadth), jnp.float32, 0.6, 1.4)
    biases = jnp.clip(0.5 * jax.random.normal(bias_key, (1, breadth), jnp.float32), -1.5, 1.5)
    return jnp.concatenate([gains, biases], axis=0)


def draw_reduce_norm(key, part):
    key = jax.random.fold_in(key, 5)
    return affine_rows(key, C_MID)


def draw_dilate_norm(key, part):
    key = jax.random.fold_in(key, 7)
    return affine_rows(key, C_MID)


def draw_expand_norm(key, part):
    key = jax.random.fold_in(key, 9)
    return affine_rows(key, C_IN)


def draw_features(key, part):
    key = jax.random.fold_in(key, 11)
    base_key, scale_key = jax.random.split(key, 2)
    samples = jnp.clip(jax.random.normal(base_key, (IMAGES, HEIGHT, WIDTH, C_IN), jnp.float32), -5.0, 5.0)
    exponent = jax.random.uniform(scale_key, (IMAGES, HEIGHT, 1, 1), jnp.float32, 0.0, 1.0)
    factor = 0.4 * jnp.exp(exponent * math.log(10.0))
    return (factor * samples).astype(jnp.float32)


def draw_depth_valid(key, part):
    key = jax.random.fold_in(key, 23)
    picture = jnp.arange(IMAGES, dtype=jnp.int32)
    threshold = 80 + 240 * picture // max(IMAGES - 1, 1)
    ticket = jax.random.randint(key, (IMAGES, HEIGHT, WIDTH), 0, 1000)
    usable = (ticket < threshold[:, None, None]).astype(jnp.int32)
    corner = (lax.broadcasted_iota(jnp.int32, (IMAGES, HEIGHT, WIDTH), 1) == 0) & (lax.broadcasted_iota(jnp.int32, (IMAGES, HEIGHT, WIDTH), 2) == 0)
    return jnp.where(corner, 1, usable).astype(jnp.int32)


def with_ends(result, rng, least, top_value):
    longest = result.shape.index(max(result.shape))
    spots = []
    for shift in (0, 1):
        where = [jax.random.randint(jax.random.fold_in(rng, axis), (), 0, length) for axis, length in enumerate(result.shape)]
        where[longest] = (where[longest] + shift) % result.shape[longest]
        spots.append(tuple(where))
    return result.at[spots[0]].set(least).at[spots[1]].set(top_value)


def levels(key, extent, cuts, least, top_value):
    level = 1.0
    for dim, shards_of in cuts:
        steps = jax.random.uniform(jax.random.fold_in(jax.random.fold_in(key, 6), dim), (shards_of,), jnp.float32, least / len(cuts), top_value / len(cuts))
        level = level * jnp.repeat(jnp.exp(steps), extent[dim] // shards_of).reshape((-1,) + (1,) * (len(extent) - 1 - dim))
    return level


def bell_draw(stream_key, shape, scale, bound, pieces=(), held_as=jnp.bfloat16):
    result = jax.random.normal(stream_key, shape, jnp.float32) * scale
    if len(pieces) > 0:
        result = levels(stream_key, shape, pieces, -0.22, 0.18) * result
    return jnp.clip(result, min=-bound, max=bound).astype(held_as)


def setup_inputs(seed: int = 0) -> dict:
    splits = jax.random.split(jax.random.key(seed), 23)
    features = draw_features(jax.random.fold_in(splits[22], 71), 0)
    reduce_weight = bell_draw(splits[1], (C_IN, C_MID), C_IN ** -0.5, 0.125, ((0, 8),), jnp.float32)
    reduce_norm = draw_reduce_norm(jax.random.fold_in(splits[22], 71), 0)
    dilate_weight = bell_draw(splits[3], (9 * C_MID, C_MID), (9 * C_MID) ** -0.5, 0.09375, ((0, 8),), jnp.float32)
    dilate_norm = draw_dilate_norm(jax.random.fold_in(splits[22], 71), 0)
    expand_weight = bell_draw(splits[5], (C_MID, C_IN), C_MID ** -0.5, 0.25, ((0, 8),), jnp.float32)
    expand_norm = draw_expand_norm(jax.random.fold_in(splits[22], 71), 0)
    depth_head = bell_draw(splits[7], (9 * C_MID, C_MID), (9 * C_MID) ** -0.5, 0.09375, ((0, 8),), jnp.float32)
    segment_head = bell_draw(splits[8], (9 * C_MID, C_MID), (9 * C_MID) ** -0.5, 0.09375, ((0, 8),), jnp.float32)
    normal_head = bell_draw(splits[9], (9 * C_MID, C_MID), (9 * C_MID) ** -0.5, 0.09375, ((0, 8),), jnp.float32)
    contour_head = bell_draw(splits[10], (9 * C_MID, C_MID), (9 * C_MID) ** -0.5, 0.09375, ((0, 8),), jnp.float32)
    depth_message = bell_draw(splits[11], (9 * C_MID, C_MID), (18 * C_MID) ** -0.5, 0.0625, ((0, 8),), jnp.float32)
    segment_message = bell_draw(splits[12], (9 * C_MID, C_MID), (18 * C_MID) ** -0.5, 0.0625, ((0, 8),), jnp.float32)
    normal_message = bell_draw(splits[13], (9 * C_MID, C_MID), (18 * C_MID) ** -0.5, 0.0625, ((0, 8),), jnp.float32)
    contour_message = bell_draw(splits[14], (9 * C_MID, C_MID), (18 * C_MID) ** -0.5, 0.0625, ((0, 8),), jnp.float32)
    depth_gate = bell_draw(splits[15], (C_MID, C_MID), C_MID ** -0.5, 0.25, ((0, 8),), jnp.float32)
    segment_gate = bell_draw(splits[16], (C_MID, C_MID), C_MID ** -0.5, 0.25, ((0, 8),), jnp.float32)
    classifier = bell_draw(splits[17], (C_MID, CLASSES), (2.0 * C_MID ** -0.5), 0.5, ((0, 8),), jnp.float32)
    depth_valid = draw_depth_valid(jax.random.fold_in(splits[22], 71), 0)
    labels = with_ends(jax.random.randint(splits[19], (IMAGES, HEIGHT, WIDTH), 0, CLASSES), jax.random.fold_in(splits[19], 1), 0, CLASSES - 1).astype(jnp.int32)
    block_cotangent = bell_draw(splits[20], (IMAGES, HEIGHT, WIDTH, C_IN), 1.0, 6.0, ((0, 8), (1, 4)), jnp.float32)
    depth_cotangent = bell_draw(splits[21], (IMAGES, HEIGHT, WIDTH, C_MID), 0.3, 1.75, ((0, 8), (1, 4)), jnp.float32)
    return dict(features=features, reduce_weight=reduce_weight, reduce_norm=reduce_norm, dilate_weight=dilate_weight, dilate_norm=dilate_norm, expand_weight=expand_weight, expand_norm=expand_norm, depth_head=depth_head, segment_head=segment_head, normal_head=normal_head, contour_head=contour_head, depth_message=depth_message, segment_message=segment_message, normal_message=normal_message, contour_message=contour_message, depth_gate=depth_gate, segment_gate=segment_gate, classifier=classifier, depth_valid=depth_valid, labels=labels, block_cotangent=block_cotangent, depth_cotangent=depth_cotangent)


EPSILON = 1e-05
PRECISE = lax.Precision.HIGHEST

def matmul(values, weight):
    return jnp.dot(values, weight, precision=PRECISE)

def convolve(values, weight, dilation):
    kernel = weight.reshape(3, 3, values.shape[-1], weight.shape[-1])
    return lax.conv_general_dilated(values, kernel, (1, 1), ((dilation, dilation), (dilation, dilation)), rhs_dilation=(dilation, dilation), dimension_numbers=('NHWC', 'HWIO', 'NHWC'), precision=PRECISE)

def normalize(values, params):
    center = lax.optimization_barrier(jnp.mean(values, axis=(0, 1, 2)))
    spread = lax.optimization_barrier(jnp.mean(values * values, axis=(0, 1, 2))) - center * center
    return (values - center) * lax.rsqrt(spread + EPSILON) * params[0] + params[1]

def reference(features, reduce_weight, reduce_norm, dilate_weight, dilate_norm, expand_weight, expand_norm, depth_head, segment_head, normal_head, contour_head, depth_message, segment_message, normal_message, contour_message, depth_gate, segment_gate, classifier, depth_valid, labels, block_cotangent, depth_cotangent):
    usable = depth_valid.astype(jnp.float32)[..., None]
    rescale = IMAGES * HEIGHT * WIDTH / jnp.sum(depth_valid.astype(jnp.float32))
    onehot = (labels[..., None] == jnp.arange(CLASSES, dtype=jnp.int32)).astype(jnp.float32)
    chan_mid = reduce_weight.shape[1]

    def network(features, reduce_weight, reduce_norm, dilate_weight, dilate_norm, expand_weight, expand_norm, depth_head, segment_head, normal_head, contour_head, depth_message, segment_message, normal_message, contour_message, depth_gate, segment_gate, classifier):
        mid_in = jax.nn.silu(normalize(matmul(features, reduce_weight), reduce_norm))
        mid_out = jax.nn.silu(normalize(convolve(mid_in, dilate_weight, 2), dilate_norm))
        summed = normalize(matmul(mid_out, expand_weight), expand_norm) + features
        block_out = jax.nn.silu(summed)
        all_heads = convolve(mid_out, jnp.concatenate([depth_head, segment_head, normal_head, contour_head], axis=1), 1)
        depth_feat = all_heads[..., :chan_mid]
        segment_feat = all_heads[..., chan_mid:2 * chan_mid]
        normal_feat = all_heads[..., 2 * chan_mid:3 * chan_mid]
        contour_feat = all_heads[..., 3 * chan_mid:]
        depth_note = convolve(segment_feat, depth_message, 1) + convolve(normal_feat, normal_message, 1)
        segment_note = convolve(depth_feat, segment_message, 1) + convolve(contour_feat, contour_message, 1)
        depth_stream = depth_feat + jax.nn.sigmoid(matmul(depth_feat, depth_gate)) * depth_note
        segment_stream = segment_feat + jax.nn.sigmoid(matmul(segment_feat, segment_gate)) * segment_note
        logits = matmul(segment_stream, classifier)
        entropy = jnp.sum(jax.nn.logsumexp(logits, axis=-1) - lax.optimization_barrier(jnp.sum(logits * onehot, axis=-1)))
        objective = jnp.sum(block_cotangent * block_out) + jnp.sum(usable * depth_cotangent * depth_stream) * rescale + entropy
        return (objective, (block_out, depth_stream, segment_stream))
    objective, pullback, outputs = jax.vjp(network, features, reduce_weight, reduce_norm, dilate_weight, dilate_norm, expand_weight, expand_norm, depth_head, segment_head, normal_head, contour_head, depth_message, segment_message, normal_message, contour_message, depth_gate, segment_gate, classifier, has_aux=True)
    gradients = pullback(jnp.ones((), jnp.float32))
    factor = (IMAGES * HEIGHT * WIDTH) ** (-0.5)
    scaled = [grad_item * factor for grad_item in gradients[1:]]
    return tuple([outputs[0], outputs[1], outputs[2], gradients[0]] + scaled)
```

```python
import math

import jax
import jax.numpy as jnp
from jax import lax
from jax.experimental import pallas as pl
from jax.experimental.pallas import tpu as pltpu
from jax.sharding import PartitionSpec as P

EPSILON = 1e-05
EXACT = lax.Precision.HIGHEST
FINE = lax.Precision.HIGH
LONGEST_RING = 8
LANES = 128


def product(left, right, left_dim, right_dim, precision=FINE):
    return lax.dot_general(
        left,
        right,
        (((left_dim,), (right_dim,)), ((), ())),
        precision=precision,
        preferred_element_type=jnp.float32,
    )


def halves(values):
    high = values.astype(jnp.bfloat16)
    return high, (values - high.astype(jnp.float32)).astype(jnp.bfloat16)


def three_pass(left, right, left_dim, right_dim):
    dims = (((left_dim,), (right_dim,)), ((), ()))

    def one(a, b):
        return lax.dot_general(a, b, dims, preferred_element_type=jnp.float32)

    return one(left[0], right[0]) + (one(left[0], right[1]) + one(left[1], right[0]))


def frame(image_ref, framed, dilation):
    height, breadth, depth = image_ref.shape
    edge = jnp.zeros((3, dilation, breadth, depth), jnp.float32)
    framed[:, :dilation] = edge
    framed[:, dilation + height :] = edge
    image = image_ref[...]
    side = jnp.zeros((height, dilation, depth), jnp.float32)
    inner = slice(dilation, dilation + height)
    framed[1, inner] = image
    framed[0, inner, dilation:, :] = image[:, : breadth - dilation]
    framed[0, inner, :dilation, :] = side
    framed[2, inner, : breadth - dilation, :] = image[:, dilation:]
    framed[2, inner, breadth - dilation :, :] = side


def shifted(framed, tap, height, dilation):
    block = framed[tap % 3, pl.ds((tap // 3) * dilation, height)]
    return block.reshape(height * block.shape[1], block.shape[2])


def conv_kernel(dilation, image_ref, weight_ref, out_ref, framed):
    tap = pl.program_id(0)

    @pl.when(tap == 0)
    def _():
        frame(image_ref, framed, dilation)
        out_ref[...] = jnp.zeros_like(out_ref)

    moved = halves(shifted(framed, tap, image_ref.shape[0], dilation))
    out_ref[...] += three_pass(moved, halves(weight_ref[...]), 1, 0)


def conv_back_kernel(dilation, image_ref, weight_ref, out_ref, framed):
    tap = pl.program_id(0)

    @pl.when(tap == 0)
    def _():
        frame(image_ref, framed, dilation)
        out_ref[...] = jnp.zeros_like(out_ref)

    moved = halves(shifted(framed, 8 - tap, image_ref.shape[0], dilation))
    out_ref[...] += three_pass(moved, halves(weight_ref[...]), 1, 1)


def conv_grad_kernel(dilation, input_ref, grad_ref, out_ref, framed, high, low):
    tap = pl.program_id(0)

    @pl.when(tap == 0)
    def _():
        frame(grad_ref, framed, dilation)
        high[...], low[...] = halves(jnp.transpose(input_ref[...]))

    moved = halves(shifted(framed, 8 - tap, grad_ref.shape[0], dilation))
    out_ref[...] = three_pass((high[...], low[...]), moved, 1, 0)


def source_rows(weight, start, count):
    return jnp.concatenate(
        [weight[:, k].reshape(-1, weight.shape[-1]) for k in range(start, start + count)], axis=0
    )


def notes_kernel(image_ref, weight_ref, out_ref, framed, total):
    tap = pl.program_id(0)

    @pl.when(tap == 0)
    def _():
        frame(image_ref, framed, 1)
        total[...] = jnp.zeros_like(total)

    moved = shifted(framed, tap, image_ref.shape[0], 1)
    weight = weight_ref[...]
    lanes = moved.shape[1] // 2
    for note in range(2):
        total[note] += three_pass(
            halves(moved[:, note * lanes : (note + 1) * lanes]),
            halves(source_rows(weight, 2 * note, 2)),
            1,
            0,
        )

    @pl.when(tap == 8)
    def _():
        nrows, _, quarter, mid = out_ref.shape
        for note in range(2):
            out_ref[:, note] = total[note].reshape(nrows, quarter, mid)


def notes_back_kernel(notes_ref, weight_ref, direct_ref, out_ref, framed):
    note, tap = pl.program_id(0), pl.program_id(1)

    @pl.when(tap == 0)
    def _():
        frame(notes_ref.at[0], framed, 1)
        part = direct_ref.shape[-1]
        out_ref[:, :part] = direct_ref[0]
        out_ref[:, part:] = jnp.zeros_like(direct_ref[0])

    moved = halves(shifted(framed, 8 - tap, notes_ref.shape[1], 1))
    out_ref[...] += three_pass(moved, halves(source_rows(weight_ref[...], 0, 2)), 1, 1)


def notes_grad_kernel(input_ref, notes_ref, out_ref, framed, high, low):
    note, tap = pl.program_id(0), pl.program_id(1)

    @pl.when(tap == 0)
    def _():
        frame(notes_ref.at[0], framed, 1)
        high[...], low[...] = halves(jnp.transpose(input_ref[...]))

    moved = halves(shifted(framed, 8 - tap, notes_ref.shape[1], 1))
    grad = three_pass((high[...], low[...]), moved, 1, 0)
    runs, _, grain, mid = out_ref.shape
    part = grad.shape[0] // 2
    for k in range(2):
        out_ref[:, k] = grad[k * part : (k + 1) * part].reshape(runs, grain, mid)


def regroup(array, run):
    runs, sources, grain, mid = array.shape
    if grain == run:
        return array
    if run > grain:
        lists = array.reshape(-1, run // grain, sources, grain, mid)
        return jnp.transpose(lists, (0, 2, 1, 3, 4)).reshape(-1, sources, run, mid)
    parts = array.reshape(runs, sources, grain // run, run, mid)
    return jnp.transpose(parts, (0, 2, 1, 3, 4)).reshape(-1, sources, run, mid)


VMEM_LIMIT = 40 * 2**20


def kernel_call(body, grid, in_specs, out_specs, out_shape, scratch, flops):
    return pl.pallas_call(
        body,
        grid=grid,
        in_specs=in_specs,
        out_specs=out_specs,
        out_shape=out_shape,
        scratch_shapes=scratch,
        compiler_params=pltpu.CompilerParams(
            dimension_semantics=("arbitrary",) * len(grid), vmem_limit_bytes=VMEM_LIMIT
        ),
        cost_estimate=pl.CostEstimate(flops=3 * flops, bytes_accessed=12 * 2**20, transcendentals=0),
    )


def framed_scratch(image, dilation):
    height, breadth, depth = image
    return pltpu.VMEM((3, height + 2 * dilation, breadth, depth), jnp.float32)


def whole_spec(shape):
    return pl.BlockSpec(shape, lambda *_: (0,) * len(shape))


def conv(image, weight, dilation, backward=False):
    height, breadth, depth = image.shape
    rows, cols = weight.shape[0] // 9, weight.shape[1]
    wide = rows if backward else cols
    body = conv_back_kernel if backward else conv_kernel

    def run(image_ref, weight_ref, out_ref, framed):
        body(dilation, image_ref, weight_ref, out_ref, framed)

    shape = (height * breadth, wide)
    return kernel_call(
        run,
        (9,),
        [whole_spec(image.shape), pl.BlockSpec((rows, cols), lambda tap: (tap, 0))],
        whole_spec(shape),
        jax.ShapeDtypeStruct(shape, jnp.float32),
        [framed_scratch(image.shape, dilation)],
        2 * 9 * height * breadth * rows * cols,
    )(image, weight)


def conv_grad(flat_input, image_grad, dilation):
    pixels, depth = flat_input.shape
    cols = image_grad.shape[2]

    def run(*refs):
        conv_grad_kernel(dilation, *refs)

    return kernel_call(
        run,
        (9,),
        [whole_spec(flat_input.shape), whole_spec(image_grad.shape)],
        pl.BlockSpec((depth, cols), lambda tap: (tap, 0)),
        jax.ShapeDtypeStruct((9 * depth, cols), jnp.float32),
        [framed_scratch(image_grad.shape, dilation)]
        + [pltpu.VMEM((depth, pixels), jnp.bfloat16)] * 2,
        2 * 9 * pixels * depth * cols,
    )(flat_input, image_grad)


def notes_forward(image, weight, nrows):
    height, breadth, depth = image.shape
    runs, mid = weight.shape[0] // 9, weight.shape[3]
    pixels = height * breadth
    shape = (nrows, 2, pixels // nrows, mid)
    return kernel_call(
        notes_kernel,
        (9,),
        [
            whole_spec(image.shape),
            pl.BlockSpec((runs,) + weight.shape[1:], lambda tap: (tap, 0, 0, 0)),
        ],
        whole_spec(shape),
        jax.ShapeDtypeStruct(shape, jnp.float32),
        [framed_scratch(image.shape, 1), pltpu.VMEM((2, pixels, mid), jnp.float32)],
        2 * 9 * pixels * depth * mid,
    )(image, weight)


def notes_back(notes, weight, direct):
    _, height, breadth, mid = notes.shape
    _, pixels, part = direct.shape
    runs, _, grain, _ = weight.shape
    runs = runs // 9
    return kernel_call(
        notes_back_kernel,
        (2, 9),
        [
            pl.BlockSpec((1, height, breadth, mid), lambda note, tap: (note, 0, 0, 0)),
            pl.BlockSpec((runs, 2, grain, mid), lambda note, tap: (tap, note, 0, 0)),
            pl.BlockSpec((1, pixels, part), lambda note, tap: (note, 0, 0)),
        ],
        pl.BlockSpec((pixels, 2 * part), lambda note, tap: (0, note)),
        jax.ShapeDtypeStruct((pixels, 4 * part), jnp.float32),
        [framed_scratch((height, breadth, mid), 1)],
        2 * 9 * pixels * 4 * part * mid,
    )(notes, weight, direct)


def notes_grad(flat_input, notes, grain):
    pixels, depth = flat_input.shape
    _, height, breadth, mid = notes.shape
    part = depth // 4
    runs = part // grain
    return kernel_call(
        notes_grad_kernel,
        (2, 9),
        [
            pl.BlockSpec((pixels, 2 * part), lambda note, tap: (0, note)),
            pl.BlockSpec((1, height, breadth, mid), lambda note, tap: (note, 0, 0, 0)),
        ],
        pl.BlockSpec((runs, 2, grain, mid), lambda note, tap: (tap, note, 0, 0)),
        jax.ShapeDtypeStruct((9 * runs, 4, grain, mid), jnp.float32),
        [framed_scratch((height, breadth, mid), 1)]
        + [pltpu.VMEM((2 * part, pixels), jnp.bfloat16)] * 2,
        2 * 9 * pixels * depth * mid,
    )(flat_input, notes)


def silu_grad(values):
    gate_val = jax.nn.sigmoid(values)
    return gate_val * (1.0 + values * (1.0 - gate_val))


def swap_rows(block, mask):
    size = lax.axis_size("rows")
    return lax.ppermute(block, "rows", [(i, i ^ mask) for i in range(size)])


def in_order(blocks, row):
    count = len(blocks)
    if count == 1:
        return blocks
    half = count // 2
    near = in_order(blocks[:half], row)
    far = in_order(blocks[half:], row)
    upper = (row & half) != 0
    first = [jnp.where(upper, f, n) for n, f in zip(near, far)]
    second = [jnp.where(upper, n, f) for n, f in zip(near, far)]
    return first + second


def gather_rows(block, row):
    size = lax.axis_size("rows")
    blocks = {0: block}
    mask = size // 2
    while mask:
        for key in sorted(blocks):
            blocks[key | mask] = swap_rows(blocks[key], mask)
        mask //= 2
    return in_order([blocks[key] for key in range(size)], row)


def scatter_rows(blocks, row):
    size = lax.axis_size("rows")
    mask = 1
    rest = blocks
    tail = blocks.shape[1:]
    while mask < size:
        pairs = rest.reshape((-1, 2) + tail)
        bit = (row // mask) % 2
        keep = lax.dynamic_index_in_dim(pairs, bit, 1, keepdims=False)
        give = lax.dynamic_index_in_dim(pairs, 1 - bit, 1, keepdims=False)
        rest = keep + swap_rows(give, mask)
        mask *= 2
    return rest.reshape(tail)


def exchange_rows(blocks, row):
    size = lax.axis_size("rows")
    got = []
    for mask in range(size):
        block = lax.dynamic_index_in_dim(blocks, row ^ mask, 0, keepdims=False)
        got.append(swap_rows(block, mask) if mask else block)
    return in_order(got, row)


def sum_batch(values):
    size = lax.axis_size("batch")
    if size & (size - 1):
        return lax.psum(values, "batch")
    mask = 1
    while mask < size:
        values = values + lax.ppermute(values, "batch", [(i, i ^ mask) for i in range(size)])
        mask *= 2
    return values


class Ring:
    def __init__(self, batch):
        size = lax.axis_size("batch")
        self.batch, self.size = batch, size
        self.order = list(range(0, size, 2)) + [i for i in reversed(range(size)) if i % 2]
        self.place = {b: p for p, b in enumerate(self.order)}
        self.up = [(self.order[p], self.order[(p + 1) % size]) for p in range(size)]
        self.down = [(b, a) for a, b in self.up]
        table = [[self.order[(self.place[b] + k) % size] for k in range(size)] for b in range(size)]
        self.row = jnp.array(table, jnp.int32)[batch]

    def at(self, offset):
        return self.row[offset % self.size]

    def steps(self, longer_up):
        more = self.size // 2
        less = self.size - 1 - more
        return (more, less) if longer_up else (less, more)

    def gather(self, block, longer_up):
        if self.size > LONGEST_RING:
            return lax.all_gather(block, "batch", axis=0, tiled=False)
        whole = jnp.zeros((self.size,) + block.shape, block.dtype)
        whole = lax.dynamic_update_index_in_dim(whole, block, self.batch, 0)
        ups, downs = self.steps(longer_up)
        rising = falling = block
        for k in range(1, max(ups, downs) + 1):
            if k <= ups:
                rising = lax.ppermute(rising, "batch", self.up)
                whole = lax.dynamic_update_index_in_dim(whole, rising, self.at(-k), 0)
            if k <= downs:
                falling = lax.ppermute(falling, "batch", self.down)
                whole = lax.dynamic_update_index_in_dim(whole, falling, self.at(k), 0)
        return whole

    def scatter(self, blocks, longer_up):
        if self.size > LONGEST_RING:
            return lax.psum_scatter(blocks, "batch", scatter_dimension=0, tiled=False)

        def own(offset):
            return lax.dynamic_index_in_dim(blocks, self.at(offset), 0, keepdims=False)

        ups, downs = self.steps(longer_up)
        rising, falling = own(ups), own(-downs)
        for k in range(max(ups, downs)):
            if k < ups:
                rising = lax.ppermute(rising, "batch", self.up)
                if k < ups - 1:
                    rising = rising + own(ups - 1 - k)
            if k < downs:
                falling = lax.ppermute(falling, "batch", self.down)
                if k < downs - 1:
                    falling = falling + own(-(downs - 1 - k))
        return own(0) + rising + falling


def norm_forward(values, gain, bias, ring_sum, count):
    total = ring_sum(jnp.stack([jnp.sum(values, axis=0), jnp.sum(values * values, axis=0)]))
    center = total[0] / count
    inverse = lax.rsqrt(total[1] / count - center * center + EPSILON)
    hat = (values - center) * inverse
    return hat, hat * gain + bias, inverse


def norm_backward(d_out, hat, inverse, gain, count):
    sums = sum_batch(jnp.stack([jnp.sum(d_out * hat, axis=0), jnp.sum(d_out, axis=0)]))
    d_values = inverse * gain * (d_out - sums[1] / count - hat * (sums[0] / count))
    return d_values, sums


def shards(
    features,
    reduce_weight,
    reduce_norm,
    dilate_weight,
    dilate_norm,
    expand_weight,
    expand_norm,
    depth_head,
    segment_head,
    normal_head,
    contour_head,
    depth_message,
    segment_message,
    normal_message,
    contour_message,
    depth_gate,
    segment_gate,
    classifier,
    depth_valid,
    labels,
    block_cotangent,
    depth_cotangent,
):
    row, batch = lax.axis_index("rows"), lax.axis_index("batch")
    nrows, nbatch = lax.axis_size("rows"), lax.axis_size("batch")
    ring = Ring(batch)
    _, local_height, breadth, wide = features.shape
    mid = reduce_weight.shape[1]
    part = mid // nrows
    quarter = local_height * breadth
    height = local_height * nrows
    pixels = quarter * nrows
    count = float(pixels * nbatch)
    factor = count ** (-0.5)
    classes = classifier.shape[1]
    held = dilate_weight.shape[0]
    grain = math.gcd(held, mid) // nrows
    groups = held // (nrows * grain)
    wide_held = wide // nbatch
    wide_part = wide_held // nrows
    mid_held = mid // nbatch

    def row_slice(array, dim):
        size = array.shape[dim] // nrows
        return lax.dynamic_slice_in_dim(array, row * size, size, dim)

    channel = jnp.arange(mid)
    slot = jnp.arange(part)
    mine = (slot // grain) * (nrows * grain) + row * grain + slot % grain
    pick = (channel[:, None] == mine[None, :]).astype(jnp.float32)
    split = jnp.arange(mid)
    natural = ((split % part) // grain) * (nrows * grain) + (split // part) * grain + split % grain
    mix = (natural[:, None] == channel[None, :]).astype(jnp.float32)

    def to_narrow(array):
        return jnp.concatenate(
            [array[:, i * part : (i + 1) * part] for i in range(nrows)], axis=0
        )

    def from_narrow(array):
        size = array.shape[1] // nrows
        return jnp.concatenate([array[:, i * size : (i + 1) * size] for i in range(nrows)], axis=2)

    tiny_width = max(mid_held, wide_part)

    def tiny(array):
        return jnp.pad(array, ((0, 0), (0, tiny_width - array.shape[1])))

    heads_mine = jnp.concatenate(
        [
            product(head, pick, 1, 0, EXACT)
            for head in (segment_head, normal_head, depth_head, contour_head)
        ],
        axis=1,
    )
    heads_full = lax.all_gather(heads_mine, "batch", axis=0, tiled=True)

    def message_runs(array):
        runs = array.reshape(groups, nrows, grain, mid)
        return lax.dynamic_index_in_dim(runs, row, 1, keepdims=True)

    messages_mine = jnp.concatenate(
        [
            message_runs(array)
            for array in (depth_message, normal_message, segment_message, contour_message)
        ],
        axis=1,
    )
    messages_full = lax.all_gather(
        messages_mine.reshape(held, mid), "batch", axis=0, tiled=True
    ).reshape(nbatch * groups, 4, grain, mid)
    run = grain if grain % 8 == 0 else part
    messages_full = regroup(messages_full, run)

    expand_norm_mine = lax.dynamic_index_in_dim(
        expand_norm.reshape(2, nrows, wide_part), row, 1, keepdims=False
    )
    params = jnp.concatenate([tiny(reduce_norm), tiny(dilate_norm), tiny(expand_norm_mine)], axis=0)
    params = jnp.pad(params, ((0, 2), (0, part - tiny_width)))
    expand_mine = lax.dynamic_index_in_dim(
        expand_weight.reshape(mid_held, nbatch, nrows, wide_part), row, 2, keepdims=False
    ).reshape(mid_held, nbatch * wide_part)
    class_lanes = -(-classes // part) * part
    pieces = {
        "reduce": to_narrow(row_slice(reduce_weight, 0)),
        "params": params,
        "dilate": row_slice(dilate_weight, 1),
        "expand": to_narrow(expand_mine),
        "depth_gate": to_narrow(depth_gate),
        "segment_gate": to_narrow(segment_gate),
        "classifier": jnp.concatenate(
            [
                jnp.pad(classifier, ((0, 0), (0, class_lanes - classes)))[:, i : i + part]
                for i in range(0, class_lanes, part)
            ],
            axis=0,
        ),
    }
    first_all = ring.gather(jnp.concatenate(list(pieces.values()), axis=0), True)
    starts, start = {}, 0
    for name, piece in pieces.items():
        starts[name] = (start, start + piece.shape[0])
        start += piece.shape[0]

    def piece_of(name):
        return first_all[:, starts[name][0] : starts[name][1]]

    reduce_full = from_narrow(piece_of("reduce")).reshape(nbatch * wide_part, mid)
    params_all = piece_of("params")
    dilate_full = piece_of("dilate").reshape(nbatch * held, part)

    def all_params(pair, size):
        return jnp.transpose(params_all[:, pair : pair + 2, :size], (1, 0, 2)).reshape(2, nbatch * size)

    reduce_gain, reduce_bias = row_slice(all_params(0, mid_held), 1)
    dilate_gain, dilate_bias = row_slice(all_params(2, mid_held), 1)
    expand_gain, expand_bias = all_params(4, wide_part)
    expand_w, depth_gate_w, segment_gate_w = [
        from_narrow(piece_of(name)).reshape(mid, mid)
        for name in ("expand", "depth_gate", "segment_gate")
    ]
    classifier_w = jnp.concatenate(
        [
            piece_of("classifier")[:, i * mid_held : (i + 1) * mid_held]
            for i in range(class_lanes // part)
        ],
        axis=2,
    ).reshape(mid, class_lanes)

    def spread_wide(array):
        blocks = jnp.transpose(array.reshape(quarter, nbatch, nrows, wide_part), (2, 0, 1, 3))
        return jnp.concatenate(
            exchange_rows(blocks.reshape(nrows, quarter, nbatch * wide_part), row), axis=0
        )

    def collect_wide(array):
        blocks = array.reshape(nrows, quarter, nbatch * wide_part)
        got = jnp.stack(exchange_rows(blocks, row))
        got = got.reshape(nrows, quarter, nbatch, wide_part)
        return jnp.transpose(got, (1, 2, 0, 3)).reshape(1, local_height, breadth, wide)

    valid = depth_valid.astype(jnp.float32).reshape(quarter)
    valid_row = jnp.full((1, LANES), jnp.sum(valid))
    mask = 1
    while mask < nrows:
        valid_row = valid_row + swap_rows(valid_row, mask)
        mask *= 2
    valid_total = sum_batch(valid_row)[0, 0]

    features, block_cotangent, _ = lax.optimization_barrier(
        (features, block_cotangent, (heads_mine, messages_mine))
    )
    inputs = spread_wide(features.reshape(quarter, wide))
    cotangent = spread_wide(block_cotangent.reshape(quarter, wide))

    def by_slices(array):
        return jnp.stack([array[:, i * part : (i + 1) * part] for i in range(nrows)])

    pre_reduce = scatter_rows(by_slices(product(inputs, reduce_full, 1, 0)), row)
    hat_one, normed_one, inverse_one = norm_forward(
        pre_reduce, reduce_gain, reduce_bias, sum_batch, count
    )
    mid_in = jnp.concatenate(gather_rows(jax.nn.silu(normed_one), row), axis=1)
    mid_in_image = mid_in.reshape(height, breadth, mid)
    pre_dilate = conv(mid_in_image, dilate_full, 2)
    hat_two, normed_two, inverse_two = norm_forward(
        pre_dilate, dilate_gain, dilate_bias, sum_batch, count
    )
    mid_out = jnp.concatenate(gather_rows(jax.nn.silu(normed_two), row), axis=1)
    feats = conv(mid_out.reshape(height, breadth, mid), heads_full, 1)
    notes = scatter_rows(
        notes_forward(feats.reshape(height, breadth, nrows * part), messages_full, nrows).reshape(
            nrows, 2 * quarter, mid
        ),
        row,
    )
    depth_note, segment_note = notes[:quarter], notes[quarter:]

    pair = jnp.concatenate(
        [
            feats[:, 2 * part : 3 * part].reshape(nrows, quarter, part),
            feats[:, :part].reshape(nrows, quarter, part),
        ],
        axis=1,
    )
    pair_got = jnp.concatenate(exchange_rows(pair, row), axis=1)
    pair_natural = product(pair_got, mix, 1, 0, EXACT)
    depth_feat, segment_feat = pair_natural[:quarter], pair_natural[quarter:]

    depth_open = jax.nn.sigmoid(product(depth_feat, depth_gate_w, 1, 0))
    segment_open = jax.nn.sigmoid(product(segment_feat, segment_gate_w, 1, 0))
    depth_stream = depth_feat + depth_open * depth_note
    segment_stream = segment_feat + segment_open * segment_note
    logits = product(segment_stream, classifier_w, 1, 0)
    lane = jnp.arange(class_lanes, dtype=jnp.int32)
    real = lane < classes
    top = jnp.max(jnp.where(real, logits, -jnp.inf), axis=-1, keepdims=True)
    shifted = jnp.where(real, jnp.exp(logits - top), 0.0)
    onehot = (labels.reshape(quarter, 1) == lane).astype(jnp.float32)
    d_logits = shifted / jnp.sum(shifted, axis=-1, keepdims=True) - onehot

    classifier_grad = product(segment_stream, d_logits, 0, 0)
    d_segment = product(d_logits, classifier_w, 1, 1)
    d_depth = valid[:, None] * depth_cotangent.reshape(quarter, mid) * (count / valid_total)
    d_depth_note = d_depth * depth_open
    d_depth_pre = d_depth_note * depth_note * (1.0 - depth_open)
    d_segment_note = d_segment * segment_open
    d_segment_pre = d_segment_note * segment_note * (1.0 - segment_open)

    d_notes = gather_rows(jnp.stack([d_depth_note, d_segment_note]), row)
    notes_image = jnp.concatenate(d_notes, axis=1).reshape(2, height, breadth, mid)
    message_grads = regroup(notes_grad(feats, notes_image, run), grain).reshape(
        nbatch * held, mid
    )
    message_grads, notes_image = lax.optimization_barrier((message_grads, notes_image))
    message_sums = lax.psum_scatter(message_grads, "batch", scatter_dimension=0, tiled=True)

    depth_gate_grad = product(depth_feat, d_depth_pre, 0, 0)
    segment_gate_grad = product(segment_feat, d_segment_pre, 0, 0)
    classifier_grad = jnp.pad(classifier_grad, ((0, 0), (0, mid - class_lanes)))

    direct = jnp.concatenate(
        [
            d_depth + product(d_depth_pre, depth_gate_w, 1, 1),
            d_segment + product(d_segment_pre, segment_gate_w, 1, 1),
        ],
        axis=0,
    )
    direct_split = product(direct, mix, 1, 1, EXACT)
    direct_got = exchange_rows(by_slices(direct_split), row)
    direct_both = jnp.stack(
        [
            jnp.concatenate([block[quarter:] for block in direct_got], axis=0),
            jnp.concatenate([block[:quarter] for block in direct_got], axis=0),
        ]
    )
    d_feats = notes_back(notes_image, messages_full, direct_both)
    d_feats_image = d_feats.reshape(height, breadth, nrows * part)
    heads_grad = conv_grad(mid_out, d_feats_image, 1).reshape(nbatch, held, nrows * part)

    hat_three, normed_three, inverse_three = norm_forward(
        product(mid_out, expand_w, 1, 0), expand_gain, expand_bias, sum_batch, count
    )
    summed = normed_three + inputs
    block_out = collect_wide(jax.nn.silu(summed))
    d_summed = cotangent * silu_grad(summed)
    d_pre_expand, expand_sums = norm_backward(d_summed, hat_three, inverse_three, expand_gain, count)
    expand_grad = product(mid_out, d_pre_expand, 0, 0).reshape(nbatch, mid_held, mid)

    gate_terms = jnp.stack([depth_gate_grad, segment_gate_grad, classifier_grad])
    gate_terms = jnp.transpose(
        gate_terms.reshape(3, nbatch, nrows, mid_held // nrows, mid), (2, 1, 0, 3, 4)
    )
    gate_sums = scatter_rows(gate_terms, row).reshape(nbatch, 3 * (mid_held // nrows), mid)

    d_mid_part = conv(d_feats_image, heads_full, 1, True) + product(d_pre_expand, expand_w, 1, 1)
    d_mid_out = scatter_rows(by_slices(d_mid_part), row)
    d_pre_dilate, dilate_sums = norm_backward(
        d_mid_out * silu_grad(normed_two), hat_two, inverse_two, dilate_gain, count
    )
    d_dilate_image = d_pre_dilate.reshape(height, breadth, part)
    d_mid_in = scatter_rows(by_slices(conv(d_dilate_image, dilate_full, 2, True)), row)
    d_pre_reduce, reduce_sums = norm_backward(
        d_mid_in * silu_grad(normed_one), hat_one, inverse_one, reduce_gain, count
    )
    dilate_grad = conv_grad(mid_in, d_dilate_image, 2).reshape(nbatch, held, part)
    square_grad = jnp.concatenate([expand_grad, gate_sums], axis=1)
    heads_grad, dilate_grad, square_grad, reduce_sums = lax.optimization_barrier(
        (heads_grad, dilate_grad, square_grad, reduce_sums)
    )
    heads_sums = ring.scatter(heads_grad, False)
    square_sums = ring.scatter(square_grad, True)
    dilate_out = ring.scatter(dilate_grad, True)
    d_pre_reduce_all = jnp.concatenate(gather_rows(d_pre_reduce, row), axis=1)
    reduce_grad = product(inputs, d_pre_reduce_all, 0, 0).reshape(nbatch, wide_part, mid)
    reduce_out = ring.scatter(reduce_grad, False)
    features_grad = collect_wide(d_summed + product(d_pre_reduce_all, reduce_full, 1, 1))

    messages_got = jnp.stack(gather_rows(message_sums * factor, row)).reshape(
        nrows, groups, 4, grain, mid
    )

    def message_out(index):
        return jnp.transpose(messages_got[:, :, index], (1, 0, 2, 3)).reshape(held, mid)

    heads_got = gather_rows(heads_sums * factor, row)

    def head_out(index):
        lanes = [block[:, index * part : (index + 1) * part] for block in heads_got]
        return product(jnp.concatenate(lanes, axis=1), mix, 1, 0, EXACT)

    squares_got = jnp.stack(gather_rows(square_sums * factor, row))
    expand_out = jnp.transpose(
        squares_got[:, :mid_held].reshape(nrows, mid_held, nbatch, wide_part), (1, 2, 0, 3)
    ).reshape(mid_held, wide)
    gate_rows = mid_held // nrows

    def gate_out(index):
        start = mid_held + index * gate_rows
        return squares_got[:, start : start + gate_rows].reshape(mid_held, mid)

    dilate_got = jnp.concatenate(gather_rows(dilate_out * factor, row), axis=1)
    reduce_got = jnp.concatenate(gather_rows(reduce_out * factor, row), axis=0)

    expand_mine_sums = lax.dynamic_slice_in_dim(expand_sums, batch * wide_part, wide_part, 1)
    pad_to = max(part, wide_part)
    norm_sums = jnp.concatenate(
        [
            jnp.pad(sums, ((0, 0), (0, pad_to - sums.shape[1])))
            for sums in (reduce_sums, dilate_sums, expand_mine_sums)
        ],
        axis=0,
    )
    norms_got = gather_rows(jnp.pad(norm_sums, ((0, 2), (0, 0))) * factor, row)

    def norm_out(start):
        full = jnp.concatenate([block[start : start + 2, :part] for block in norms_got], axis=1)
        return lax.dynamic_slice_in_dim(full, batch * mid_held, mid_held, 1)

    expand_norm_out = jnp.concatenate([block[4:6, :wide_part] for block in norms_got], axis=1)

    return (
        block_out,
        depth_stream.reshape(1, local_height, breadth, mid),
        segment_stream.reshape(1, local_height, breadth, mid),
        features_grad,
        reduce_got,
        norm_out(0),
        dilate_got,
        norm_out(2),
        expand_out,
        expand_norm_out,
        head_out(2),
        head_out(0),
        head_out(1),
        head_out(3),
        message_out(0),
        message_out(2),
        message_out(1),
        message_out(3),
        gate_out(0),
        gate_out(1),
        gate_out(2)[:, :classes],
    )


def solution(mesh):
    pixels = P("batch", "rows", None, None)
    plane = P("batch", "rows", None)
    weight = P("batch", None)
    norm = P(None, "batch")
    in_specs = (
        (pixels, weight, norm, weight, norm, weight, norm) + (weight,) * 11 + (plane, plane, pixels, pixels)
    )
    out_specs = (pixels,) * 4 + (weight, norm) * 3 + (weight,) * 11
    return jax.shard_map(shards, mesh=mesh, in_specs=in_specs, out_specs=out_specs, check_vma=False)
```

```python
import math

import jax
import jax.numpy as jnp
from jax import lax
from jax.experimental import pallas as pl
from jax.experimental.pallas import tpu as pltpu
from jax.sharding import PartitionSpec as P

EPSILON = 1e-05
EXACT = lax.Precision.HIGHEST
FINE = lax.Precision.HIGH
LONGEST_RING = 8
LANES = 128


def product(left, right, left_dim, right_dim, precision=FINE):
    return lax.dot_general(
        left,
        right,
        (((left_dim,), (right_dim,)), ((), ())),
        precision=precision,
        preferred_element_type=jnp.float32,
    )


def halves(values):
    high = values.astype(jnp.bfloat16)
    return high, (values - high.astype(jnp.float32)).astype(jnp.bfloat16)


def three_pass(left, right, left_dim, right_dim):
    dims = (((left_dim,), (right_dim,)), ((), ()))

    def one(a, b):
        return lax.dot_general(a, b, dims, preferred_element_type=jnp.float32)

    return one(left[0], right[0]) + (one(left[0], right[1]) + one(left[1], right[0]))


def frame(image_ref, framed, dilation):
    height, breadth, depth = image_ref.shape
    edge = jnp.zeros((3, dilation, breadth, depth), jnp.float32)
    framed[:, :dilation] = edge
    framed[:, dilation + height :] = edge
    image = image_ref[...]
    side = jnp.zeros((height, dilation, depth), jnp.float32)
    inner = slice(dilation, dilation + height)
    framed[1, inner] = image
    framed[0, inner, dilation:, :] = image[:, : breadth - dilation]
    framed[0, inner, :dilation, :] = side
    framed[2, inner, : breadth - dilation, :] = image[:, dilation:]
    framed[2, inner, breadth - dilation :, :] = side


def shifted(framed, tap, height, dilation):
    block = framed[tap % 3, pl.ds((tap // 3) * dilation, height)]
    return block.reshape(height * block.shape[1], block.shape[2])


def exact_pick(values, choice, choice_dim):
    high = values.astype(jnp.bfloat16)
    rest = values - high.astype(jnp.float32)
    middle = rest.astype(jnp.bfloat16)
    low = (rest - middle.astype(jnp.float32)).astype(jnp.bfloat16)
    dims = (((1,), (choice_dim,)), ((), ()))

    def one(part):
        return lax.dot_general(part, choice, dims, preferred_element_type=jnp.float32)

    return one(high) + (one(middle) + one(low))


def at_lanes(index, size):
    return pl.ds(pl.multiple_of(index * size, size), size)


def keep_and_give(row, load, keep_ref, give_ref):
    core, side = row & 1, row >> 1
    for k in range(2):
        base = (side ^ k) * 2
        keep_ref[k] = load(base + core)
        give_ref[k] = load(base + 1 - core)


def joined_conv_kernel(dilation, row_ref, one, two, three, four, weight_ref, out_ref, image_ref, framed):
    tap = pl.program_id(0)

    @pl.when(tap == 0)
    def _():
        part = one.shape[2]
        for key, block in enumerate((one, two, three, four)):
            image_ref[:, :, at_lanes(row_ref[0] ^ key, part)] = block[...]
        frame(image_ref, framed, dilation)
        out_ref[...] = jnp.zeros_like(out_ref)

    moved = halves(shifted(framed, tap, image_ref.shape[0], dilation))
    out_ref[...] += three_pass(moved, halves(weight_ref[...]), 1, 0)


def heads_kernel(
    row_ref, one, two, three, four, weight_ref, out_ref, image_ref, pairs_ref, framed
):
    joined_conv_kernel(1, row_ref, one, two, three, four, weight_ref, out_ref, image_ref, framed)

    @pl.when(pl.program_id(0) == 8)
    def _():
        _, double, part = pairs_ref.shape
        quarter = double // 2
        for key in range(4):
            rows = pl.ds((row_ref[0] ^ key) * quarter, quarter)
            pairs_ref[key, :quarter] = out_ref[rows, 2 * part : 3 * part]
            pairs_ref[key, quarter:] = out_ref[rows, :part]


def split_product_kernel(row_ref, left_ref, right_ref, extra_ref, keep_ref, give_ref, total):
    total[...] = three_pass(halves(left_ref[...]), halves(right_ref[...]), 1, 0)
    pixels, part = left_ref.shape[0], keep_ref.shape[2]
    keep_and_give(
        row_ref[0],
        lambda j: total[:, at_lanes(j, part)],
        keep_ref.at[:, :pixels],
        give_ref.at[:, :pixels],
    )
    for ref in (keep_ref, give_ref):
        ref[:, pixels:] = jnp.broadcast_to(extra_ref[...], (2, 8, part))


def conv_back_kernel(dilation, row_ref, image_ref, weight_ref, *rest):
    extra_ref = rest[0] if len(rest) == 5 else None
    keep_ref, give_ref, framed, total = rest[-4:]
    tap = pl.program_id(0)

    @pl.when(tap == 0)
    def _():
        frame(image_ref, framed, dilation)
        total[...] = jnp.zeros_like(total) if extra_ref is None else extra_ref[...]

    moved = halves(shifted(framed, 8 - tap, image_ref.shape[0], dilation))
    total[...] += three_pass(moved, halves(weight_ref[...]), 1, 1)

    @pl.when(tap == 8)
    def _():
        part = keep_ref.shape[2]
        keep_and_give(row_ref[0], lambda j: total[:, at_lanes(j, part)], keep_ref, give_ref)


def conv_grad_kernel(dilation, input_ref, grad_ref, out_ref, framed, high, low):
    tap = pl.program_id(0)

    @pl.when(tap == 0)
    def _():
        frame(grad_ref, framed, dilation)
        high[...], low[...] = halves(jnp.transpose(input_ref[...]))

    moved = halves(shifted(framed, 8 - tap, grad_ref.shape[0], dilation))
    out_ref[...] = three_pass((high[...], low[...]), moved, 1, 0)


def heads_grad_kernel(
    row_ref, input_ref, first_ref, second_ref, direct_ref, out_ref, image_ref, framed, high, low
):
    tap = pl.program_id(0)

    @pl.when(tap == 0)
    def _():
        lanes = first_ref.shape[2]
        _, double, breadth, part = direct_ref.shape
        lines = double // 2
        image_ref[:, :, :lanes] = first_ref[...]
        image_ref[:, :, lanes:] = second_ref[...]
        for key in range(4):
            rows = pl.ds((row_ref[0] ^ key) * lines, lines)
            image_ref[rows, :, :part] += direct_ref[key, :lines]
            image_ref[rows, :, lanes : lanes + part] += direct_ref[key, lines:]

    conv_grad_kernel(1, input_ref, image_ref, out_ref, framed, high, low)


def source_rows(weight):
    return jnp.concatenate(
        [weight[:, k].reshape(-1, weight.shape[-1]) for k in range(weight.shape[1])], axis=0
    )


def note_kernel(row_ref, image_ref, weight_ref, keep_ref, give_ref, framed, total):
    tap = pl.program_id(0)

    @pl.when(tap == 0)
    def _():
        frame(image_ref, framed, 1)
        total[...] = jnp.zeros_like(total)

    moved = shifted(framed, tap, image_ref.shape[0], 1)
    total[...] += three_pass(halves(moved), halves(source_rows(weight_ref[...])), 1, 0)

    @pl.when(tap == 8)
    def _():
        quarter = keep_ref.shape[1]
        keep_and_give(
            row_ref[0], lambda j: total[pl.ds(j * quarter, quarter), :], keep_ref, give_ref
        )


def note_back_kernel(note_ref, weight_ref, out_ref, framed):
    tap = pl.program_id(0)

    @pl.when(tap == 0)
    def _():
        frame(note_ref, framed, 1)
        out_ref[...] = jnp.zeros_like(out_ref)

    moved = halves(shifted(framed, 8 - tap, note_ref.shape[0], 1))
    out_ref[...] += three_pass(moved, halves(source_rows(weight_ref[...])), 1, 1)


def note_grad_kernel(
    row_ref, input_ref, one, two, three, four, out_ref, image_ref, framed, high, low
):
    tap = pl.program_id(0)

    @pl.when(tap == 0)
    def _():
        lines = one.shape[0]
        for key, block in enumerate((one, two, three, four)):
            image_ref[pl.ds((row_ref[0] ^ key) * lines, lines)] = block[...]
        frame(image_ref, framed, 1)
        high[...], low[...] = halves(jnp.transpose(input_ref[...]))

    moved = halves(shifted(framed, 8 - tap, image_ref.shape[0], 1))
    grad = three_pass((high[...], low[...]), moved, 1, 0)
    runs, _, grain, mid = out_ref.shape
    part = grad.shape[0] // 2
    for k in range(2):
        out_ref[:, k] = grad[k * part : (k + 1) * part].reshape(runs, grain, mid)


def gates_kernel(
    row_ref, pairs_ref, mix_ref, depth_gate_ref, segment_gate_ref, cotangent_ref, scale_ref,
    feat_ref, open_ref, d_note_ref, joined,
):
    _, double, part = pairs_ref.shape
    quarter = double // 2
    for key in range(4):
        joined[:, at_lanes(row_ref[0] ^ key, part)] = pairs_ref[key]
    feat = exact_pick(joined[...], mix_ref[...], 0)
    feat_ref[...] = feat
    for index, gate_ref in enumerate((depth_gate_ref, segment_gate_ref)):
        rows = slice(index * quarter, (index + 1) * quarter)
        gate = three_pass(halves(feat[rows]), halves(gate_ref[...]), 1, 0)
        open_ref[rows] = jax.nn.sigmoid(gate)
    d_note_ref[...] = cotangent_ref[...] * scale_ref[...] * open_ref[:quarter]


def gate_back(row_ref, feat, opened, note, d_stream, d_note, gate_ref, mix_ref, gate_grad_ref, joined):
    d_pre = halves(d_note * note * (1.0 - opened))
    gate_grad_ref[...] = three_pass(halves(jnp.transpose(feat)), d_pre, 1, 0)
    direct = d_stream + three_pass(d_pre, halves(gate_ref[...]), 1, 1)
    joined[...] = exact_pick(direct, mix_ref[...], 1)


def segment_kernel(
    classes, row_ref, mine_ref, got_ref, feat_ref, open_ref, labels_ref, classifier_ref, gate_ref, mix_ref,
    stream_ref, d_note_ref, direct_ref, gate_grad_ref, classifier_grad_ref, joined,
):
    note = mine_ref[...] + got_ref[...]
    feat, opened = feat_ref[...], open_ref[...]
    stream = feat + opened * note
    stream_ref[...] = stream
    weight = halves(classifier_ref[...])
    logits = three_pass(halves(stream), weight, 1, 0)
    lane = lax.broadcasted_iota(jnp.int32, logits.shape, 1)
    real = lane < classes
    top = jnp.max(jnp.where(real, logits, -3e38), axis=1, keepdims=True)
    powers = jnp.where(real, jnp.exp(jnp.where(real, logits - top, 0.0)), 0.0)
    onehot = jnp.where(lane == labels_ref[...], 1.0, 0.0)
    d_logits = powers / jnp.sum(powers, axis=1, keepdims=True) - onehot
    d_stream = three_pass(halves(d_logits), weight, 1, 1)
    d_note = d_stream * opened
    d_note_ref[...] = d_note
    classifier_grad_ref[...] = three_pass(halves(jnp.transpose(stream)), halves(d_logits), 1, 0)
    gate_back(row_ref, feat, opened, note, d_stream, d_note, gate_ref, mix_ref, gate_grad_ref, joined)
    part = direct_ref.shape[2]
    for key in range(4):
        direct_ref[key] = joined[:, at_lanes(row_ref[0] ^ key, part)]


def depth_kernel(
    row_ref, mine_ref, got_ref, feat_ref, open_ref, cotangent_ref, scale_ref, gate_ref, mix_ref, other_ref,
    stream_ref, direct_ref, gate_grad_ref, joined,
):
    note = mine_ref[...] + got_ref[...]
    feat, opened = feat_ref[...], open_ref[...]
    stream_ref[...] = feat + opened * note
    d_stream = cotangent_ref[...] * scale_ref[...]
    gate_back(
        row_ref, feat, opened, note, d_stream, d_stream * opened, gate_ref, mix_ref, gate_grad_ref, joined
    )
    _, double, part = direct_ref.shape
    quarter = double // 2
    for key in range(4):
        direct_ref[key, :quarter] = other_ref[key]
        direct_ref[key, quarter:] = joined[:, at_lanes(row_ref[0] ^ key, part)]


def reduce_back_kernel(
    row_ref, one, two, three, four, input_ref, weight_ref, d_summed_ref, grad_ref, out_ref, joined
):
    part = one.shape[1]
    for key, block in enumerate((one, two, three, four)):
        joined[:, at_lanes(row_ref[0] ^ key, part)] = block[...]
    d_pre = halves(joined[...])
    grad_ref[...] = three_pass(halves(jnp.transpose(input_ref[...])), d_pre, 1, 0)
    out_ref[...] = d_summed_ref[...] + three_pass(d_pre, halves(weight_ref[...]), 1, 1)


def heads_out_kernel(row_ref, one, two, three, four, mix_ref, *rest):
    outs, joined = rest[:-1], rest[-1]
    part = joined.shape[1] // 4
    for index, out_ref in enumerate(outs):
        lanes = slice(index * part, (index + 1) * part)
        for key, block in enumerate((one, two, three, four)):
            joined[:, at_lanes(row_ref[0] ^ key, part)] = block[:, lanes]
        out_ref[...] = exact_pick(joined[...], mix_ref[...], 0)


def spread_kernel(row_ref, array_ref, out_ref):
    low = lax.broadcasted_iota(jnp.int32, (array_ref.shape[0], 128), 1) < 64
    for device in range(4):
        key = row_ref[0] ^ device
        for k in range(out_ref.shape[2] // 128):
            start = 512 * k + 128 * (device // 2)
            even = array_ref[:, start : start + 128]
            odd = array_ref[:, start + 256 : start + 384]
            if device % 2:
                block = jnp.where(low, pltpu.roll(even, 64, 1), odd)
            else:
                block = jnp.where(low, even, pltpu.roll(odd, 64, 1))
            out_ref[key, :, 128 * k : 128 * (k + 1)] = block


def collect_kernel(row_ref, one, two, three, four, out_ref, ordered):
    for key, block in enumerate((one, two, three, four)):
        ordered[row_ref[0] ^ key] = block[...]
    low = lax.broadcasted_iota(jnp.int32, (one.shape[0], 128), 1) < 64
    for k in range(one.shape[1] // 128):
        for pair in range(2):
            first = ordered[2 * pair, :, 128 * k : 128 * (k + 1)]
            second = ordered[2 * pair + 1, :, 128 * k : 128 * (k + 1)]
            start = 512 * k + 128 * pair
            out_ref[:, start : start + 128] = jnp.where(low, first, pltpu.roll(second, 64, 1))
            out_ref[:, start + 256 : start + 384] = jnp.where(low, pltpu.roll(first, 64, 1), second)


def regroup(array, run):
    runs, sources, grain, mid = array.shape
    if grain == run:
        return array
    if run > grain:
        lists = array.reshape(-1, run // grain, sources, grain, mid)
        return jnp.transpose(lists, (0, 2, 1, 3, 4)).reshape(-1, sources, run, mid)
    parts = array.reshape(runs, sources, grain // run, run, mid)
    return jnp.transpose(parts, (0, 2, 1, 3, 4)).reshape(-1, sources, run, mid)


VMEM_LIMIT = 56 * 2**20
SCALAR = pl.BlockSpec(memory_space=pltpu.SMEM)


def kernel_call(body, grid, in_specs, out_specs, out_shape, scratch, flops):
    return pl.pallas_call(
        body,
        grid=grid,
        in_specs=in_specs,
        out_specs=out_specs,
        out_shape=out_shape,
        scratch_shapes=scratch,
        compiler_params=pltpu.CompilerParams(
            dimension_semantics=("arbitrary",) * len(grid), vmem_limit_bytes=VMEM_LIMIT
        ),
        cost_estimate=pl.CostEstimate(flops=3 * flops, bytes_accessed=12 * 2**20, transcendentals=0),
    )


def single_call(body, args, outs, scratch, flops):
    return kernel_call(
        body,
        (1,),
        [SCALAR] + [whole_spec(arg.shape) for arg in args[1:]],
        [whole_spec(out) for out in outs],
        [jax.ShapeDtypeStruct(out, jnp.float32) for out in outs],
        [pltpu.VMEM(shape, jnp.float32) for shape in scratch],
        flops,
    )(*args)


def framed_scratch(image, dilation):
    height, breadth, depth = image
    return pltpu.VMEM((3, height + 2 * dilation, breadth, depth), jnp.float32)


def whole_spec(shape):
    return pl.BlockSpec(shape, lambda *_: (0,) * len(shape))


def struct(shape):
    return jax.ShapeDtypeStruct(shape, jnp.float32)


def tap_rows(rows, cols):
    return pl.BlockSpec((rows, cols), lambda tap: (tap, 0))


def tap_runs(weight_shape):
    return pl.BlockSpec((weight_shape[0] // 9,) + weight_shape[1:], lambda tap: (tap, 0, 0, 0))


def joined_conv(row, blocks, weight, dilation, with_pairs=False):
    height, breadth, part = blocks[0].shape
    image = (height, breadth, 4 * part)
    rows, cols = weight.shape[0] // 9, weight.shape[1]
    shapes = [(height * breadth, cols), image]
    if with_pairs:
        body = heads_kernel
        shapes.append((4, height * breadth // 2, part))
    else:

        def body(*refs):
            joined_conv_kernel(dilation, *refs)

    return kernel_call(
        body,
        (9,),
        [SCALAR] + [whole_spec(blocks[0].shape)] * 4 + [tap_rows(rows, cols)],
        [whole_spec(shape) for shape in shapes],
        [struct(shape) for shape in shapes],
        [framed_scratch(image, dilation)],
        2 * 9 * height * breadth * rows * cols,
    )(row, *blocks, weight)


def conv_back(row, image, weight, dilation, extra=None):
    height, breadth, _ = image.shape
    rows, cols = weight.shape[0] // 9, weight.shape[1]
    pixels = height * breadth
    shape = (2, pixels, rows // 4)

    def body(*refs):
        conv_back_kernel(dilation, *refs)

    extras = [] if extra is None else [extra]
    return kernel_call(
        body,
        (9,),
        [SCALAR, whole_spec(image.shape), tap_rows(rows, cols)]
        + [whole_spec(array.shape) for array in extras],
        [whole_spec(shape)] * 2,
        [struct(shape)] * 2,
        [framed_scratch(image.shape, dilation), pltpu.VMEM((pixels, rows), jnp.float32)],
        2 * 9 * pixels * rows * cols,
    )(row, image, weight, *extras)


def conv_grad(flat_input, image_grad, dilation):
    pixels, depth = flat_input.shape
    cols = image_grad.shape[2]

    def body(*refs):
        conv_grad_kernel(dilation, *refs)

    return kernel_call(
        body,
        (9,),
        [whole_spec(flat_input.shape), whole_spec(image_grad.shape)],
        tap_rows(depth, cols),
        struct((9 * depth, cols)),
        [framed_scratch(image_grad.shape, dilation)]
        + [pltpu.VMEM((depth, pixels), jnp.bfloat16)] * 2,
        2 * 9 * pixels * depth * cols,
    )(flat_input, image_grad)


def heads_grad_of(row, flat_input, first, second, direct):
    pixels, depth = flat_input.shape
    height, breadth, lanes = first.shape
    image = (height, breadth, 2 * lanes)
    return kernel_call(
        heads_grad_kernel,
        (9,),
        [SCALAR] + [whole_spec(array.shape) for array in (flat_input, first, second, direct)],
        [tap_rows(depth, 2 * lanes), whole_spec(image)],
        [struct((9 * depth, 2 * lanes)), struct(image)],
        [framed_scratch(image, 1)] + [pltpu.VMEM((depth, pixels), jnp.bfloat16)] * 2,
        2 * 9 * pixels * depth * 2 * lanes,
    )(row, flat_input, first, second, direct)


def note_forward(row, image, pair, weight):
    height, breadth, depth = image.shape
    depth = depth // 2
    mid = weight.shape[3]
    pixels = height * breadth
    shape = (2, pixels // 4, mid)
    return kernel_call(
        note_kernel,
        (9,),
        [
            SCALAR,
            pl.BlockSpec((height, breadth, depth), lambda tap: (0, 0, pair)),
            tap_runs(weight.shape),
        ],
        [whole_spec(shape)] * 2,
        [struct(shape)] * 2,
        [framed_scratch((height, breadth, depth), 1), pltpu.VMEM((pixels, mid), jnp.float32)],
        2 * 9 * pixels * depth * mid,
    )(row, image, weight)


def note_back(note, weight):
    height, breadth, mid = note.shape
    shape = (height * breadth, weight.shape[0] // 9 * weight.shape[1] * weight.shape[2])
    return kernel_call(
        note_back_kernel,
        (9,),
        [whole_spec(note.shape), tap_runs(weight.shape)],
        whole_spec(shape),
        struct(shape),
        [framed_scratch(note.shape, 1)],
        2 * 9 * shape[0] * shape[1] * mid,
    )(note, weight)


def note_grad(row, flat_input, pair, blocks, grain):
    pixels, depth = flat_input.shape
    depth = depth // 2
    lines, breadth, mid = blocks[0].shape
    image = (4 * lines, breadth, mid)
    runs = depth // 2 // grain
    grad = (9 * runs, 2, grain, mid)
    return kernel_call(
        note_grad_kernel,
        (9,),
        [SCALAR, pl.BlockSpec((pixels, depth), lambda tap: (0, pair))]
        + [whole_spec(blocks[0].shape)] * 4,
        [tap_runs(grad), whole_spec(image)],
        [struct(grad), struct(image)],
        [framed_scratch(image, 1)] + [pltpu.VMEM((depth, pixels), jnp.bfloat16)] * 2,
        2 * 9 * pixels * depth * mid,
    )(row, flat_input, *blocks)


def silu_grad(values):
    gate_val = jax.nn.sigmoid(values)
    return gate_val * (1.0 + values * (1.0 - gate_val))


def swap_rows(block, mask):
    size = lax.axis_size("rows")
    return lax.ppermute(block, "rows", [(i, i ^ mask) for i in range(size)])


def in_order(blocks, row):
    count = len(blocks)
    if count == 1:
        return blocks
    half = count // 2
    near = in_order(blocks[:half], row)
    far = in_order(blocks[half:], row)
    upper = (row & half) != 0
    first = [jnp.where(upper, f, n) for n, f in zip(near, far)]
    second = [jnp.where(upper, n, f) for n, f in zip(near, far)]
    return first + second


def gather_keyed(block):
    far = swap_rows(block, 2)
    return [block, swap_rows(block, 1), far, swap_rows(far, 1)]


def gather_rows(block, row):
    return in_order(gather_keyed(block), row)


def scatter_end(keep, give):
    got = swap_rows(give, 1)
    other = keep[1] + got[1]
    return keep[0] + got[0], swap_rows(other, 2)


def scatter_rows(blocks, row):
    core, side = row & 1, row >> 1
    pairs = blocks.reshape((2, 2) + blocks.shape[1:])
    keep = lax.dynamic_index_in_dim(pairs, core, 1, keepdims=False)
    got = keep + swap_rows(lax.dynamic_index_in_dim(pairs, 1 - core, 1, keepdims=False), 1)
    mine = lax.dynamic_index_in_dim(got, side, 0, keepdims=False)
    return mine + swap_rows(lax.dynamic_index_in_dim(got, 1 - side, 0, keepdims=False), 2)


def exchange_keyed(blocks):
    return [blocks[0]] + [swap_rows(blocks[mask], mask) for mask in range(1, 4)]


def sum_batch(values, direct=False):
    size = lax.axis_size("batch")
    if size & (size - 1):
        return lax.psum(values, "batch")

    def swap(block, mask):
        return lax.ppermute(block, "batch", [(i, i ^ mask) for i in range(size)])

    if direct and size <= LONGEST_RING:
        return values + sum(swap(values, mask) for mask in range(1, size))
    mask = 1
    while mask < size:
        values = values + swap(values, mask)
        mask *= 2
    return values


class Ring:
    def __init__(self, batch):
        size = lax.axis_size("batch")
        self.batch, self.size = batch, size
        self.order = list(range(0, size, 2)) + [i for i in reversed(range(size)) if i % 2]
        self.place = {b: p for p, b in enumerate(self.order)}
        self.up = [(self.order[p], self.order[(p + 1) % size]) for p in range(size)]
        self.down = [(b, a) for a, b in self.up]
        table = [[self.order[(self.place[b] + k) % size] for k in range(size)] for b in range(size)]
        self.row = jnp.array(table, jnp.int32)[batch]

    def at(self, offset):
        return self.row[offset % self.size]

    def steps(self, longer_up):
        more = self.size // 2
        less = self.size - 1 - more
        return (more, less) if longer_up else (less, more)

    def gather(self, block, longer_up, beside=None, beside_step=0):
        if self.size > LONGEST_RING:
            return lax.all_gather(block, "batch", axis=0, tiled=False), beside
        whole = jnp.zeros((self.size,) + block.shape, block.dtype)
        whole = lax.dynamic_update_index_in_dim(whole, block, self.batch, 0)
        ups, downs = self.steps(longer_up)
        rising = falling = block
        for k in range(1, max(ups, downs) + 1):
            if k == beside_step and beside is not None:
                rising, falling, beside = lax.optimization_barrier((rising, falling, beside))
            if k <= ups:
                rising = lax.ppermute(rising, "batch", self.up)
                whole = lax.dynamic_update_index_in_dim(whole, rising, self.at(-k), 0)
            if k <= downs:
                falling = lax.ppermute(falling, "batch", self.down)
                whole = lax.dynamic_update_index_in_dim(whole, falling, self.at(k), 0)
        return whole, beside

    def scatter(self, blocks, longer_up, beside=None, beside_step=0):
        if self.size > LONGEST_RING:
            return lax.psum_scatter(blocks, "batch", scatter_dimension=0, tiled=False), beside

        def own(offset):
            return lax.dynamic_index_in_dim(blocks, self.at(offset), 0, keepdims=False)

        ups, downs = self.steps(longer_up)
        rising, falling = own(ups), own(-downs)
        for k in range(max(ups, downs)):
            if k + 1 == beside_step and beside is not None:
                rising, falling, beside = lax.optimization_barrier((rising, falling, beside))
            if k < ups:
                rising = lax.ppermute(rising, "batch", self.up)
                if k < ups - 1:
                    rising = rising + own(ups - 1 - k)
            if k < downs:
                falling = lax.ppermute(falling, "batch", self.down)
                if k < downs - 1:
                    falling = falling + own(-(downs - 1 - k))
        return own(0) + rising + falling, beside


def sums_of(values, others):
    return jnp.stack([jnp.sum(values, axis=0), jnp.sum(values * others, axis=0)])


def norm_forward(values, total, gain, bias, count):
    center = total[0] / count
    inverse = lax.rsqrt(total[1] / count - center * center + EPSILON)
    hat = (values - center) * inverse
    return hat, hat * gain + bias, inverse


def norm_backward(d_out, hat, inverse, gain, count, direct):
    sums = sum_batch(jnp.stack([jnp.sum(d_out * hat, axis=0), jnp.sum(d_out, axis=0)]), direct)
    d_values = inverse * gain * (d_out - sums[1] / count - hat * (sums[0] / count))
    return d_values, sums


def shards(
    features,
    reduce_weight,
    reduce_norm,
    dilate_weight,
    dilate_norm,
    expand_weight,
    expand_norm,
    depth_head,
    segment_head,
    normal_head,
    contour_head,
    depth_message,
    segment_message,
    normal_message,
    contour_message,
    depth_gate,
    segment_gate,
    classifier,
    depth_valid,
    labels,
    block_cotangent,
    depth_cotangent,
):
    row, batch = lax.axis_index("rows"), lax.axis_index("batch")
    nrows, nbatch = lax.axis_size("rows"), lax.axis_size("batch")
    ring = Ring(batch)
    _, local_height, breadth, wide = features.shape
    mid = reduce_weight.shape[1]
    part = mid // nrows
    quarter = local_height * breadth
    height = local_height * nrows
    pixels = quarter * nrows
    count = float(pixels * nbatch)
    factor = count ** (-0.5)
    classes = classifier.shape[1]
    held = dilate_weight.shape[0]
    grain = math.gcd(held, mid) // nrows
    groups = held // (nrows * grain)
    wide_held = wide // nbatch
    wide_part = wide_held // nrows
    mid_held = mid // nbatch

    def row_slice(array, dim):
        size = array.shape[dim] // nrows
        return lax.dynamic_slice_in_dim(array, row * size, size, dim)

    channel = jnp.arange(mid)
    slot = jnp.arange(part)
    mine = (slot // grain) * (nrows * grain) + row * grain + slot % grain
    pick = (channel[:, None] == mine[None, :]).astype(jnp.float32)
    split = jnp.arange(mid)
    natural = ((split % part) // grain) * (nrows * grain) + (split // part) * grain + split % grain
    mix = (natural[:, None] == channel[None, :]).astype(jnp.bfloat16)
    here = row.astype(jnp.int32).reshape(1)

    def to_narrow(array):
        return jnp.concatenate(
            [array[:, i * part : (i + 1) * part] for i in range(nrows)], axis=0
        )

    def from_narrow(array):
        size = array.shape[1] // nrows
        return jnp.concatenate([array[:, i * size : (i + 1) * size] for i in range(nrows)], axis=2)

    tiny_width = max(mid_held, wide_part)

    def tiny(array):
        return jnp.pad(array, ((0, 0), (0, tiny_width - array.shape[1])))

    heads_mine = jnp.concatenate(
        [
            product(head, pick, 1, 0, EXACT)
            for head in (segment_head, normal_head, depth_head, contour_head)
        ],
        axis=1,
    )
    heads_full = lax.all_gather(heads_mine, "batch", axis=0, tiled=True)

    def message_runs(array):
        runs = array.reshape(groups, nrows, grain, mid)
        return lax.dynamic_index_in_dim(runs, row, 1, keepdims=True)

    def message_pair(first, second):
        return jnp.concatenate([message_runs(first), message_runs(second)], axis=1)

    run = grain if grain % 8 == 0 else part
    segment_pair_mine = message_pair(segment_message, contour_message).reshape(held // 2, mid)
    depth_pair_mine = message_pair(depth_message, normal_message).reshape(held // 2, mid)
    segment_pair_w, depth_pair_w = [
        regroup(
            lax.all_gather(mine, "batch", axis=0, tiled=True).reshape(
                nbatch * groups, 2, grain, mid
            ),
            run,
        )
        for mine in (segment_pair_mine, depth_pair_mine)
    ]

    expand_norm_mine = lax.dynamic_index_in_dim(
        expand_norm.reshape(2, nrows, wide_part), row, 1, keepdims=False
    )
    params = jnp.concatenate([tiny(reduce_norm), tiny(dilate_norm), tiny(expand_norm_mine)], axis=0)
    params = jnp.pad(params, ((0, 2), (0, part - tiny_width)))
    expand_mine = lax.dynamic_index_in_dim(
        expand_weight.reshape(mid_held, nbatch, nrows, wide_part), row, 2, keepdims=False
    ).reshape(mid_held, nbatch * wide_part)
    class_lanes = -(-classes // part) * part

    def packed(pieces):
        spans, start = {}, 0
        for name, piece in pieces.items():
            spans[name] = slice(start, start + piece.shape[0])
            start += piece.shape[0]
        return jnp.concatenate(list(pieces.values()), axis=0), spans

    first_mine, first_spans = packed(
        {
            "reduce": to_narrow(row_slice(reduce_weight, 0)),
            "params": params,
            "dilate": row_slice(dilate_weight, 1),
        }
    )
    first_all, _ = ring.gather(first_mine, True)
    reduce_full = from_narrow(first_all[:, first_spans["reduce"]]).reshape(nbatch * wide_part, mid)
    params_all = first_all[:, first_spans["params"]]
    dilate_full = first_all[:, first_spans["dilate"]].reshape(nbatch * held, part)

    def all_params(pair, size):
        return jnp.transpose(params_all[:, pair : pair + 2, :size], (1, 0, 2)).reshape(2, nbatch * size)

    reduce_gain, reduce_bias = row_slice(all_params(0, mid_held), 1)
    dilate_gain, dilate_bias = row_slice(all_params(2, mid_held), 1)
    expand_gain, expand_bias = all_params(4, wide_part)

    spread_by_kernel = wide_part == 64 and part % 128 == 0

    def spread_wide(array):
        if spread_by_kernel:
            (blocks,) = single_call(
                spread_kernel, (here, array), [(nrows, quarter, wide // nrows)], [], 1
            )
            blocks = [blocks[key] for key in range(4)]
        else:
            split_blocks = jnp.transpose(array.reshape(quarter, nbatch, nrows, wide_part), (2, 0, 1, 3))
            split_blocks = split_blocks.reshape(nrows, quarter, nbatch * wide_part)
            blocks = [
                lax.dynamic_index_in_dim(split_blocks, row ^ key, 0, keepdims=False)
                for key in range(4)
            ]
        return jnp.concatenate(in_order(exchange_keyed(blocks), row), axis=0)

    def collect_wide(array):
        blocks = array.reshape(nrows, quarter, nbatch * wide_part)
        got = exchange_keyed(
            [lax.dynamic_index_in_dim(blocks, row ^ key, 0, keepdims=False) for key in range(4)]
        )
        if spread_by_kernel:
            (out,) = single_call(
                collect_kernel,
                (here, *got),
                [(quarter, wide)],
                [(nrows, quarter, wide // nrows)],
                1,
            )
        else:
            out = jnp.stack(in_order(got, row)).reshape(nrows, quarter, nbatch, wide_part)
            out = jnp.transpose(out, (1, 2, 0, 3))
        return out.reshape(1, local_height, breadth, wide)

    def image_of(array):
        return array.reshape(height, breadth, array.shape[-1])

    features, _ = lax.optimization_barrier((features, (heads_mine, segment_pair_mine, first_mine)))
    inputs = spread_wide(features.reshape(quarter, wide))

    valid = depth_valid.astype(jnp.float32).reshape(quarter, 1)
    keep, give = single_call(
        split_product_kernel,
        (here, inputs, reduce_full, jnp.full((1, part), jnp.sum(valid))),
        [(2, pixels + 8, part)] * 2,
        [(pixels, mid)],
        2 * pixels * mid * mid,
    )
    mine_terms, got_terms = scatter_end(keep, give)
    pre_reduce = mine_terms + got_terms
    valid_row = pre_reduce[pixels]
    pre_reduce = pre_reduce[:pixels]
    total_one = sum_batch(jnp.concatenate([sums_of(pre_reduce, pre_reduce), valid_row[None]]))
    scale = valid * (count / total_one[2, 0])
    hat_one, normed_one, inverse_one = norm_forward(
        pre_reduce, total_one, reduce_gain, reduce_bias, count
    )
    pre_dilate, mid_in = joined_conv(
        here, gather_keyed(image_of(jax.nn.silu(normed_one))), dilate_full, 2
    )
    hat_two, normed_two, inverse_two = norm_forward(
        pre_dilate, sum_batch(sums_of(pre_dilate, pre_dilate)), dilate_gain, dilate_bias, count
    )

    beside = mid // class_lanes
    square_mine, square_spans = packed(
        {
            "depth_gate": depth_gate,
            "segment_gate": segment_gate,
            "expand": expand_mine,
            "classifier": jnp.pad(classifier, ((0, 0), (0, class_lanes - classes)))
            .reshape(beside, mid_held // beside, class_lanes)
            .transpose(1, 0, 2)
            .reshape(mid_held // beside, mid),
        }
    )
    square_mine, inverse_two = lax.optimization_barrier((square_mine, inverse_two))
    feats, mid_out, pairs = joined_conv(
        here, gather_keyed(image_of(jax.nn.silu(normed_two))), heads_full, 1, True
    )
    square_all, feats = ring.gather(square_mine, False, feats, 2)
    depth_gate_w, segment_gate_w, expand_w = [
        square_all[:, square_spans[name]].reshape(mid, mid)
        for name in ("depth_gate", "segment_gate", "expand")
    ]
    classifier_w = (
        square_all[:, square_spans["classifier"]]
        .reshape(nbatch, mid_held // beside, beside, class_lanes)
        .transpose(0, 2, 1, 3)
        .reshape(mid, class_lanes)
    )
    feats_image = image_of(feats)

    segment_mine, segment_got = scatter_end(*note_forward(here, feats_image, 1, segment_pair_w))
    pairs_got = jnp.stack(exchange_keyed([pairs[key] for key in range(4)]))
    depth_cotangent = depth_cotangent.reshape(quarter, mid)
    both, one_map = (2 * quarter, mid), (quarter, mid)
    feat_pair, open_pair, d_depth_note = single_call(
        gates_kernel,
        (here, pairs_got, mix, depth_gate_w, segment_gate_w, depth_cotangent, scale),
        [both, both, one_map],
        [both],
        8 * quarter * mid * mid,
    )
    feat_pair, open_pair, segment_mine = lax.optimization_barrier((feat_pair, open_pair, segment_mine))

    def segment_body(*refs):
        segment_kernel(classes, *refs)

    segment_stream, d_segment_note, direct_segment, segment_gate_grad, classifier_grad = single_call(
        segment_body,
        (
            here,
            segment_mine,
            segment_got,
            feat_pair[quarter:],
            open_pair[quarter:],
            labels.reshape(quarter, 1),
            classifier_w,
            segment_gate_w,
            mix,
        ),
        [one_map, one_map, (4, quarter, part), (mid, mid), (mid, class_lanes)],
        [one_map],
        8 * quarter * mid * mid,
    )

    def lines(array):
        return array.reshape(local_height, breadth, mid)

    depth_pair_grad, d_depth_image = note_grad(here, feats, 0, gather_keyed(lines(d_depth_note)), run)
    depth_pair_sums = lax.psum_scatter(
        regroup(depth_pair_grad, grain).reshape(-1, mid), "batch", scatter_dimension=0, tiled=True
    )
    segment_pair_grad, d_segment_image = note_grad(
        here, feats, 1, gather_keyed(lines(d_segment_note)), run
    )
    segment_pair_sums = lax.psum_scatter(
        regroup(segment_pair_grad, grain).reshape(-1, mid), "batch", scatter_dimension=0, tiled=True
    )
    feats_late, d_segment_image, depth_pair_grad = lax.optimization_barrier(
        (feats_image, d_segment_image, depth_pair_grad)
    )
    depth_mine, depth_got = scatter_end(*note_forward(here, feats_late, 0, depth_pair_w))
    depth_stream, direct_both, depth_gate_grad = single_call(
        depth_kernel,
        (
            here,
            depth_mine,
            depth_got,
            feat_pair[:quarter],
            open_pair[:quarter],
            depth_cotangent,
            scale,
            depth_gate_w,
            mix,
            direct_segment,
        ),
        [one_map, (4, 2 * quarter, part), (mid, mid)],
        [one_map],
        8 * quarter * mid * mid,
    )
    direct_got = jnp.stack(exchange_keyed([direct_both[key] for key in range(4)]))
    flat_mid_out = mid_out.reshape(pixels, mid)
    heads_grad, d_feats = heads_grad_of(
        here,
        flat_mid_out,
        image_of(note_back(d_depth_image, depth_pair_w)),
        image_of(note_back(d_segment_image, segment_pair_w)),
        direct_got.reshape(4, 2 * local_height, breadth, part),
    )
    heads_sums, _ = ring.scatter(heads_grad.reshape(nbatch, held, nrows * part), True)

    expand_input, _ = lax.optimization_barrier((flat_mid_out, segment_pair_grad))
    block_cotangent, _ = lax.optimization_barrier((block_cotangent, feats))
    cotangent = spread_wide(block_cotangent.reshape(quarter, wide))
    pre_expand = product(expand_input, expand_w, 1, 0)
    hat_three, normed_three, inverse_three = norm_forward(
        pre_expand, sum_batch(sums_of(pre_expand, pre_expand)), expand_gain, expand_bias, count
    )
    summed = normed_three + inputs
    block_out = collect_wide(jax.nn.silu(summed))
    d_summed = cotangent * silu_grad(summed)
    d_pre_expand, expand_sums = norm_backward(
        d_summed, hat_three, inverse_three, expand_gain, count, False
    )
    expand_grad = product(flat_mid_out, d_pre_expand, 0, 0).reshape(nbatch, mid_held, mid)

    gate_terms = jnp.stack(
        [
            depth_gate_grad,
            segment_gate_grad,
            jnp.pad(classifier_grad, ((0, 0), (0, mid - class_lanes))),
        ]
    )
    gate_rows = mid_held // nrows
    gate_terms = jnp.transpose(gate_terms.reshape(3, nbatch, nrows, gate_rows, mid), (2, 1, 0, 3, 4))
    gate_sums = scatter_rows(gate_terms, row).reshape(nbatch, 3 * gate_rows, mid)

    mine_terms, got_terms = scatter_end(
        *conv_back(here, d_feats, heads_full, 1, product(d_pre_expand, expand_w, 1, 1))
    )
    d_pre_dilate, dilate_sums = norm_backward(
        (mine_terms + got_terms) * silu_grad(normed_two), hat_two, inverse_two, dilate_gain, count, True
    )
    d_dilate_image = image_of(d_pre_dilate)
    mine_terms, got_terms = scatter_end(*conv_back(here, d_dilate_image, dilate_full, 2))
    d_pre_reduce, reduce_sums = norm_backward(
        (mine_terms + got_terms) * silu_grad(normed_one), hat_one, inverse_one, reduce_gain, count, True
    )
    reduce_grad, features_back = single_call(
        reduce_back_kernel,
        (here, *gather_keyed(d_pre_reduce), inputs, reduce_full, d_summed),
        [(mid, mid), (pixels, mid)],
        [(pixels, mid)],
        4 * pixels * mid * mid,
    )
    dilate_grad = conv_grad(mid_in.reshape(pixels, mid), d_dilate_image, 2).reshape(
        nbatch, held, part
    )
    narrow = held // nrows
    square_grad = jnp.concatenate(
        [
            jnp.concatenate(
                [dilate_grad[:, i * narrow : (i + 1) * narrow] for i in range(nrows)], axis=2
            ),
            expand_grad,
            gate_sums,
        ],
        axis=1,
    )
    square_grad, reduce_sums, depth_pair_sums = lax.optimization_barrier(
        (square_grad, reduce_sums, depth_pair_sums)
    )
    square_sums, _ = ring.scatter(square_grad, False)
    reduce_out, segment_pair_sums = ring.scatter(
        reduce_grad.reshape(nbatch, wide_part, mid), True, segment_pair_sums, 2
    )
    features_grad = collect_wide(features_back)

    depth_pair_out, segment_pair_out = [
        jnp.stack(gather_rows(sums * factor, row)).reshape(nrows, groups, 2, grain, mid)
        for sums in (depth_pair_sums, segment_pair_sums)
    ]

    def message_out(pair_got, index):
        return jnp.transpose(pair_got[:, :, index], (1, 0, 2, 3)).reshape(held, mid)

    segment_out, normal_out, depth_out, contour_out = single_call(
        heads_out_kernel,
        (here, *gather_keyed(heads_sums * factor), mix),
        [(held, mid)] * 4,
        [(held, mid)],
        8 * held * mid * mid,
    )

    expand_mine_sums = lax.dynamic_slice_in_dim(expand_sums, batch * wide_part, wide_part, 1)
    norm_sums = jnp.concatenate(
        [
            jnp.pad(sums, ((0, 0), (0, mid - sums.shape[1])))
            for sums in (reduce_sums, dilate_sums, expand_mine_sums)
        ],
        axis=0,
    )
    small = jnp.concatenate([square_sums, jnp.pad(norm_sums, ((0, 2), (0, 0)))], axis=0) * factor
    small_got = gather_rows(small, row)
    squares_got = jnp.stack([block[narrow : narrow + mid_held + 3 * gate_rows] for block in small_got])
    dilate_out = jnp.concatenate(
        [
            jnp.concatenate(
                [block[:narrow, i * part : (i + 1) * part] for i in range(nrows)], axis=0
            )
            for block in small_got
        ],
        axis=1,
    )
    expand_out = jnp.transpose(
        squares_got[:, :mid_held].reshape(nrows, mid_held, nbatch, wide_part), (1, 2, 0, 3)
    ).reshape(mid_held, wide)

    def gate_out(index):
        start = mid_held + index * gate_rows
        return squares_got[:, start : start + gate_rows].reshape(mid_held, mid)

    norms_got = [block[-8:] for block in small_got]

    def norm_out(start):
        full = jnp.concatenate([block[start : start + 2, :part] for block in norms_got], axis=1)
        return lax.dynamic_slice_in_dim(full, batch * mid_held, mid_held, 1)

    expand_norm_out = jnp.concatenate([block[4:6, :wide_part] for block in norms_got], axis=1)
    reduce_got = jnp.concatenate(gather_rows(reduce_out * factor, row), axis=0)

    return (
        block_out,
        depth_stream.reshape(1, local_height, breadth, mid),
        segment_stream.reshape(1, local_height, breadth, mid),
        features_grad,
        reduce_got,
        norm_out(0),
        dilate_out,
        norm_out(2),
        expand_out,
        expand_norm_out,
        depth_out,
        segment_out,
        normal_out,
        contour_out,
        message_out(depth_pair_out, 0),
        message_out(segment_pair_out, 0),
        message_out(depth_pair_out, 1),
        message_out(segment_pair_out, 1),
        gate_out(0),
        gate_out(1),
        gate_out(2)[:, :classes],
    )


def solution(mesh):
    pixels = P("batch", "rows", None, None)
    plane = P("batch", "rows", None)
    weight = P("batch", None)
    norm = P(None, "batch")
    in_specs = (
        (pixels, weight, norm, weight, norm, weight, norm) + (weight,) * 11 + (plane, plane, pixels, pixels)
    )
    out_specs = (pixels,) * 4 + (weight, norm) * 3 + (weight,) * 11
    return jax.shard_map(shards, mesh=mesh, in_specs=in_specs, out_specs=out_specs, check_vma=False)
```

```python
import math

import jax
import jax.numpy as jnp
from jax import lax
from jax.experimental import pallas as pl
from jax.experimental.pallas import tpu as pltpu
from jax.sharding import PartitionSpec as P

EPSILON = 1e-05
EXACT = lax.Precision.HIGHEST
FINE = lax.Precision.HIGH
LONGEST_RING = 8
LANES = 128


def product(left, right, left_dim, right_dim, precision=FINE):
    return lax.dot_general(
        left,
        right,
        (((left_dim,), (right_dim,)), ((), ())),
        precision=precision,
        preferred_element_type=jnp.float32,
    )


def halves(values):
    high = values.astype(jnp.bfloat16)
    return high, (values - high.astype(jnp.float32)).astype(jnp.bfloat16)


def three_pass(left, right, left_dim, right_dim):
    dims = (((left_dim,), (right_dim,)), ((), ()))

    def one(a, b):
        return lax.dot_general(a, b, dims, preferred_element_type=jnp.float32)

    return one(left[0], right[0]) + (one(left[0], right[1]) + one(left[1], right[0]))


def frame(image_ref, framed, dilation):
    height, breadth, depth = image_ref.shape
    edge = jnp.zeros((3, dilation, breadth, depth), jnp.float32)
    framed[:, :dilation] = edge
    framed[:, dilation + height :] = edge
    image = image_ref[...]
    side = jnp.zeros((height, dilation, depth), jnp.float32)
    inner = slice(dilation, dilation + height)
    framed[1, inner] = image
    framed[0, inner, dilation:, :] = image[:, : breadth - dilation]
    framed[0, inner, :dilation, :] = side
    framed[2, inner, : breadth - dilation, :] = image[:, dilation:]
    framed[2, inner, breadth - dilation :, :] = side


def shifted(framed, tap, height, dilation):
    block = framed[tap % 3, pl.ds((tap // 3) * dilation, height)]
    return block.reshape(height * block.shape[1], block.shape[2])


def exact_pick(values, choice, choice_dim):
    high = values.astype(jnp.bfloat16)
    rest = values - high.astype(jnp.float32)
    middle = rest.astype(jnp.bfloat16)
    low = (rest - middle.astype(jnp.float32)).astype(jnp.bfloat16)
    dims = (((1,), (choice_dim,)), ((), ()))

    def one(part):
        return lax.dot_general(part, choice, dims, preferred_element_type=jnp.float32)

    return one(high) + (one(middle) + one(low))


def at_lanes(index, size):
    return pl.ds(pl.multiple_of(index * size, size), size)


def keep_and_give(row, load, keep_ref, give_ref):
    core, side = row & 1, row >> 1
    for k in range(2):
        base = (side ^ k) * 2
        keep_ref[k] = load(base + core)
        give_ref[k] = load(base + 1 - core)


def joined_conv_kernel(dilation, row_ref, one, two, three, four, weight_ref, out_ref, image_ref, framed):
    tap = pl.program_id(0)

    @pl.when(tap == 0)
    def _():
        part = one.shape[2]
        for key, block in enumerate((one, two, three, four)):
            image_ref[:, :, at_lanes(row_ref[0] ^ key, part)] = block[...]
        frame(image_ref, framed, dilation)
        out_ref[...] = jnp.zeros_like(out_ref)

    moved = halves(shifted(framed, tap, image_ref.shape[0], dilation))
    out_ref[...] += three_pass(moved, halves(weight_ref[...]), 1, 0)


def heads_kernel(
    row_ref, one, two, three, four, weight_ref, out_ref, image_ref, pairs_ref, framed
):
    joined_conv_kernel(1, row_ref, one, two, three, four, weight_ref, out_ref, image_ref, framed)

    @pl.when(pl.program_id(0) == 8)
    def _():
        _, double, part = pairs_ref.shape
        quarter = double // 2
        for key in range(4):
            rows = pl.ds((row_ref[0] ^ key) * quarter, quarter)
            pairs_ref[key, :quarter] = out_ref[rows, 2 * part : 3 * part]
            pairs_ref[key, quarter:] = out_ref[rows, :part]


def split_product_kernel(row_ref, left_ref, right_ref, extra_ref, keep_ref, give_ref, total):
    total[...] = three_pass(halves(left_ref[...]), halves(right_ref[...]), 1, 0)
    pixels, part = left_ref.shape[0], keep_ref.shape[2]
    keep_and_give(
        row_ref[0],
        lambda j: total[:, at_lanes(j, part)],
        keep_ref.at[:, :pixels],
        give_ref.at[:, :pixels],
    )
    for ref in (keep_ref, give_ref):
        ref[:, pixels:] = jnp.broadcast_to(extra_ref[...], (2, 8, part))


def conv_back_kernel(dilation, row_ref, image_ref, weight_ref, *rest):
    extra_ref = rest[0] if len(rest) == 5 else None
    keep_ref, give_ref, framed, total = rest[-4:]
    tap = pl.program_id(0)

    @pl.when(tap == 0)
    def _():
        frame(image_ref, framed, dilation)
        total[...] = jnp.zeros_like(total) if extra_ref is None else extra_ref[...]

    moved = halves(shifted(framed, 8 - tap, image_ref.shape[0], dilation))
    total[...] += three_pass(moved, halves(weight_ref[...]), 1, 1)

    @pl.when(tap == 8)
    def _():
        part = keep_ref.shape[2]
        keep_and_give(row_ref[0], lambda j: total[:, at_lanes(j, part)], keep_ref, give_ref)


def conv_grad_kernel(dilation, input_ref, grad_ref, out_ref, framed, high, low):
    tap = pl.program_id(0)

    @pl.when(tap == 0)
    def _():
        frame(grad_ref, framed, dilation)
        high[...], low[...] = halves(jnp.transpose(input_ref[...]))

    moved = halves(shifted(framed, 8 - tap, grad_ref.shape[0], dilation))
    out_ref[...] = three_pass((high[...], low[...]), moved, 1, 0)


def heads_grad_kernel(
    row_ref, input_ref, first_ref, second_ref, direct_ref, out_ref, image_ref, framed, high, low
):
    tap = pl.program_id(0)

    @pl.when(tap == 0)
    def _():
        lanes = first_ref.shape[2]
        _, double, breadth, part = direct_ref.shape
        lines = double // 2
        image_ref[:, :, :lanes] = first_ref[...]
        image_ref[:, :, lanes:] = second_ref[...]
        for key in range(4):
            rows = pl.ds((row_ref[0] ^ key) * lines, lines)
            image_ref[rows, :, :part] += direct_ref[key, :lines]
            image_ref[rows, :, lanes : lanes + part] += direct_ref[key, lines:]

    conv_grad_kernel(1, input_ref, image_ref, out_ref, framed, high, low)


def source_rows(weight):
    return jnp.concatenate(
        [weight[:, k].reshape(-1, weight.shape[-1]) for k in range(weight.shape[1])], axis=0
    )


def note_kernel(row_ref, image_ref, weight_ref, keep_ref, give_ref, framed, total):
    tap = pl.program_id(0)

    @pl.when(tap == 0)
    def _():
        frame(image_ref, framed, 1)
        total[...] = jnp.zeros_like(total)

    moved = shifted(framed, tap, image_ref.shape[0], 1)
    total[...] += three_pass(halves(moved), halves(source_rows(weight_ref[...])), 1, 0)

    @pl.when(tap == 8)
    def _():
        quarter = keep_ref.shape[1]
        keep_and_give(
            row_ref[0], lambda j: total[pl.ds(j * quarter, quarter), :], keep_ref, give_ref
        )


def note_back_kernel(note_ref, weight_ref, out_ref, framed):
    tap = pl.program_id(0)

    @pl.when(tap == 0)
    def _():
        frame(note_ref, framed, 1)
        out_ref[...] = jnp.zeros_like(out_ref)

    moved = halves(shifted(framed, 8 - tap, note_ref.shape[0], 1))
    out_ref[...] += three_pass(moved, halves(source_rows(weight_ref[...])), 1, 1)


def note_grad_kernel(
    row_ref, input_ref, one, two, three, four, out_ref, image_ref, framed, high, low
):
    tap = pl.program_id(0)

    @pl.when(tap == 0)
    def _():
        lines = one.shape[0]
        for key, block in enumerate((one, two, three, four)):
            image_ref[pl.ds((row_ref[0] ^ key) * lines, lines)] = block[...]
        frame(image_ref, framed, 1)
        high[...], low[...] = halves(jnp.transpose(input_ref[...]))

    moved = halves(shifted(framed, 8 - tap, image_ref.shape[0], 1))
    grad = three_pass((high[...], low[...]), moved, 1, 0)
    runs, _, grain, mid = out_ref.shape
    part = grad.shape[0] // 2
    for k in range(2):
        out_ref[:, k] = grad[k * part : (k + 1) * part].reshape(runs, grain, mid)


def gates_kernel(
    row_ref, pairs_ref, mix_ref, depth_gate_ref, segment_gate_ref, cotangent_ref, scale_ref,
    feat_ref, open_ref, d_note_ref, joined,
):
    _, double, part = pairs_ref.shape
    quarter = double // 2
    for key in range(4):
        joined[:, at_lanes(row_ref[0] ^ key, part)] = pairs_ref[key]
    feat = exact_pick(joined[...], mix_ref[...], 0)
    feat_ref[...] = feat
    for index, gate_ref in enumerate((depth_gate_ref, segment_gate_ref)):
        rows = slice(index * quarter, (index + 1) * quarter)
        gate = three_pass(halves(feat[rows]), halves(gate_ref[...]), 1, 0)
        open_ref[rows] = jax.nn.sigmoid(gate)
    d_note_ref[...] = cotangent_ref[...] * scale_ref[...] * open_ref[:quarter]


def gate_back(row_ref, feat, opened, note, d_stream, d_note, gate_ref, mix_ref, gate_grad_ref, joined):
    d_pre = halves(d_note * note * (1.0 - opened))
    gate_grad_ref[...] = three_pass(halves(jnp.transpose(feat)), d_pre, 1, 0)
    direct = d_stream + three_pass(d_pre, halves(gate_ref[...]), 1, 1)
    joined[...] = exact_pick(direct, mix_ref[...], 1)


def segment_kernel(
    classes, row_ref, mine_ref, got_ref, feat_ref, open_ref, labels_ref, classifier_ref, gate_ref, mix_ref,
    stream_ref, d_note_ref, direct_ref, gate_grad_ref, classifier_grad_ref, joined,
):
    note = mine_ref[...] + got_ref[...]
    feat, opened = feat_ref[...], open_ref[...]
    stream = feat + opened * note
    stream_ref[...] = stream
    weight = halves(classifier_ref[...])
    logits = three_pass(halves(stream), weight, 1, 0)
    lane = lax.broadcasted_iota(jnp.int32, logits.shape, 1)
    real = lane < classes
    top = jnp.max(jnp.where(real, logits, -3e38), axis=1, keepdims=True)
    powers = jnp.where(real, jnp.exp(jnp.where(real, logits - top, 0.0)), 0.0)
    onehot = jnp.where(lane == labels_ref[...], 1.0, 0.0)
    d_logits = powers / jnp.sum(powers, axis=1, keepdims=True) - onehot
    d_stream = three_pass(halves(d_logits), weight, 1, 1)
    d_note = d_stream * opened
    d_note_ref[...] = d_note
    classifier_grad_ref[...] = three_pass(halves(jnp.transpose(stream)), halves(d_logits), 1, 0)
    gate_back(row_ref, feat, opened, note, d_stream, d_note, gate_ref, mix_ref, gate_grad_ref, joined)
    part = direct_ref.shape[2]
    for key in range(4):
        direct_ref[key] = joined[:, at_lanes(row_ref[0] ^ key, part)]


def depth_kernel(
    row_ref, mine_ref, got_ref, feat_ref, open_ref, cotangent_ref, scale_ref, gate_ref, mix_ref, other_ref,
    stream_ref, direct_ref, gate_grad_ref, joined,
):
    note = mine_ref[...] + got_ref[...]
    feat, opened = feat_ref[...], open_ref[...]
    stream_ref[...] = feat + opened * note
    d_stream = cotangent_ref[...] * scale_ref[...]
    gate_back(
        row_ref, feat, opened, note, d_stream, d_stream * opened, gate_ref, mix_ref, gate_grad_ref, joined
    )
    _, double, part = direct_ref.shape
    quarter = double // 2
    for key in range(4):
        direct_ref[key, :quarter] = other_ref[key]
        direct_ref[key, quarter:] = joined[:, at_lanes(row_ref[0] ^ key, part)]


def reduce_back_kernel(
    row_ref, one, two, three, four, input_ref, weight_ref, d_summed_ref, grad_ref, out_ref, joined
):
    part = one.shape[1]
    for key, block in enumerate((one, two, three, four)):
        joined[:, at_lanes(row_ref[0] ^ key, part)] = block[...]
    d_pre = halves(joined[...])
    grad_ref[...] = three_pass(halves(jnp.transpose(input_ref[...])), d_pre, 1, 0)
    out_ref[...] = d_summed_ref[...] + three_pass(d_pre, halves(weight_ref[...]), 1, 1)


def heads_out_kernel(row_ref, one, two, three, four, mix_ref, *rest):
    outs, joined = rest[:-1], rest[-1]
    part = joined.shape[1] // 4
    for index, out_ref in enumerate(outs):
        lanes = slice(index * part, (index + 1) * part)
        for key, block in enumerate((one, two, three, four)):
            joined[:, at_lanes(row_ref[0] ^ key, part)] = block[:, lanes]
        out_ref[...] = exact_pick(joined[...], mix_ref[...], 0)


def spread_kernel(row_ref, array_ref, out_ref):
    low = lax.broadcasted_iota(jnp.int32, (array_ref.shape[0], 128), 1) < 64
    for device in range(4):
        key = row_ref[0] ^ device
        for k in range(out_ref.shape[2] // 128):
            start = 512 * k + 128 * (device // 2)
            even = array_ref[:, start : start + 128]
            odd = array_ref[:, start + 256 : start + 384]
            if device % 2:
                block = jnp.where(low, pltpu.roll(even, 64, 1), odd)
            else:
                block = jnp.where(low, even, pltpu.roll(odd, 64, 1))
            out_ref[key, :, 128 * k : 128 * (k + 1)] = block


def collect_kernel(row_ref, one, two, three, four, out_ref, ordered):
    for key, block in enumerate((one, two, three, four)):
        ordered[row_ref[0] ^ key] = block[...]
    low = lax.broadcasted_iota(jnp.int32, (one.shape[0], 128), 1) < 64
    for k in range(one.shape[1] // 128):
        for pair in range(2):
            first = ordered[2 * pair, :, 128 * k : 128 * (k + 1)]
            second = ordered[2 * pair + 1, :, 128 * k : 128 * (k + 1)]
            start = 512 * k + 128 * pair
            out_ref[:, start : start + 128] = jnp.where(low, first, pltpu.roll(second, 64, 1))
            out_ref[:, start + 256 : start + 384] = jnp.where(low, pltpu.roll(first, 64, 1), second)


def regroup(array, run):
    runs, sources, grain, mid = array.shape
    if grain == run:
        return array
    if run > grain:
        lists = array.reshape(-1, run // grain, sources, grain, mid)
        return jnp.transpose(lists, (0, 2, 1, 3, 4)).reshape(-1, sources, run, mid)
    parts = array.reshape(runs, sources, grain // run, run, mid)
    return jnp.transpose(parts, (0, 2, 1, 3, 4)).reshape(-1, sources, run, mid)


VMEM_LIMIT = 56 * 2**20
SCALAR = pl.BlockSpec(memory_space=pltpu.SMEM)


def kernel_call(body, grid, in_specs, out_specs, out_shape, scratch, flops):
    return pl.pallas_call(
        body,
        grid=grid,
        in_specs=in_specs,
        out_specs=out_specs,
        out_shape=out_shape,
        scratch_shapes=scratch,
        compiler_params=pltpu.CompilerParams(
            dimension_semantics=("arbitrary",) * len(grid), vmem_limit_bytes=VMEM_LIMIT
        ),
        cost_estimate=pl.CostEstimate(flops=3 * flops, bytes_accessed=12 * 2**20, transcendentals=0),
    )


def single_call(body, args, outs, scratch, flops):
    return kernel_call(
        body,
        (1,),
        [SCALAR] + [whole_spec(arg.shape) for arg in args[1:]],
        [whole_spec(out) for out in outs],
        [jax.ShapeDtypeStruct(out, jnp.float32) for out in outs],
        [pltpu.VMEM(shape, jnp.float32) for shape in scratch],
        flops,
    )(*args)


def framed_scratch(image, dilation):
    height, breadth, depth = image
    return pltpu.VMEM((3, height + 2 * dilation, breadth, depth), jnp.float32)


def whole_spec(shape):
    return pl.BlockSpec(shape, lambda *_: (0,) * len(shape))


def struct(shape):
    return jax.ShapeDtypeStruct(shape, jnp.float32)


def tap_rows(rows, cols):
    return pl.BlockSpec((rows, cols), lambda tap: (tap, 0))


def tap_runs(weight_shape):
    return pl.BlockSpec((weight_shape[0] // 9,) + weight_shape[1:], lambda tap: (tap, 0, 0, 0))


def joined_conv(row, blocks, weight, dilation, with_pairs=False):
    height, breadth, part = blocks[0].shape
    image = (height, breadth, 4 * part)
    rows, cols = weight.shape[0] // 9, weight.shape[1]
    shapes = [(height * breadth, cols), image]
    if with_pairs:
        body = heads_kernel
        shapes.append((4, height * breadth // 2, part))
    else:

        def body(*refs):
            joined_conv_kernel(dilation, *refs)

    return kernel_call(
        body,
        (9,),
        [SCALAR] + [whole_spec(blocks[0].shape)] * 4 + [tap_rows(rows, cols)],
        [whole_spec(shape) for shape in shapes],
        [struct(shape) for shape in shapes],
        [framed_scratch(image, dilation)],
        2 * 9 * height * breadth * rows * cols,
    )(row, *blocks, weight)


def conv_back(row, image, weight, dilation, extra=None):
    height, breadth, _ = image.shape
    rows, cols = weight.shape[0] // 9, weight.shape[1]
    pixels = height * breadth
    shape = (2, pixels, rows // 4)

    def body(*refs):
        conv_back_kernel(dilation, *refs)

    extras = [] if extra is None else [extra]
    return kernel_call(
        body,
        (9,),
        [SCALAR, whole_spec(image.shape), tap_rows(rows, cols)]
        + [whole_spec(array.shape) for array in extras],
        [whole_spec(shape)] * 2,
        [struct(shape)] * 2,
        [framed_scratch(image.shape, dilation), pltpu.VMEM((pixels, rows), jnp.float32)],
        2 * 9 * pixels * rows * cols,
    )(row, image, weight, *extras)


def conv_grad(flat_input, image_grad, dilation):
    pixels, depth = flat_input.shape
    cols = image_grad.shape[2]

    def body(*refs):
        conv_grad_kernel(dilation, *refs)

    return kernel_call(
        body,
        (9,),
        [whole_spec(flat_input.shape), whole_spec(image_grad.shape)],
        tap_rows(depth, cols),
        struct((9 * depth, cols)),
        [framed_scratch(image_grad.shape, dilation)]
        + [pltpu.VMEM((depth, pixels), jnp.bfloat16)] * 2,
        2 * 9 * pixels * depth * cols,
    )(flat_input, image_grad)


def heads_grad_of(row, flat_input, first, second, direct):
    pixels, depth = flat_input.shape
    height, breadth, lanes = first.shape
    image = (height, breadth, 2 * lanes)
    return kernel_call(
        heads_grad_kernel,
        (9,),
        [SCALAR] + [whole_spec(array.shape) for array in (flat_input, first, second, direct)],
        [tap_rows(depth, 2 * lanes), whole_spec(image)],
        [struct((9 * depth, 2 * lanes)), struct(image)],
        [framed_scratch(image, 1)] + [pltpu.VMEM((depth, pixels), jnp.bfloat16)] * 2,
        2 * 9 * pixels * depth * 2 * lanes,
    )(row, flat_input, first, second, direct)


def note_forward(row, image, pair, weight):
    height, breadth, depth = image.shape
    depth = depth // 2
    mid = weight.shape[3]
    pixels = height * breadth
    shape = (2, pixels // 4, mid)
    return kernel_call(
        note_kernel,
        (9,),
        [
            SCALAR,
            pl.BlockSpec((height, breadth, depth), lambda tap: (0, 0, pair)),
            tap_runs(weight.shape),
        ],
        [whole_spec(shape)] * 2,
        [struct(shape)] * 2,
        [framed_scratch((height, breadth, depth), 1), pltpu.VMEM((pixels, mid), jnp.float32)],
        2 * 9 * pixels * depth * mid,
    )(row, image, weight)


def note_back(note, weight):
    height, breadth, mid = note.shape
    shape = (height * breadth, weight.shape[0] // 9 * weight.shape[1] * weight.shape[2])
    return kernel_call(
        note_back_kernel,
        (9,),
        [whole_spec(note.shape), tap_runs(weight.shape)],
        whole_spec(shape),
        struct(shape),
        [framed_scratch(note.shape, 1)],
        2 * 9 * shape[0] * shape[1] * mid,
    )(note, weight)


def note_grad(row, flat_input, pair, blocks, grain):
    pixels, depth = flat_input.shape
    depth = depth // 2
    lines, breadth, mid = blocks[0].shape
    image = (4 * lines, breadth, mid)
    runs = depth // 2 // grain
    grad = (9 * runs, 2, grain, mid)
    return kernel_call(
        note_grad_kernel,
        (9,),
        [SCALAR, pl.BlockSpec((pixels, depth), lambda tap: (0, pair))]
        + [whole_spec(blocks[0].shape)] * 4,
        [tap_runs(grad), whole_spec(image)],
        [struct(grad), struct(image)],
        [framed_scratch(image, 1)] + [pltpu.VMEM((depth, pixels), jnp.bfloat16)] * 2,
        2 * 9 * pixels * depth * mid,
    )(row, flat_input, *blocks)


def silu_grad(values):
    gate_val = jax.nn.sigmoid(values)
    return gate_val * (1.0 + values * (1.0 - gate_val))


def swap_rows(block, mask):
    size = lax.axis_size("rows")
    return lax.ppermute(block, "rows", [(i, i ^ mask) for i in range(size)])


def in_order(blocks, row):
    count = len(blocks)
    if count == 1:
        return blocks
    half = count // 2
    near = in_order(blocks[:half], row)
    far = in_order(blocks[half:], row)
    upper = (row & half) != 0
    first = [jnp.where(upper, f, n) for n, f in zip(near, far)]
    second = [jnp.where(upper, n, f) for n, f in zip(near, far)]
    return first + second


def gather_keyed(block):
    far = swap_rows(block, 2)
    return [block, swap_rows(block, 1), far, swap_rows(far, 1)]


def gather_rows(block, row):
    return in_order(gather_keyed(block), row)


def scatter_end(keep, give):
    got = swap_rows(give, 1)
    other = keep[1] + got[1]
    return keep[0] + got[0], swap_rows(other, 2)


def scatter_rows(blocks, row):
    core, side = row & 1, row >> 1
    pairs = blocks.reshape((2, 2) + blocks.shape[1:])
    keep = lax.dynamic_index_in_dim(pairs, core, 1, keepdims=False)
    got = keep + swap_rows(lax.dynamic_index_in_dim(pairs, 1 - core, 1, keepdims=False), 1)
    mine = lax.dynamic_index_in_dim(got, side, 0, keepdims=False)
    return mine + swap_rows(lax.dynamic_index_in_dim(got, 1 - side, 0, keepdims=False), 2)


def exchange_keyed(blocks):
    return [blocks[0]] + [swap_rows(blocks[mask], mask) for mask in range(1, 4)]


def sum_batch(values, direct=False):
    size = lax.axis_size("batch")
    if size & (size - 1):
        return lax.psum(values, "batch")

    def swap(block, mask):
        return lax.ppermute(block, "batch", [(i, i ^ mask) for i in range(size)])

    if direct and size <= LONGEST_RING:
        return values + sum(swap(values, mask) for mask in range(1, size))
    mask = 1
    while mask < size:
        values = values + swap(values, mask)
        mask *= 2
    return values


class Ring:
    def __init__(self, batch):
        size = lax.axis_size("batch")
        self.batch, self.size = batch, size
        self.order = list(range(0, size, 2)) + [i for i in reversed(range(size)) if i % 2]
        self.place = {b: p for p, b in enumerate(self.order)}
        self.up = [(self.order[p], self.order[(p + 1) % size]) for p in range(size)]
        self.down = [(b, a) for a, b in self.up]
        table = [[self.order[(self.place[b] + k) % size] for k in range(size)] for b in range(size)]
        self.row = jnp.array(table, jnp.int32)[batch]

    def at(self, offset):
        return self.row[offset % self.size]

    def steps(self, longer_up):
        more = self.size // 2
        less = self.size - 1 - more
        return (more, less) if longer_up else (less, more)

    def gather(self, block, longer_up, beside=None, beside_step=0):
        if self.size > LONGEST_RING:
            return lax.all_gather(block, "batch", axis=0, tiled=False), beside
        whole = jnp.zeros((self.size,) + block.shape, block.dtype)
        whole = lax.dynamic_update_index_in_dim(whole, block, self.batch, 0)
        ups, downs = self.steps(longer_up)
        rising = falling = block
        for k in range(1, max(ups, downs) + 1):
            if k == beside_step and beside is not None:
                rising, falling, beside = lax.optimization_barrier((rising, falling, beside))
            if k <= ups:
                rising = lax.ppermute(rising, "batch", self.up)
                whole = lax.dynamic_update_index_in_dim(whole, rising, self.at(-k), 0)
            if k <= downs:
                falling = lax.ppermute(falling, "batch", self.down)
                whole = lax.dynamic_update_index_in_dim(whole, falling, self.at(k), 0)
        return whole, beside

    def scatter(self, blocks, longer_up):
        hops = Hops(self, blocks, longer_up)
        while not hops.done:
            hops.step()
        return hops.result()


class Hops:
    def __init__(self, ring, blocks, longer_up):
        self.ring, self.blocks, self.hop = ring, blocks, 0
        if ring.size > LONGEST_RING:
            self.sums = lax.psum_scatter(blocks, "batch", scatter_dimension=0, tiled=False)
            self.done = True
            return
        self.sums, self.done = None, False
        self.ups, self.downs = ring.steps(longer_up)
        self.rising, self.falling = self.own(self.ups), self.own(-self.downs)

    def own(self, offset):
        return lax.dynamic_index_in_dim(self.blocks, self.ring.at(offset), 0, keepdims=False)

    def step(self, later=None):
        if self.done:
            return later
        k = self.hop
        if k < self.ups:
            self.rising = lax.ppermute(self.rising, "batch", self.ring.up)
        if k < self.downs:
            self.falling = lax.ppermute(self.falling, "batch", self.ring.down)
        if later is not None:
            self.rising, self.falling, later = lax.optimization_barrier(
                (self.rising, self.falling, later)
            )
        if k < self.ups - 1:
            self.rising = self.rising + self.own(self.ups - 1 - k)
        if k < self.downs - 1:
            self.falling = self.falling + self.own(-(self.downs - 1 - k))
        self.hop += 1
        self.done = self.hop == max(self.ups, self.downs)
        return later

    def result(self):
        return self.sums if self.sums is not None else self.own(0) + self.rising + self.falling


def sums_of(values, others):
    return jnp.stack([jnp.sum(values, axis=0), jnp.sum(values * others, axis=0)])


def norm_forward(values, total, gain, bias, count):
    center = total[0] / count
    inverse = lax.rsqrt(total[1] / count - center * center + EPSILON)
    hat = (values - center) * inverse
    return hat, hat * gain + bias, inverse


def norm_backward(d_out, hat, inverse, gain, count, direct):
    sums = sum_batch(jnp.stack([jnp.sum(d_out * hat, axis=0), jnp.sum(d_out, axis=0)]), direct)
    d_values = inverse * gain * (d_out - sums[1] / count - hat * (sums[0] / count))
    return d_values, sums


def shards(
    features,
    reduce_weight,
    reduce_norm,
    dilate_weight,
    dilate_norm,
    expand_weight,
    expand_norm,
    depth_head,
    segment_head,
    normal_head,
    contour_head,
    depth_message,
    segment_message,
    normal_message,
    contour_message,
    depth_gate,
    segment_gate,
    classifier,
    depth_valid,
    labels,
    block_cotangent,
    depth_cotangent,
):
    row, batch = lax.axis_index("rows"), lax.axis_index("batch")
    nrows, nbatch = lax.axis_size("rows"), lax.axis_size("batch")
    ring = Ring(batch)
    _, local_height, breadth, wide = features.shape
    mid = reduce_weight.shape[1]
    part = mid // nrows
    quarter = local_height * breadth
    height = local_height * nrows
    pixels = quarter * nrows
    count = float(pixels * nbatch)
    factor = count ** (-0.5)
    classes = classifier.shape[1]
    held = dilate_weight.shape[0]
    grain = math.gcd(held, mid) // nrows
    groups = held // (nrows * grain)
    wide_held = wide // nbatch
    wide_part = wide_held // nrows
    mid_held = mid // nbatch

    def row_slice(array, dim):
        size = array.shape[dim] // nrows
        return lax.dynamic_slice_in_dim(array, row * size, size, dim)

    channel = jnp.arange(mid)
    slot = jnp.arange(part)
    mine = (slot // grain) * (nrows * grain) + row * grain + slot % grain
    pick = (channel[:, None] == mine[None, :]).astype(jnp.float32)
    split = jnp.arange(mid)
    natural = ((split % part) // grain) * (nrows * grain) + (split // part) * grain + split % grain
    mix = (natural[:, None] == channel[None, :]).astype(jnp.bfloat16)
    here = row.astype(jnp.int32).reshape(1)

    def to_narrow(array):
        return jnp.concatenate(
            [array[:, i * part : (i + 1) * part] for i in range(nrows)], axis=0
        )

    def from_narrow(array):
        size = array.shape[1] // nrows
        return jnp.concatenate([array[:, i * size : (i + 1) * size] for i in range(nrows)], axis=2)

    tiny_width = max(mid_held, wide_part)

    def tiny(array):
        return jnp.pad(array, ((0, 0), (0, tiny_width - array.shape[1])))

    heads_mine = jnp.concatenate(
        [
            product(head, pick, 1, 0, EXACT)
            for head in (segment_head, normal_head, depth_head, contour_head)
        ],
        axis=1,
    )
    heads_full = lax.all_gather(heads_mine, "batch", axis=0, tiled=True)

    def message_runs(array):
        runs = array.reshape(groups, nrows, grain, mid)
        return lax.dynamic_index_in_dim(runs, row, 1, keepdims=True)

    def message_pair(first, second):
        return jnp.concatenate([message_runs(first), message_runs(second)], axis=1)

    run = grain if grain % 8 == 0 else part
    segment_pair_mine = message_pair(segment_message, contour_message).reshape(held // 2, mid)
    depth_pair_mine = message_pair(depth_message, normal_message).reshape(held // 2, mid)
    segment_pair_w, depth_pair_w = [
        regroup(
            lax.all_gather(mine, "batch", axis=0, tiled=True).reshape(
                nbatch * groups, 2, grain, mid
            ),
            run,
        )
        for mine in (segment_pair_mine, depth_pair_mine)
    ]

    expand_norm_mine = lax.dynamic_index_in_dim(
        expand_norm.reshape(2, nrows, wide_part), row, 1, keepdims=False
    )
    params = jnp.concatenate([tiny(reduce_norm), tiny(dilate_norm), tiny(expand_norm_mine)], axis=0)
    params = jnp.pad(params, ((0, 2), (0, part - tiny_width)))
    expand_mine = lax.dynamic_index_in_dim(
        expand_weight.reshape(mid_held, nbatch, nrows, wide_part), row, 2, keepdims=False
    ).reshape(mid_held, nbatch * wide_part)
    class_lanes = -(-classes // part) * part

    def packed(pieces):
        spans, start = {}, 0
        for name, piece in pieces.items():
            spans[name] = slice(start, start + piece.shape[0])
            start += piece.shape[0]
        return jnp.concatenate(list(pieces.values()), axis=0), spans

    first_mine, first_spans = packed(
        {
            "reduce": to_narrow(row_slice(reduce_weight, 0)),
            "params": params,
            "dilate": row_slice(dilate_weight, 1),
        }
    )
    first_all, _ = ring.gather(first_mine, True)
    reduce_full = from_narrow(first_all[:, first_spans["reduce"]]).reshape(nbatch * wide_part, mid)
    params_all = first_all[:, first_spans["params"]]
    dilate_full = first_all[:, first_spans["dilate"]].reshape(nbatch * held, part)

    def all_params(pair, size):
        return jnp.transpose(params_all[:, pair : pair + 2, :size], (1, 0, 2)).reshape(2, nbatch * size)

    reduce_gain, reduce_bias = row_slice(all_params(0, mid_held), 1)
    dilate_gain, dilate_bias = row_slice(all_params(2, mid_held), 1)
    expand_gain, expand_bias = all_params(4, wide_part)

    spread_by_kernel = wide_part == 64 and part % 128 == 0

    def spread_wide(array):
        if spread_by_kernel:
            (blocks,) = single_call(
                spread_kernel, (here, array), [(nrows, quarter, wide // nrows)], [], 1
            )
            blocks = [blocks[key] for key in range(4)]
        else:
            split_blocks = jnp.transpose(array.reshape(quarter, nbatch, nrows, wide_part), (2, 0, 1, 3))
            split_blocks = split_blocks.reshape(nrows, quarter, nbatch * wide_part)
            blocks = [
                lax.dynamic_index_in_dim(split_blocks, row ^ key, 0, keepdims=False)
                for key in range(4)
            ]
        return jnp.concatenate(in_order(exchange_keyed(blocks), row), axis=0)

    def exchange_wide(array):
        blocks = array.reshape(nrows, quarter, nbatch * wide_part)
        return exchange_keyed(
            [lax.dynamic_index_in_dim(blocks, row ^ key, 0, keepdims=False) for key in range(4)]
        )

    def collect_wide(got):
        if spread_by_kernel:
            (out,) = single_call(
                collect_kernel,
                (here, *got),
                [(quarter, wide)],
                [(nrows, quarter, wide // nrows)],
                1,
            )
        else:
            out = jnp.stack(in_order(got, row)).reshape(nrows, quarter, nbatch, wide_part)
            out = jnp.transpose(out, (1, 2, 0, 3))
        return out.reshape(1, local_height, breadth, wide)

    def image_of(array):
        return array.reshape(height, breadth, array.shape[-1])

    features, _ = lax.optimization_barrier((features, (heads_mine, segment_pair_mine, first_mine)))
    inputs = spread_wide(features.reshape(quarter, wide))

    valid = depth_valid.astype(jnp.float32).reshape(quarter, 1)
    keep, give = single_call(
        split_product_kernel,
        (here, inputs, reduce_full, jnp.full((1, part), jnp.sum(valid))),
        [(2, pixels + 8, part)] * 2,
        [(pixels, mid)],
        2 * pixels * mid * mid,
    )
    mine_terms, got_terms = scatter_end(keep, give)
    pre_reduce = mine_terms + got_terms
    valid_row = pre_reduce[pixels]
    pre_reduce = pre_reduce[:pixels]
    total_one = sum_batch(jnp.concatenate([sums_of(pre_reduce, pre_reduce), valid_row[None]]))
    scale = valid * (count / total_one[2, 0])
    hat_one, normed_one, inverse_one = norm_forward(
        pre_reduce, total_one, reduce_gain, reduce_bias, count
    )
    pre_dilate, mid_in = joined_conv(
        here, gather_keyed(image_of(jax.nn.silu(normed_one))), dilate_full, 2
    )
    total_two = sum_batch(sums_of(pre_dilate, pre_dilate))
    total_two, heads_full = lax.optimization_barrier((total_two, heads_full))
    hat_two, normed_two, inverse_two = norm_forward(
        pre_dilate, total_two, dilate_gain, dilate_bias, count
    )

    beside = mid // class_lanes
    square_mine, square_spans = packed(
        {
            "depth_gate": depth_gate,
            "segment_gate": segment_gate,
            "expand": expand_mine,
            "classifier": jnp.pad(classifier, ((0, 0), (0, class_lanes - classes)))
            .reshape(beside, mid_held // beside, class_lanes)
            .transpose(1, 0, 2)
            .reshape(mid_held // beside, mid),
        }
    )
    square_mine, inverse_two = lax.optimization_barrier((square_mine, inverse_two))
    feats, mid_out, pairs = joined_conv(
        here, gather_keyed(image_of(jax.nn.silu(normed_two))), heads_full, 1, True
    )
    square_all, feats = ring.gather(square_mine, False, feats, 2)
    square_all, segment_pair_w = lax.optimization_barrier((square_all, segment_pair_w))
    depth_gate_w, segment_gate_w, expand_w = [
        square_all[:, square_spans[name]].reshape(mid, mid)
        for name in ("depth_gate", "segment_gate", "expand")
    ]
    classifier_w = (
        square_all[:, square_spans["classifier"]]
        .reshape(nbatch, mid_held // beside, beside, class_lanes)
        .transpose(0, 2, 1, 3)
        .reshape(mid, class_lanes)
    )
    feats_image = image_of(feats)

    segment_mine, segment_got = scatter_end(*note_forward(here, feats_image, 1, segment_pair_w))
    pairs_got = jnp.stack(exchange_keyed([pairs[key] for key in range(4)]))
    block_cotangent, _ = lax.optimization_barrier((block_cotangent, feats))
    cotangent = spread_wide(block_cotangent.reshape(quarter, wide))
    pairs_got, segment_mine, cotangent = lax.optimization_barrier((pairs_got, segment_mine, cotangent))
    depth_cotangent = depth_cotangent.reshape(quarter, mid)
    both, one_map = (2 * quarter, mid), (quarter, mid)
    feat_pair, open_pair, d_depth_note = single_call(
        gates_kernel,
        (here, pairs_got, mix, depth_gate_w, segment_gate_w, depth_cotangent, scale),
        [both, both, one_map],
        [both],
        8 * quarter * mid * mid,
    )

    def segment_body(*refs):
        segment_kernel(classes, *refs)

    segment_stream, d_segment_note, direct_segment, segment_gate_grad, classifier_grad = single_call(
        segment_body,
        (
            here,
            segment_mine,
            segment_got,
            feat_pair[quarter:],
            open_pair[quarter:],
            labels.reshape(quarter, 1),
            classifier_w,
            segment_gate_w,
            mix,
        ),
        [one_map, one_map, (4, quarter, part), (mid, mid), (mid, class_lanes)],
        [one_map],
        8 * quarter * mid * mid,
    )

    def lines(array):
        return array.reshape(local_height, breadth, mid)

    d_depth_blocks, d_segment_note = lax.optimization_barrier(
        (gather_keyed(lines(d_depth_note)), d_segment_note)
    )
    depth_pair_grad, d_depth_image = note_grad(here, feats, 0, d_depth_blocks, run)
    depth_pair_sums = lax.psum_scatter(
        regroup(depth_pair_grad, grain).reshape(-1, mid), "batch", scatter_dimension=0, tiled=True
    )
    segment_pair_grad, d_segment_image = note_grad(
        here, feats, 1, gather_keyed(lines(d_segment_note)), run
    )
    flat_mid_out = mid_out.reshape(pixels, mid)
    expand_input, _ = lax.optimization_barrier((flat_mid_out, d_segment_note))
    pre_expand = product(expand_input, expand_w, 1, 0)
    hat_three, normed_three, inverse_three = norm_forward(
        pre_expand, sum_batch(sums_of(pre_expand, pre_expand)), expand_gain, expand_bias, count
    )
    summed = normed_three + inputs
    block_blocks = exchange_wide(jax.nn.silu(summed))
    d_summed = cotangent * silu_grad(summed)
    d_pre_expand, expand_sums = norm_backward(
        d_summed, hat_three, inverse_three, expand_gain, count, False
    )

    feats_late, depth_pair_w, _ = lax.optimization_barrier(
        (feats_image, depth_pair_w, (segment_pair_grad, depth_pair_grad, expand_sums))
    )
    segment_pair_grad, _ = lax.optimization_barrier((segment_pair_grad, expand_sums))
    hops = Hops(ring, regroup(segment_pair_grad, grain).reshape(nbatch, held // 2, mid), True)
    depth_mine, depth_got = scatter_end(*note_forward(here, feats_late, 0, depth_pair_w))
    depth_back = note_back(hops.step(d_depth_image), depth_pair_w)
    depth_stream, direct_both, depth_gate_grad = single_call(
        depth_kernel,
        (
            here,
            depth_mine,
            depth_got,
            feat_pair[:quarter],
            open_pair[:quarter],
            depth_cotangent,
            scale,
            depth_gate_w,
            mix,
            direct_segment,
        ),
        [one_map, (4, 2 * quarter, part), (mid, mid)],
        [one_map],
        8 * quarter * mid * mid,
    )
    direct_got = jnp.stack(exchange_keyed([direct_both[key] for key in range(4)]))
    segment_back = note_back(hops.step(d_segment_image), segment_pair_w)
    heads_grad, d_feats = heads_grad_of(
        here,
        hops.step(flat_mid_out),
        image_of(depth_back),
        image_of(segment_back),
        direct_got.reshape(4, 2 * local_height, breadth, part),
    )
    heads_sums = lax.psum_scatter(heads_grad, "batch", scatter_dimension=0, tiled=True)

    expand_grad = product(flat_mid_out, d_pre_expand, 0, 0).reshape(nbatch, mid_held, mid)

    gate_terms = jnp.stack(
        [
            depth_gate_grad,
            segment_gate_grad,
            jnp.pad(classifier_grad, ((0, 0), (0, mid - class_lanes))),
        ]
    )
    gate_rows = mid_held // nrows
    gate_terms = jnp.transpose(gate_terms.reshape(3, nbatch, nrows, gate_rows, mid), (2, 1, 0, 3, 4))
    gate_sums = scatter_rows(gate_terms, row).reshape(nbatch, 3 * gate_rows, mid)

    d_feats, block_blocks = lax.optimization_barrier((hops.step(d_feats), block_blocks))
    block_out = collect_wide(block_blocks)
    segment_pair_sums = hops.result()
    mine_terms, got_terms = scatter_end(
        *conv_back(here, d_feats, heads_full, 1, product(d_pre_expand, expand_w, 1, 1))
    )
    d_pre_dilate, dilate_sums = norm_backward(
        (mine_terms + got_terms) * silu_grad(normed_two), hat_two, inverse_two, dilate_gain, count, False
    )
    d_dilate_image = image_of(d_pre_dilate)
    mine_terms, got_terms = scatter_end(*conv_back(here, d_dilate_image, dilate_full, 2))
    d_pre_reduce, reduce_sums = norm_backward(
        (mine_terms + got_terms) * silu_grad(normed_one), hat_one, inverse_one, reduce_gain, count, False
    )
    reduce_grad, features_back = single_call(
        reduce_back_kernel,
        (here, *gather_keyed(d_pre_reduce), inputs, reduce_full, d_summed),
        [(mid, mid), (pixels, mid)],
        [(pixels, mid)],
        4 * pixels * mid * mid,
    )
    dilate_grad = conv_grad(mid_in.reshape(pixels, mid), d_dilate_image, 2).reshape(
        nbatch, held, part
    )
    narrow = held // nrows
    square_grad = jnp.concatenate(
        [
            jnp.concatenate(
                [dilate_grad[:, i * narrow : (i + 1) * narrow] for i in range(nrows)], axis=2
            ),
            expand_grad,
            gate_sums,
        ],
        axis=1,
    )
    square_grad, reduce_sums, depth_pair_sums, segment_pair_sums = lax.optimization_barrier(
        (square_grad, reduce_sums, depth_pair_sums, segment_pair_sums)
    )
    square_sums = ring.scatter(square_grad, False)
    reduce_out = ring.scatter(reduce_grad.reshape(nbatch, wide_part, mid), True)
    features_grad = collect_wide(exchange_wide(features_back))

    pair_sums = jnp.concatenate([depth_pair_sums, segment_pair_sums], axis=0) * factor
    pairs_out = jnp.stack(gather_rows(pair_sums, row)).reshape(nrows, 2, groups, 2, grain, mid)
    depth_pair_out, segment_pair_out = pairs_out[:, 0], pairs_out[:, 1]

    def message_out(pair_got, index):
        return jnp.transpose(pair_got[:, :, index], (1, 0, 2, 3)).reshape(held, mid)

    segment_out, normal_out, depth_out, contour_out = single_call(
        heads_out_kernel,
        (here, *gather_keyed(heads_sums * factor), mix),
        [(held, mid)] * 4,
        [(held, mid)],
        8 * held * mid * mid,
    )

    expand_mine_sums = lax.dynamic_slice_in_dim(expand_sums, batch * wide_part, wide_part, 1)
    norm_sums = jnp.concatenate(
        [
            jnp.pad(sums, ((0, 0), (0, mid - sums.shape[1])))
            for sums in (reduce_sums, dilate_sums, expand_mine_sums)
        ],
        axis=0,
    )
    small = jnp.concatenate([square_sums, jnp.pad(norm_sums, ((0, 2), (0, 0)))], axis=0) * factor
    small_got = gather_rows(small, row)
    squares_got = jnp.stack([block[narrow : narrow + mid_held + 3 * gate_rows] for block in small_got])
    dilate_out = jnp.concatenate(
        [
            jnp.concatenate(
                [block[:narrow, i * part : (i + 1) * part] for i in range(nrows)], axis=0
            )
            for block in small_got
        ],
        axis=1,
    )
    expand_out = jnp.transpose(
        squares_got[:, :mid_held].reshape(nrows, mid_held, nbatch, wide_part), (1, 2, 0, 3)
    ).reshape(mid_held, wide)

    def gate_out(index):
        start = mid_held + index * gate_rows
        return squares_got[:, start : start + gate_rows].reshape(mid_held, mid)

    norms_got = [block[-8:] for block in small_got]

    def norm_out(start):
        full = jnp.concatenate([block[start : start + 2, :part] for block in norms_got], axis=1)
        return lax.dynamic_slice_in_dim(full, batch * mid_held, mid_held, 1)

    expand_norm_out = jnp.concatenate([block[4:6, :wide_part] for block in norms_got], axis=1)
    reduce_got = jnp.concatenate(gather_rows(reduce_out * factor, row), axis=0)

    return (
        block_out,
        depth_stream.reshape(1, local_height, breadth, mid),
        segment_stream.reshape(1, local_height, breadth, mid),
        features_grad,
        reduce_got,
        norm_out(0),
        dilate_out,
        norm_out(2),
        expand_out,
        expand_norm_out,
        depth_out,
        segment_out,
        normal_out,
        contour_out,
        message_out(depth_pair_out, 0),
        message_out(segment_pair_out, 0),
        message_out(depth_pair_out, 1),
        message_out(segment_pair_out, 1),
        gate_out(0),
        gate_out(1),
        gate_out(2)[:, :classes],
    )


def solution(mesh):
    pixels = P("batch", "rows", None, None)
    plane = P("batch", "rows", None)
    weight = P("batch", None)
    norm = P(None, "batch")
    in_specs = (
        (pixels, weight, norm, weight, norm, weight, norm) + (weight,) * 11 + (plane, plane, pixels, pixels)
    )
    out_specs = (pixels,) * 4 + (weight, norm) * 3 + (weight,) * 11
    return jax.shard_map(shards, mesh=mesh, in_specs=in_specs, out_specs=out_specs, check_vma=False)
```

```python
import math

import jax
import jax.numpy as jnp
from jax import lax
from jax.experimental import pallas as pl
from jax.experimental.pallas import tpu as pltpu
from jax.sharding import PartitionSpec as P

EPSILON = 1e-05
EXACT = lax.Precision.HIGHEST
FINE = lax.Precision.HIGH
LONGEST_RING = 8
LANES = 128


def product(left, right, left_dim, right_dim, precision=FINE):
    return lax.dot_general(
        left,
        right,
        (((left_dim,), (right_dim,)), ((), ())),
        precision=precision,
        preferred_element_type=jnp.float32,
    )


def halves(values):
    high = values.astype(jnp.bfloat16)
    return high, (values - high.astype(jnp.float32)).astype(jnp.bfloat16)


def three_pass(left, right, left_dim, right_dim):
    dims = (((left_dim,), (right_dim,)), ((), ()))

    def one(a, b):
        return lax.dot_general(a, b, dims, preferred_element_type=jnp.float32)

    return one(left[0], right[0]) + (one(left[0], right[1]) + one(left[1], right[0]))


def frame(image_ref, framed, dilation):
    height, breadth, depth = image_ref.shape
    edge = jnp.zeros((3, dilation, breadth, depth), jnp.float32)
    framed[:, :dilation] = edge
    framed[:, dilation + height :] = edge
    image = image_ref[...]
    side = jnp.zeros((height, dilation, depth), jnp.float32)
    inner = slice(dilation, dilation + height)
    framed[1, inner] = image
    framed[0, inner, dilation:, :] = image[:, : breadth - dilation]
    framed[0, inner, :dilation, :] = side
    framed[2, inner, : breadth - dilation, :] = image[:, dilation:]
    framed[2, inner, breadth - dilation :, :] = side


def shifted(framed, tap, height, dilation):
    block = framed[tap % 3, pl.ds((tap // 3) * dilation, height)]
    return block.reshape(height * block.shape[1], block.shape[2])


def exact_pick(values, choice, choice_dim):
    high = values.astype(jnp.bfloat16)
    rest = values - high.astype(jnp.float32)
    middle = rest.astype(jnp.bfloat16)
    low = (rest - middle.astype(jnp.float32)).astype(jnp.bfloat16)
    dims = (((1,), (choice_dim,)), ((), ()))

    def one(part):
        return lax.dot_general(part, choice, dims, preferred_element_type=jnp.float32)

    return one(high) + (one(middle) + one(low))


def at_lanes(index, size):
    return pl.ds(pl.multiple_of(index * size, size), size)


def keep_and_give(row, load, keep_ref, give_ref):
    core, side = row & 1, row >> 1
    for k in range(2):
        base = (side ^ k) * 2
        keep_ref[k] = load(base + core)
        give_ref[k] = load(base + 1 - core)


def joined_conv_kernel(dilation, row_ref, one, two, three, four, weight_ref, out_ref, image_ref, framed):
    tap = pl.program_id(0)

    @pl.when(tap == 0)
    def _():
        part = one.shape[2]
        for key, block in enumerate((one, two, three, four)):
            image_ref[:, :, at_lanes(row_ref[0] ^ key, part)] = block[...]
        frame(image_ref, framed, dilation)
        out_ref[...] = jnp.zeros_like(out_ref)

    moved = halves(shifted(framed, tap, image_ref.shape[0], dilation))
    out_ref[...] += three_pass(moved, halves(weight_ref[...]), 1, 0)


def heads_kernel(
    row_ref, one, two, three, four, weight_ref, out_ref, image_ref, pairs_ref, framed
):
    joined_conv_kernel(1, row_ref, one, two, three, four, weight_ref, out_ref, image_ref, framed)

    @pl.when(pl.program_id(0) == 8)
    def _():
        _, double, part = pairs_ref.shape
        quarter = double // 2
        for key in range(4):
            rows = pl.ds((row_ref[0] ^ key) * quarter, quarter)
            pairs_ref[key, :quarter] = out_ref[rows, 2 * part : 3 * part]
            pairs_ref[key, quarter:] = out_ref[rows, :part]


def split_product_kernel(row_ref, left_ref, right_ref, extra_ref, keep_ref, give_ref, total):
    total[...] = three_pass(halves(left_ref[...]), halves(right_ref[...]), 1, 0)
    pixels, part = left_ref.shape[0], keep_ref.shape[2]
    keep_and_give(
        row_ref[0],
        lambda j: total[:, at_lanes(j, part)],
        keep_ref.at[:, :pixels],
        give_ref.at[:, :pixels],
    )
    for ref in (keep_ref, give_ref):
        ref[:, pixels:] = jnp.broadcast_to(extra_ref[...], (2, 8, part))


def conv_back_kernel(dilation, row_ref, image_ref, weight_ref, *rest):
    extra_ref = rest[0] if len(rest) == 5 else None
    keep_ref, give_ref, framed, total = rest[-4:]
    tap = pl.program_id(0)

    @pl.when(tap == 0)
    def _():
        frame(image_ref, framed, dilation)
        total[...] = jnp.zeros_like(total) if extra_ref is None else extra_ref[...]

    moved = halves(shifted(framed, 8 - tap, image_ref.shape[0], dilation))
    total[...] += three_pass(moved, halves(weight_ref[...]), 1, 1)

    @pl.when(tap == 8)
    def _():
        part = keep_ref.shape[2]
        keep_and_give(row_ref[0], lambda j: total[:, at_lanes(j, part)], keep_ref, give_ref)


def conv_grad_kernel(dilation, input_ref, grad_ref, out_ref, framed, high, low):
    tap = pl.program_id(0)

    @pl.when(tap == 0)
    def _():
        frame(grad_ref, framed, dilation)
        high[...], low[...] = halves(jnp.transpose(input_ref[...]))

    moved = halves(shifted(framed, 8 - tap, grad_ref.shape[0], dilation))
    out_ref[...] = three_pass((high[...], low[...]), moved, 1, 0)


def heads_grad_kernel(
    row_ref, input_ref, first_ref, second_ref, direct_ref, out_ref, image_ref, framed, high, low
):
    tap = pl.program_id(0)

    @pl.when(tap == 0)
    def _():
        lanes = first_ref.shape[2]
        _, double, breadth, part = direct_ref.shape
        lines = double // 2
        image_ref[:, :, :lanes] = first_ref[...]
        image_ref[:, :, lanes:] = second_ref[...]
        for key in range(4):
            rows = pl.ds((row_ref[0] ^ key) * lines, lines)
            image_ref[rows, :, :part] += direct_ref[key, :lines]
            image_ref[rows, :, lanes : lanes + part] += direct_ref[key, lines:]

    conv_grad_kernel(1, input_ref, image_ref, out_ref, framed, high, low)


def source_rows(weight):
    return jnp.concatenate(
        [weight[:, k].reshape(-1, weight.shape[-1]) for k in range(weight.shape[1])], axis=0
    )


def note_kernel(row_ref, image_ref, weight_ref, keep_ref, give_ref, framed, total):
    tap = pl.program_id(0)

    @pl.when(tap == 0)
    def _():
        frame(image_ref, framed, 1)
        total[...] = jnp.zeros_like(total)

    moved = shifted(framed, tap, image_ref.shape[0], 1)
    total[...] += three_pass(halves(moved), halves(source_rows(weight_ref[...])), 1, 0)

    @pl.when(tap == 8)
    def _():
        quarter = keep_ref.shape[1]
        keep_and_give(
            row_ref[0], lambda j: total[pl.ds(j * quarter, quarter), :], keep_ref, give_ref
        )


def note_back_kernel(note_ref, weight_ref, out_ref, framed):
    tap = pl.program_id(0)

    @pl.when(tap == 0)
    def _():
        frame(note_ref, framed, 1)
        out_ref[...] = jnp.zeros_like(out_ref)

    moved = halves(shifted(framed, 8 - tap, note_ref.shape[0], 1))
    out_ref[...] += three_pass(moved, halves(source_rows(weight_ref[...])), 1, 1)


def note_grad_kernel(
    row_ref, input_ref, one, two, three, four, out_ref, image_ref, framed, high, low
):
    tap = pl.program_id(0)

    @pl.when(tap == 0)
    def _():
        lines = one.shape[0]
        for key, block in enumerate((one, two, three, four)):
            image_ref[pl.ds((row_ref[0] ^ key) * lines, lines)] = block[...]
        frame(image_ref, framed, 1)
        high[...], low[...] = halves(jnp.transpose(input_ref[...]))

    moved = halves(shifted(framed, 8 - tap, image_ref.shape[0], 1))
    grad = three_pass((high[...], low[...]), moved, 1, 0)
    runs, _, grain, mid = out_ref.shape
    part = grad.shape[0] // 2
    for k in range(2):
        out_ref[:, k] = grad[k * part : (k + 1) * part].reshape(runs, grain, mid)


def gates_kernel(
    row_ref, pairs_ref, mix_ref, depth_gate_ref, segment_gate_ref, cotangent_ref, scale_ref,
    feat_ref, open_ref, d_note_ref, joined,
):
    _, double, part = pairs_ref.shape
    quarter = double // 2
    for key in range(4):
        joined[:, at_lanes(row_ref[0] ^ key, part)] = pairs_ref[key]
    feat = exact_pick(joined[...], mix_ref[...], 0)
    feat_ref[...] = feat
    for index, gate_ref in enumerate((depth_gate_ref, segment_gate_ref)):
        rows = slice(index * quarter, (index + 1) * quarter)
        gate = three_pass(halves(feat[rows]), halves(gate_ref[...]), 1, 0)
        open_ref[rows] = jax.nn.sigmoid(gate)
    d_note_ref[...] = cotangent_ref[...] * scale_ref[...] * open_ref[:quarter]


def gate_back(row_ref, feat, opened, note, d_stream, d_note, gate_ref, mix_ref, gate_grad_ref, joined):
    d_pre = halves(d_note * note * (1.0 - opened))
    gate_grad_ref[...] = three_pass(halves(jnp.transpose(feat)), d_pre, 1, 0)
    direct = d_stream + three_pass(d_pre, halves(gate_ref[...]), 1, 1)
    joined[...] = exact_pick(direct, mix_ref[...], 1)


def segment_kernel(
    classes, row_ref, mine_ref, got_ref, feat_ref, open_ref, labels_ref, classifier_ref, gate_ref, mix_ref,
    stream_ref, d_note_ref, direct_ref, gate_grad_ref, classifier_grad_ref, joined,
):
    note = mine_ref[...] + got_ref[...]
    feat, opened = feat_ref[...], open_ref[...]
    stream = feat + opened * note
    stream_ref[...] = stream
    weight = halves(classifier_ref[...])
    logits = three_pass(halves(stream), weight, 1, 0)
    lane = lax.broadcasted_iota(jnp.int32, logits.shape, 1)
    real = lane < classes
    top = jnp.max(jnp.where(real, logits, -3e38), axis=1, keepdims=True)
    powers = jnp.where(real, jnp.exp(jnp.where(real, logits - top, 0.0)), 0.0)
    onehot = jnp.where(lane == labels_ref[...], 1.0, 0.0)
    d_logits = powers / jnp.sum(powers, axis=1, keepdims=True) - onehot
    d_stream = three_pass(halves(d_logits), weight, 1, 1)
    d_note = d_stream * opened
    d_note_ref[...] = d_note
    classifier_grad_ref[...] = three_pass(halves(jnp.transpose(stream)), halves(d_logits), 1, 0)
    gate_back(row_ref, feat, opened, note, d_stream, d_note, gate_ref, mix_ref, gate_grad_ref, joined)
    part = direct_ref.shape[2]
    for key in range(4):
        direct_ref[key] = joined[:, at_lanes(row_ref[0] ^ key, part)]


def depth_kernel(
    row_ref, mine_ref, got_ref, feat_ref, open_ref, cotangent_ref, scale_ref, gate_ref, mix_ref, other_ref,
    stream_ref, direct_ref, gate_grad_ref, joined,
):
    note = mine_ref[...] + got_ref[...]
    feat, opened = feat_ref[...], open_ref[...]
    stream_ref[...] = feat + opened * note
    d_stream = cotangent_ref[...] * scale_ref[...]
    gate_back(
        row_ref, feat, opened, note, d_stream, d_stream * opened, gate_ref, mix_ref, gate_grad_ref, joined
    )
    _, double, part = direct_ref.shape
    quarter = double // 2
    for key in range(4):
        direct_ref[key, :quarter] = other_ref[key]
        direct_ref[key, quarter:] = joined[:, at_lanes(row_ref[0] ^ key, part)]


def reduce_back_kernel(
    row_ref, one, two, three, four, input_ref, weight_ref, d_summed_ref, grad_ref, out_ref, joined
):
    part = one.shape[1]
    for key, block in enumerate((one, two, three, four)):
        joined[:, at_lanes(row_ref[0] ^ key, part)] = block[...]
    d_pre = halves(joined[...])
    grad_ref[...] = three_pass(halves(jnp.transpose(input_ref[...])), d_pre, 1, 0)
    out_ref[...] = d_summed_ref[...] + three_pass(d_pre, halves(weight_ref[...]), 1, 1)


def heads_out_kernel(row_ref, one, two, three, four, mix_ref, *rest):
    outs, joined = rest[:-1], rest[-1]
    part = joined.shape[1] // 4
    for index, out_ref in enumerate(outs):
        lanes = slice(index * part, (index + 1) * part)
        for key, block in enumerate((one, two, three, four)):
            joined[:, at_lanes(row_ref[0] ^ key, part)] = block[:, lanes]
        out_ref[...] = exact_pick(joined[...], mix_ref[...], 0)


def spread_kernel(row_ref, array_ref, out_ref):
    low = lax.broadcasted_iota(jnp.int32, (array_ref.shape[0], 128), 1) < 64
    for device in range(4):
        key = row_ref[0] ^ device
        for k in range(out_ref.shape[2] // 128):
            start = 512 * k + 128 * (device // 2)
            even = array_ref[:, start : start + 128]
            odd = array_ref[:, start + 256 : start + 384]
            if device % 2:
                block = jnp.where(low, pltpu.roll(even, 64, 1), odd)
            else:
                block = jnp.where(low, even, pltpu.roll(odd, 64, 1))
            out_ref[key, :, 128 * k : 128 * (k + 1)] = block


def collect_kernel(row_ref, one, two, three, four, out_ref, ordered):
    for key, block in enumerate((one, two, three, four)):
        ordered[row_ref[0] ^ key] = block[...]
    low = lax.broadcasted_iota(jnp.int32, (one.shape[0], 128), 1) < 64
    for k in range(one.shape[1] // 128):
        for pair in range(2):
            first = ordered[2 * pair, :, 128 * k : 128 * (k + 1)]
            second = ordered[2 * pair + 1, :, 128 * k : 128 * (k + 1)]
            start = 512 * k + 128 * pair
            out_ref[:, start : start + 128] = jnp.where(low, first, pltpu.roll(second, 64, 1))
            out_ref[:, start + 256 : start + 384] = jnp.where(low, pltpu.roll(first, 64, 1), second)


def regroup(array, run):
    runs, sources, grain, mid = array.shape
    if grain == run:
        return array
    if run > grain:
        lists = array.reshape(-1, run // grain, sources, grain, mid)
        return jnp.transpose(lists, (0, 2, 1, 3, 4)).reshape(-1, sources, run, mid)
    parts = array.reshape(runs, sources, grain // run, run, mid)
    return jnp.transpose(parts, (0, 2, 1, 3, 4)).reshape(-1, sources, run, mid)


VMEM_LIMIT = 56 * 2**20
SCALAR = pl.BlockSpec(memory_space=pltpu.SMEM)


def kernel_call(body, grid, in_specs, out_specs, out_shape, scratch, flops):
    return pl.pallas_call(
        body,
        grid=grid,
        in_specs=in_specs,
        out_specs=out_specs,
        out_shape=out_shape,
        scratch_shapes=scratch,
        compiler_params=pltpu.CompilerParams(
            dimension_semantics=("arbitrary",) * len(grid), vmem_limit_bytes=VMEM_LIMIT
        ),
        cost_estimate=pl.CostEstimate(flops=3 * flops, bytes_accessed=12 * 2**20, transcendentals=0),
    )


def single_call(body, args, outs, scratch, flops):
    return kernel_call(
        body,
        (1,),
        [SCALAR] + [whole_spec(arg.shape) for arg in args[1:]],
        [whole_spec(out) for out in outs],
        [jax.ShapeDtypeStruct(out, jnp.float32) for out in outs],
        [pltpu.VMEM(shape, jnp.float32) for shape in scratch],
        flops,
    )(*args)


def framed_scratch(image, dilation):
    height, breadth, depth = image
    return pltpu.VMEM((3, height + 2 * dilation, breadth, depth), jnp.float32)


def whole_spec(shape):
    return pl.BlockSpec(shape, lambda *_: (0,) * len(shape))


def struct(shape):
    return jax.ShapeDtypeStruct(shape, jnp.float32)


def tap_rows(rows, cols):
    return pl.BlockSpec((rows, cols), lambda tap: (tap, 0))


def tap_runs(weight_shape):
    return pl.BlockSpec((weight_shape[0] // 9,) + weight_shape[1:], lambda tap: (tap, 0, 0, 0))


def joined_conv(row, blocks, weight, dilation, with_pairs=False):
    height, breadth, part = blocks[0].shape
    image = (height, breadth, 4 * part)
    rows, cols = weight.shape[0] // 9, weight.shape[1]
    shapes = [(height * breadth, cols), image]
    if with_pairs:
        body = heads_kernel
        shapes.append((4, height * breadth // 2, part))
    else:

        def body(*refs):
            joined_conv_kernel(dilation, *refs)

    return kernel_call(
        body,
        (9,),
        [SCALAR] + [whole_spec(blocks[0].shape)] * 4 + [tap_rows(rows, cols)],
        [whole_spec(shape) for shape in shapes],
        [struct(shape) for shape in shapes],
        [framed_scratch(image, dilation)],
        2 * 9 * height * breadth * rows * cols,
    )(row, *blocks, weight)


def conv_back(row, image, weight, dilation, extra=None):
    height, breadth, _ = image.shape
    rows, cols = weight.shape[0] // 9, weight.shape[1]
    pixels = height * breadth
    shape = (2, pixels, rows // 4)

    def body(*refs):
        conv_back_kernel(dilation, *refs)

    extras = [] if extra is None else [extra]
    return kernel_call(
        body,
        (9,),
        [SCALAR, whole_spec(image.shape), tap_rows(rows, cols)]
        + [whole_spec(array.shape) for array in extras],
        [whole_spec(shape)] * 2,
        [struct(shape)] * 2,
        [framed_scratch(image.shape, dilation), pltpu.VMEM((pixels, rows), jnp.float32)],
        2 * 9 * pixels * rows * cols,
    )(row, image, weight, *extras)


def conv_grad(flat_input, image_grad, dilation):
    pixels, depth = flat_input.shape
    cols = image_grad.shape[2]

    def body(*refs):
        conv_grad_kernel(dilation, *refs)

    return kernel_call(
        body,
        (9,),
        [whole_spec(flat_input.shape), whole_spec(image_grad.shape)],
        tap_rows(depth, cols),
        struct((9 * depth, cols)),
        [framed_scratch(image_grad.shape, dilation)]
        + [pltpu.VMEM((depth, pixels), jnp.bfloat16)] * 2,
        2 * 9 * pixels * depth * cols,
    )(flat_input, image_grad)


def heads_grad_of(row, flat_input, first, second, direct):
    pixels, depth = flat_input.shape
    height, breadth, lanes = first.shape
    image = (height, breadth, 2 * lanes)
    return kernel_call(
        heads_grad_kernel,
        (9,),
        [SCALAR] + [whole_spec(array.shape) for array in (flat_input, first, second, direct)],
        [tap_rows(depth, 2 * lanes), whole_spec(image)],
        [struct((9 * depth, 2 * lanes)), struct(image)],
        [framed_scratch(image, 1)] + [pltpu.VMEM((depth, pixels), jnp.bfloat16)] * 2,
        2 * 9 * pixels * depth * 2 * lanes,
    )(row, flat_input, first, second, direct)


def note_forward(row, image, pair, weight):
    height, breadth, depth = image.shape
    depth = depth // 2
    mid = weight.shape[3]
    pixels = height * breadth
    shape = (2, pixels // 4, mid)
    return kernel_call(
        note_kernel,
        (9,),
        [
            SCALAR,
            pl.BlockSpec((height, breadth, depth), lambda tap: (0, 0, pair)),
            tap_runs(weight.shape),
        ],
        [whole_spec(shape)] * 2,
        [struct(shape)] * 2,
        [framed_scratch((height, breadth, depth), 1), pltpu.VMEM((pixels, mid), jnp.float32)],
        2 * 9 * pixels * depth * mid,
    )(row, image, weight)


def note_back(note, weight):
    height, breadth, mid = note.shape
    shape = (height * breadth, weight.shape[0] // 9 * weight.shape[1] * weight.shape[2])
    return kernel_call(
        note_back_kernel,
        (9,),
        [whole_spec(note.shape), tap_runs(weight.shape)],
        whole_spec(shape),
        struct(shape),
        [framed_scratch(note.shape, 1)],
        2 * 9 * shape[0] * shape[1] * mid,
    )(note, weight)


def note_grad(row, flat_input, pair, blocks, grain):
    pixels, depth = flat_input.shape
    depth = depth // 2
    lines, breadth, mid = blocks[0].shape
    image = (4 * lines, breadth, mid)
    runs = depth // 2 // grain
    grad = (9 * runs, 2, grain, mid)
    return kernel_call(
        note_grad_kernel,
        (9,),
        [SCALAR, pl.BlockSpec((pixels, depth), lambda tap: (0, pair))]
        + [whole_spec(blocks[0].shape)] * 4,
        [tap_runs(grad), whole_spec(image)],
        [struct(grad), struct(image)],
        [framed_scratch(image, 1)] + [pltpu.VMEM((depth, pixels), jnp.bfloat16)] * 2,
        2 * 9 * pixels * depth * mid,
    )(row, flat_input, *blocks)


def silu_grad(values):
    gate_val = jax.nn.sigmoid(values)
    return gate_val * (1.0 + values * (1.0 - gate_val))


def swap_rows(block, mask):
    size = lax.axis_size("rows")
    return lax.ppermute(block, "rows", [(i, i ^ mask) for i in range(size)])


def in_order(blocks, row):
    count = len(blocks)
    if count == 1:
        return blocks
    half = count // 2
    near = in_order(blocks[:half], row)
    far = in_order(blocks[half:], row)
    upper = (row & half) != 0
    first = [jnp.where(upper, f, n) for n, f in zip(near, far)]
    second = [jnp.where(upper, n, f) for n, f in zip(near, far)]
    return first + second


def gather_keyed(block):
    far = swap_rows(block, 2)
    return [block, swap_rows(block, 1), far, swap_rows(far, 1)]


def gather_rows(block, row):
    return in_order(gather_keyed(block), row)


def scatter_end(keep, give):
    got = swap_rows(give, 1)
    other = keep[1] + got[1]
    return keep[0] + got[0], swap_rows(other, 2)


def scatter_rows(blocks, row):
    core, side = row & 1, row >> 1
    pairs = blocks.reshape((2, 2) + blocks.shape[1:])
    keep = lax.dynamic_index_in_dim(pairs, core, 1, keepdims=False)
    got = keep + swap_rows(lax.dynamic_index_in_dim(pairs, 1 - core, 1, keepdims=False), 1)
    mine = lax.dynamic_index_in_dim(got, side, 0, keepdims=False)
    return mine + swap_rows(lax.dynamic_index_in_dim(got, 1 - side, 0, keepdims=False), 2)


def exchange_keyed(blocks):
    return [blocks[0]] + [swap_rows(blocks[mask], mask) for mask in range(1, 4)]


def sum_batch(values, direct=False):
    size = lax.axis_size("batch")
    if size & (size - 1):
        return lax.psum(values, "batch")

    def swap(block, mask):
        return lax.ppermute(block, "batch", [(i, i ^ mask) for i in range(size)])

    if direct and size <= LONGEST_RING:
        return values + sum(swap(values, mask) for mask in range(1, size))
    mask = 1
    while mask < size:
        values = values + swap(values, mask)
        mask *= 2
    return values


class Ring:
    def __init__(self, batch):
        size = lax.axis_size("batch")
        self.batch, self.size = batch, size
        self.order = list(range(0, size, 2)) + [i for i in reversed(range(size)) if i % 2]
        self.place = {b: p for p, b in enumerate(self.order)}
        self.up = [(self.order[p], self.order[(p + 1) % size]) for p in range(size)]
        self.down = [(b, a) for a, b in self.up]
        table = [[self.order[(self.place[b] + k) % size] for k in range(size)] for b in range(size)]
        self.row = jnp.array(table, jnp.int32)[batch]

    def at(self, offset):
        return self.row[offset % self.size]

    def steps(self, longer_up):
        more = self.size // 2
        less = self.size - 1 - more
        return (more, less) if longer_up else (less, more)

    def gather(self, block, longer_up, beside=None, beside_step=0):
        if self.size > LONGEST_RING:
            return lax.all_gather(block, "batch", axis=0, tiled=False), beside
        whole = jnp.zeros((self.size,) + block.shape, block.dtype)
        whole = lax.dynamic_update_index_in_dim(whole, block, self.batch, 0)
        ups, downs = self.steps(longer_up)
        rising = falling = block
        for k in range(1, max(ups, downs) + 1):
            if k == beside_step and beside is not None:
                rising, falling, beside = lax.optimization_barrier((rising, falling, beside))
            if k <= ups:
                rising = lax.ppermute(rising, "batch", self.up)
                whole = lax.dynamic_update_index_in_dim(whole, rising, self.at(-k), 0)
            if k <= downs:
                falling = lax.ppermute(falling, "batch", self.down)
                whole = lax.dynamic_update_index_in_dim(whole, falling, self.at(k), 0)
        return whole, beside

    def scatter(self, blocks, longer_up):
        hops = Hops(self, blocks, longer_up)
        while not hops.done:
            hops.step()
        return hops.result()


class Hops:
    def __init__(self, ring, blocks, longer_up):
        self.ring, self.blocks, self.hop = ring, blocks, 0
        if ring.size > LONGEST_RING:
            self.sums = lax.psum_scatter(blocks, "batch", scatter_dimension=0, tiled=False)
            self.done = True
            return
        self.sums, self.done = None, False
        self.ups, self.downs = ring.steps(longer_up)
        self.rising, self.falling = self.own(self.ups), self.own(-self.downs)

    def own(self, offset):
        return lax.dynamic_index_in_dim(self.blocks, self.ring.at(offset), 0, keepdims=False)

    def step(self, later=None):
        if self.done:
            return later
        k = self.hop
        if k < self.ups:
            self.rising = lax.ppermute(self.rising, "batch", self.ring.up)
        if k < self.downs:
            self.falling = lax.ppermute(self.falling, "batch", self.ring.down)
        if later is not None:
            self.rising, self.falling, later = lax.optimization_barrier(
                (self.rising, self.falling, later)
            )
        if k < self.ups - 1:
            self.rising = self.rising + self.own(self.ups - 1 - k)
        if k < self.downs - 1:
            self.falling = self.falling + self.own(-(self.downs - 1 - k))
        self.hop += 1
        self.done = self.hop == max(self.ups, self.downs)
        return later

    def result(self):
        return self.sums if self.sums is not None else self.own(0) + self.rising + self.falling


def sums_of(values, others):
    return jnp.stack([jnp.sum(values, axis=0), jnp.sum(values * others, axis=0)])


def norm_forward(values, total, gain, bias, count):
    center = total[0] / count
    inverse = lax.rsqrt(total[1] / count - center * center + EPSILON)
    hat = (values - center) * inverse
    return hat, hat * gain + bias, inverse


def norm_backward(d_out, hat, inverse, gain, count, direct):
    sums = sum_batch(jnp.stack([jnp.sum(d_out * hat, axis=0), jnp.sum(d_out, axis=0)]), direct)
    d_values = inverse * gain * (d_out - sums[1] / count - hat * (sums[0] / count))
    return d_values, sums


def shards(
    features,
    reduce_weight,
    reduce_norm,
    dilate_weight,
    dilate_norm,
    expand_weight,
    expand_norm,
    depth_head,
    segment_head,
    normal_head,
    contour_head,
    depth_message,
    segment_message,
    normal_message,
    contour_message,
    depth_gate,
    segment_gate,
    classifier,
    depth_valid,
    labels,
    block_cotangent,
    depth_cotangent,
):
    row, batch = lax.axis_index("rows"), lax.axis_index("batch")
    nrows, nbatch = lax.axis_size("rows"), lax.axis_size("batch")
    ring = Ring(batch)
    _, local_height, breadth, wide = features.shape
    mid = reduce_weight.shape[1]
    part = mid // nrows
    quarter = local_height * breadth
    height = local_height * nrows
    pixels = quarter * nrows
    count = float(pixels * nbatch)
    factor = count ** (-0.5)
    classes = classifier.shape[1]
    held = dilate_weight.shape[0]
    grain = math.gcd(held, mid) // nrows
    groups = held // (nrows * grain)
    wide_held = wide // nbatch
    wide_part = wide_held // nrows
    mid_held = mid // nbatch

    def row_slice(array, dim):
        size = array.shape[dim] // nrows
        return lax.dynamic_slice_in_dim(array, row * size, size, dim)

    channel = jnp.arange(mid)
    slot = jnp.arange(part)
    mine = (slot // grain) * (nrows * grain) + row * grain + slot % grain
    pick = (channel[:, None] == mine[None, :]).astype(jnp.float32)
    split = jnp.arange(mid)
    natural = ((split % part) // grain) * (nrows * grain) + (split // part) * grain + split % grain
    mix = (natural[:, None] == channel[None, :]).astype(jnp.bfloat16)
    here = row.astype(jnp.int32).reshape(1)

    def to_narrow(array):
        return jnp.concatenate(
            [array[:, i * part : (i + 1) * part] for i in range(nrows)], axis=0
        )

    def from_narrow(array):
        size = array.shape[1] // nrows
        return jnp.concatenate([array[:, i * size : (i + 1) * size] for i in range(nrows)], axis=2)

    tiny_width = max(mid_held, wide_part)

    def tiny(array):
        return jnp.pad(array, ((0, 0), (0, tiny_width - array.shape[1])))

    heads_mine = jnp.concatenate(
        [
            product(head, pick, 1, 0, EXACT)
            for head in (segment_head, normal_head, depth_head, contour_head)
        ],
        axis=1,
    )
    def message_runs(array):
        runs = array.reshape(groups, nrows, grain, mid)
        return lax.dynamic_index_in_dim(runs, row, 1, keepdims=True)

    def message_pair(first, second):
        return jnp.concatenate([message_runs(first), message_runs(second)], axis=1)

    run = grain if grain % 8 == 0 else part
    segment_pair_mine = message_pair(segment_message, contour_message).reshape(held // 2, mid)
    depth_pair_mine = message_pair(depth_message, normal_message).reshape(held // 2, mid)
    expand_norm_mine = lax.dynamic_index_in_dim(
        expand_norm.reshape(2, nrows, wide_part), row, 1, keepdims=False
    )
    params = jnp.concatenate([tiny(reduce_norm), tiny(dilate_norm), tiny(expand_norm_mine)], axis=0)
    params = jnp.pad(params, ((0, 2), (0, part - tiny_width)))
    expand_mine = lax.dynamic_index_in_dim(
        expand_weight.reshape(mid_held, nbatch, nrows, wide_part), row, 2, keepdims=False
    ).reshape(mid_held, nbatch * wide_part)
    class_lanes = -(-classes // part) * part

    def packed(pieces):
        spans, start = {}, 0
        for name, piece in pieces.items():
            spans[name] = slice(start, start + piece.shape[0])
            start += piece.shape[0]
        return jnp.concatenate(list(pieces.values()), axis=0), spans

    first_mine, first_spans = packed(
        {
            "reduce": to_narrow(row_slice(reduce_weight, 0)),
            "params": params,
            "dilate": row_slice(dilate_weight, 1),
        }
    )
    spread_by_kernel = wide_part == 64 and part % 128 == 0

    def spread_wide(array):
        if spread_by_kernel:
            (blocks,) = single_call(
                spread_kernel, (here, array), [(nrows, quarter, wide // nrows)], [], 1
            )
            blocks = [blocks[key] for key in range(4)]
        else:
            split_blocks = jnp.transpose(array.reshape(quarter, nbatch, nrows, wide_part), (2, 0, 1, 3))
            split_blocks = split_blocks.reshape(nrows, quarter, nbatch * wide_part)
            blocks = [
                lax.dynamic_index_in_dim(split_blocks, row ^ key, 0, keepdims=False)
                for key in range(4)
            ]
        return jnp.concatenate(in_order(exchange_keyed(blocks), row), axis=0)

    features, _ = lax.optimization_barrier((features, first_mine))
    inputs = spread_wide(features.reshape(quarter, wide))
    first_all, inputs = ring.gather(first_mine, True, inputs, 3)
    first_all, heads_mine, segment_pair_mine, depth_pair_mine = lax.optimization_barrier(
        (first_all, heads_mine, segment_pair_mine, depth_pair_mine)
    )
    heads_full = lax.all_gather(heads_mine, "batch", axis=0, tiled=True)
    segment_pair_w, depth_pair_w = [
        regroup(
            lax.all_gather(mine, "batch", axis=0, tiled=True).reshape(
                nbatch * groups, 2, grain, mid
            ),
            run,
        )
        for mine in (segment_pair_mine, depth_pair_mine)
    ]

    reduce_full = from_narrow(first_all[:, first_spans["reduce"]]).reshape(nbatch * wide_part, mid)
    params_all = first_all[:, first_spans["params"]]
    dilate_full = first_all[:, first_spans["dilate"]].reshape(nbatch * held, part)

    def all_params(pair, size):
        return jnp.transpose(params_all[:, pair : pair + 2, :size], (1, 0, 2)).reshape(2, nbatch * size)

    reduce_gain, reduce_bias = row_slice(all_params(0, mid_held), 1)
    dilate_gain, dilate_bias = row_slice(all_params(2, mid_held), 1)
    expand_gain, expand_bias = all_params(4, wide_part)

    def exchange_wide(array):
        blocks = array.reshape(nrows, quarter, nbatch * wide_part)
        return exchange_keyed(
            [lax.dynamic_index_in_dim(blocks, row ^ key, 0, keepdims=False) for key in range(4)]
        )

    def collect_wide(got):
        if spread_by_kernel:
            (out,) = single_call(
                collect_kernel,
                (here, *got),
                [(quarter, wide)],
                [(nrows, quarter, wide // nrows)],
                1,
            )
        else:
            out = jnp.stack(in_order(got, row)).reshape(nrows, quarter, nbatch, wide_part)
            out = jnp.transpose(out, (1, 2, 0, 3))
        return out.reshape(1, local_height, breadth, wide)

    def image_of(array):
        return array.reshape(height, breadth, array.shape[-1])

    valid = depth_valid.astype(jnp.float32).reshape(quarter, 1)
    keep, give = single_call(
        split_product_kernel,
        (here, inputs, reduce_full, jnp.full((1, part), jnp.sum(valid))),
        [(2, pixels + 8, part)] * 2,
        [(pixels, mid)],
        2 * pixels * mid * mid,
    )
    mine_terms, got_terms = scatter_end(keep, give)
    pre_reduce = mine_terms + got_terms
    valid_row = pre_reduce[pixels]
    pre_reduce = pre_reduce[:pixels]
    total_one = sum_batch(jnp.concatenate([sums_of(pre_reduce, pre_reduce), valid_row[None]]))
    scale = valid * (count / total_one[2, 0])
    hat_one, normed_one, inverse_one = norm_forward(
        pre_reduce, total_one, reduce_gain, reduce_bias, count
    )
    pre_dilate, mid_in = joined_conv(
        here, gather_keyed(image_of(jax.nn.silu(normed_one))), dilate_full, 2
    )
    total_two = sum_batch(sums_of(pre_dilate, pre_dilate))
    hat_two, normed_two, inverse_two = norm_forward(
        pre_dilate, total_two, dilate_gain, dilate_bias, count
    )

    beside = mid // class_lanes
    square_mine, square_spans = packed(
        {
            "depth_gate": depth_gate,
            "segment_gate": segment_gate,
            "expand": expand_mine,
            "classifier": jnp.pad(classifier, ((0, 0), (0, class_lanes - classes)))
            .reshape(beside, mid_held // beside, class_lanes)
            .transpose(1, 0, 2)
            .reshape(mid_held // beside, mid),
        }
    )
    square_mine, inverse_two = lax.optimization_barrier((square_mine, inverse_two))
    square_all, _ = ring.gather(square_mine, False)
    square_all, heads_full = lax.optimization_barrier((square_all, heads_full))
    feats, mid_out, pairs = joined_conv(
        here, gather_keyed(image_of(jax.nn.silu(normed_two))), heads_full, 1, True
    )
    depth_gate_w, segment_gate_w, expand_w = [
        square_all[:, square_spans[name]].reshape(mid, mid)
        for name in ("depth_gate", "segment_gate", "expand")
    ]
    classifier_w = (
        square_all[:, square_spans["classifier"]]
        .reshape(nbatch, mid_held // beside, beside, class_lanes)
        .transpose(0, 2, 1, 3)
        .reshape(mid, class_lanes)
    )
    feats_image = image_of(feats)

    pairs_got = jnp.stack(exchange_keyed([pairs[key] for key in range(4)]))
    block_cotangent, _ = lax.optimization_barrier((block_cotangent, inverse_two))
    cotangent = spread_wide(block_cotangent.reshape(quarter, wide))
    pairs_got, cotangent = lax.optimization_barrier((pairs_got, cotangent))
    depth_cotangent = depth_cotangent.reshape(quarter, mid)
    both, one_map = (2 * quarter, mid), (quarter, mid)
    feat_pair, open_pair, d_depth_note = single_call(
        gates_kernel,
        (here, pairs_got, mix, depth_gate_w, segment_gate_w, depth_cotangent, scale),
        [both, both, one_map],
        [both],
        8 * quarter * mid * mid,
    )

    def lines(array):
        return array.reshape(local_height, breadth, mid)

    depth_pair_grad, d_depth_image = note_grad(here, feats, 0, gather_keyed(lines(d_depth_note)), run)
    depth_pair_sums = lax.psum_scatter(
        regroup(depth_pair_grad, grain).reshape(-1, mid), "batch", scatter_dimension=0, tiled=True
    )
    flat_mid_out = mid_out.reshape(pixels, mid)
    pre_expand = product(flat_mid_out, expand_w, 1, 0)
    hat_three, normed_three, inverse_three = norm_forward(
        pre_expand, sum_batch(sums_of(pre_expand, pre_expand)), expand_gain, expand_bias, count
    )
    summed = normed_three + inputs
    block_blocks = exchange_wide(jax.nn.silu(summed))
    d_summed = cotangent * silu_grad(summed)
    d_pre_expand, expand_sums = norm_backward(
        d_summed, hat_three, inverse_three, expand_gain, count, False
    )
    segment_pair_w, block_blocks, _ = lax.optimization_barrier(
        (segment_pair_w, block_blocks, (expand_sums, depth_pair_grad))
    )
    block_out = collect_wide(block_blocks)

    segment_mine, segment_got = scatter_end(*note_forward(here, feats_image, 1, segment_pair_w))

    def segment_body(*refs):
        segment_kernel(classes, *refs)

    segment_stream, d_segment_note, direct_segment, segment_gate_grad, classifier_grad = single_call(
        segment_body,
        (
            here,
            segment_mine,
            segment_got,
            feat_pair[quarter:],
            open_pair[quarter:],
            labels.reshape(quarter, 1),
            classifier_w,
            segment_gate_w,
            mix,
        ),
        [one_map, one_map, (4, quarter, part), (mid, mid), (mid, class_lanes)],
        [one_map],
        8 * quarter * mid * mid,
    )

    segment_pair_grad, d_segment_image = note_grad(
        here, feats, 1, gather_keyed(lines(d_segment_note)), run
    )
    hops = Hops(ring, regroup(segment_pair_grad, grain).reshape(nbatch, held // 2, mid), True)
    segment_back = note_back(d_segment_image, segment_pair_w)
    depth_pair_w, segment_back = hops.step((depth_pair_w, segment_back))
    depth_mine, depth_got = scatter_end(*note_forward(here, feats_image, 0, depth_pair_w))
    depth_back = note_back(hops.step(d_depth_image), depth_pair_w)
    depth_stream, direct_both, depth_gate_grad = single_call(
        depth_kernel,
        (
            here,
            depth_mine,
            depth_got,
            feat_pair[:quarter],
            open_pair[:quarter],
            depth_cotangent,
            scale,
            depth_gate_w,
            mix,
            direct_segment,
        ),
        [one_map, (4, 2 * quarter, part), (mid, mid)],
        [one_map],
        8 * quarter * mid * mid,
    )
    direct_got = jnp.stack(exchange_keyed([direct_both[key] for key in range(4)]))
    heads_grad, d_feats = heads_grad_of(
        here,
        hops.step(flat_mid_out),
        image_of(depth_back),
        image_of(segment_back),
        direct_got.reshape(4, 2 * local_height, breadth, part),
    )
    heads_sums = lax.psum_scatter(heads_grad, "batch", scatter_dimension=0, tiled=True)

    expand_grad = product(flat_mid_out, d_pre_expand, 0, 0).reshape(nbatch, mid_held, mid)

    gate_terms = jnp.stack(
        [
            depth_gate_grad,
            segment_gate_grad,
            jnp.pad(classifier_grad, ((0, 0), (0, mid - class_lanes))),
        ]
    )
    gate_rows = mid_held // nrows
    gate_terms = jnp.transpose(gate_terms.reshape(3, nbatch, nrows, gate_rows, mid), (2, 1, 0, 3, 4))
    gate_sums = scatter_rows(gate_terms, row).reshape(nbatch, 3 * gate_rows, mid)

    d_feats = hops.step(d_feats)
    segment_pair_sums = hops.result()
    mine_terms, got_terms = scatter_end(
        *conv_back(here, d_feats, heads_full, 1, product(d_pre_expand, expand_w, 1, 1))
    )
    d_pre_dilate, dilate_sums = norm_backward(
        (mine_terms + got_terms) * silu_grad(normed_two), hat_two, inverse_two, dilate_gain, count, False
    )
    d_dilate_image = image_of(d_pre_dilate)
    mine_terms, got_terms = scatter_end(*conv_back(here, d_dilate_image, dilate_full, 2))
    d_pre_reduce, reduce_sums = norm_backward(
        (mine_terms + got_terms) * silu_grad(normed_one), hat_one, inverse_one, reduce_gain, count, False
    )
    reduce_grad, features_back = single_call(
        reduce_back_kernel,
        (here, *gather_keyed(d_pre_reduce), inputs, reduce_full, d_summed),
        [(mid, mid), (pixels, mid)],
        [(pixels, mid)],
        4 * pixels * mid * mid,
    )
    dilate_grad = conv_grad(mid_in.reshape(pixels, mid), d_dilate_image, 2).reshape(
        nbatch, held, part
    )
    narrow = held // nrows
    square_grad = jnp.concatenate(
        [
            jnp.concatenate(
                [dilate_grad[:, i * narrow : (i + 1) * narrow] for i in range(nrows)], axis=2
            ),
            expand_grad,
            gate_sums,
        ],
        axis=1,
    )
    square_grad, reduce_sums, depth_pair_sums, segment_pair_sums = lax.optimization_barrier(
        (square_grad, reduce_sums, depth_pair_sums, segment_pair_sums)
    )
    square_hops = Hops(ring, square_grad, False)
    square_hops.step()
    square_hops.step()
    heads_sums = square_hops.step(heads_sums)
    square_hops.step()
    square_sums = square_hops.result()
    reduce_out = ring.scatter(reduce_grad.reshape(nbatch, wide_part, mid), True)
    features_grad = collect_wide(exchange_wide(features_back))

    pair_sums = jnp.concatenate([depth_pair_sums, segment_pair_sums], axis=0) * factor
    pairs_out = jnp.stack(gather_rows(pair_sums, row)).reshape(nrows, 2, groups, 2, grain, mid)
    depth_pair_out, segment_pair_out = pairs_out[:, 0], pairs_out[:, 1]

    def message_out(pair_got, index):
        return jnp.transpose(pair_got[:, :, index], (1, 0, 2, 3)).reshape(held, mid)

    segment_out, normal_out, depth_out, contour_out = single_call(
        heads_out_kernel,
        (here, *gather_keyed(heads_sums * factor), mix),
        [(held, mid)] * 4,
        [(held, mid)],
        8 * held * mid * mid,
    )

    expand_mine_sums = lax.dynamic_slice_in_dim(expand_sums, batch * wide_part, wide_part, 1)
    norm_sums = jnp.concatenate(
        [
            jnp.pad(sums, ((0, 0), (0, mid - sums.shape[1])))
            for sums in (reduce_sums, dilate_sums, expand_mine_sums)
        ],
        axis=0,
    )
    small = jnp.concatenate([square_sums, jnp.pad(norm_sums, ((0, 2), (0, 0)))], axis=0) * factor
    small_got = gather_rows(small, row)
    squares_got = jnp.stack([block[narrow : narrow + mid_held + 3 * gate_rows] for block in small_got])
    dilate_out = jnp.concatenate(
        [
            jnp.concatenate(
                [block[:narrow, i * part : (i + 1) * part] for i in range(nrows)], axis=0
            )
            for block in small_got
        ],
        axis=1,
    )
    expand_out = jnp.transpose(
        squares_got[:, :mid_held].reshape(nrows, mid_held, nbatch, wide_part), (1, 2, 0, 3)
    ).reshape(mid_held, wide)

    def gate_out(index):
        start = mid_held + index * gate_rows
        return squares_got[:, start : start + gate_rows].reshape(mid_held, mid)

    norms_got = [block[-8:] for block in small_got]

    def norm_out(start):
        full = jnp.concatenate([block[start : start + 2, :part] for block in norms_got], axis=1)
        return lax.dynamic_slice_in_dim(full, batch * mid_held, mid_held, 1)

    expand_norm_out = jnp.concatenate([block[4:6, :wide_part] for block in norms_got], axis=1)
    reduce_got = jnp.concatenate(gather_rows(reduce_out * factor, row), axis=0)

    return (
        block_out,
        depth_stream.reshape(1, local_height, breadth, mid),
        segment_stream.reshape(1, local_height, breadth, mid),
        features_grad,
        reduce_got,
        norm_out(0),
        dilate_out,
        norm_out(2),
        expand_out,
        expand_norm_out,
        depth_out,
        segment_out,
        normal_out,
        contour_out,
        message_out(depth_pair_out, 0),
        message_out(segment_pair_out, 0),
        message_out(depth_pair_out, 1),
        message_out(segment_pair_out, 1),
        gate_out(0),
        gate_out(1),
        gate_out(2)[:, :classes],
    )


def solution(mesh):
    pixels = P("batch", "rows", None, None)
    plane = P("batch", "rows", None)
    weight = P("batch", None)
    norm = P(None, "batch")
    in_specs = (
        (pixels, weight, norm, weight, norm, weight, norm) + (weight,) * 11 + (plane, plane, pixels, pixels)
    )
    out_specs = (pixels,) * 4 + (weight, norm) * 3 + (weight,) * 11
    return jax.shard_map(shards, mesh=mesh, in_specs=in_specs, out_specs=out_specs, check_vma=False)
```

```python
import math

import jax
import jax.numpy as jnp
from jax import lax
from jax.experimental import pallas as pl
from jax.experimental.pallas import tpu as pltpu
from jax.sharding import PartitionSpec as P

EPSILON = 1e-05
EXACT = lax.Precision.HIGHEST
FINE = lax.Precision.HIGH
LONGEST_RING = 8
LANES = 128


def product(left, right, left_dim, right_dim, precision=FINE):
    return lax.dot_general(
        left,
        right,
        (((left_dim,), (right_dim,)), ((), ())),
        precision=precision,
        preferred_element_type=jnp.float32,
    )


def halves(values):
    high = values.astype(jnp.bfloat16)
    return high, (values - high.astype(jnp.float32)).astype(jnp.bfloat16)


def three_pass(left, right, left_dim, right_dim):
    dims = (((left_dim,), (right_dim,)), ((), ()))

    def one(a, b):
        return lax.dot_general(a, b, dims, preferred_element_type=jnp.float32)

    return one(left[0], right[0]) + (one(left[0], right[1]) + one(left[1], right[0]))


def frame(image_ref, framed, dilation):
    height, breadth, depth = image_ref.shape
    edge = jnp.zeros((3, dilation, breadth, depth), jnp.float32)
    framed[:, :dilation] = edge
    framed[:, dilation + height :] = edge
    image = image_ref[...]
    side = jnp.zeros((height, dilation, depth), jnp.float32)
    inner = slice(dilation, dilation + height)
    framed[1, inner] = image
    framed[0, inner, dilation:, :] = image[:, : breadth - dilation]
    framed[0, inner, :dilation, :] = side
    framed[2, inner, : breadth - dilation, :] = image[:, dilation:]
    framed[2, inner, breadth - dilation :, :] = side


def shifted(framed, tap, height, dilation):
    block = framed[tap % 3, pl.ds((tap // 3) * dilation, height)]
    return block.reshape(height * block.shape[1], block.shape[2])


def exact_pick(values, choice, choice_dim):
    high = values.astype(jnp.bfloat16)
    rest = values - high.astype(jnp.float32)
    middle = rest.astype(jnp.bfloat16)
    low = (rest - middle.astype(jnp.float32)).astype(jnp.bfloat16)
    dims = (((1,), (choice_dim,)), ((), ()))

    def one(part):
        return lax.dot_general(part, choice, dims, preferred_element_type=jnp.float32)

    return one(high) + (one(middle) + one(low))


def at_lanes(index, size):
    return pl.ds(pl.multiple_of(index * size, size), size)


def keep_and_give(row, load, keep_ref, give_ref):
    core, side = row & 1, row >> 1
    for k in range(2):
        base = (side ^ k) * 2
        keep_ref[k] = load(base + core)
        give_ref[k] = load(base + 1 - core)


def joined_conv_kernel(dilation, row_ref, one, two, three, four, weight_ref, out_ref, image_ref, framed):
    tap = pl.program_id(0)

    @pl.when(tap == 0)
    def _():
        part = one.shape[2]
        for key, block in enumerate((one, two, three, four)):
            image_ref[:, :, at_lanes(row_ref[0] ^ key, part)] = block[...]
        frame(image_ref, framed, dilation)
        out_ref[...] = jnp.zeros_like(out_ref)

    moved = halves(shifted(framed, tap, image_ref.shape[0], dilation))
    out_ref[...] += three_pass(moved, halves(weight_ref[...]), 1, 0)


def heads_kernel(
    row_ref, one, two, three, four, weight_ref, out_ref, image_ref, pairs_ref, framed
):
    joined_conv_kernel(1, row_ref, one, two, three, four, weight_ref, out_ref, image_ref, framed)

    @pl.when(pl.program_id(0) == 8)
    def _():
        _, double, part = pairs_ref.shape
        quarter = double // 2
        for key in range(4):
            rows = pl.ds((row_ref[0] ^ key) * quarter, quarter)
            pairs_ref[key, :quarter] = out_ref[rows, 2 * part : 3 * part]
            pairs_ref[key, quarter:] = out_ref[rows, :part]


def split_product_kernel(row_ref, left_ref, right_ref, extra_ref, keep_ref, give_ref, total):
    total[...] = three_pass(halves(left_ref[...]), halves(right_ref[...]), 1, 0)
    pixels, part = left_ref.shape[0], keep_ref.shape[2]
    keep_and_give(
        row_ref[0],
        lambda j: total[:, at_lanes(j, part)],
        keep_ref.at[:, :pixels],
        give_ref.at[:, :pixels],
    )
    for ref in (keep_ref, give_ref):
        ref[:, pixels:] = jnp.broadcast_to(extra_ref[...], (2, 8, part))


def conv_back_kernel(dilation, row_ref, image_ref, weight_ref, *rest):
    extra_ref = rest[0] if len(rest) == 5 else None
    keep_ref, give_ref, framed, total = rest[-4:]
    tap = pl.program_id(0)

    @pl.when(tap == 0)
    def _():
        frame(image_ref, framed, dilation)
        total[...] = jnp.zeros_like(total) if extra_ref is None else extra_ref[...]

    moved = halves(shifted(framed, 8 - tap, image_ref.shape[0], dilation))
    total[...] += three_pass(moved, halves(weight_ref[...]), 1, 1)

    @pl.when(tap == 8)
    def _():
        part = keep_ref.shape[2]
        keep_and_give(row_ref[0], lambda j: total[:, at_lanes(j, part)], keep_ref, give_ref)


def conv_grad_kernel(dilation, input_ref, grad_ref, out_ref, framed, high, low):
    tap = pl.program_id(0)

    @pl.when(tap == 0)
    def _():
        frame(grad_ref, framed, dilation)
        high[...], low[...] = halves(jnp.transpose(input_ref[...]))

    moved = halves(shifted(framed, 8 - tap, grad_ref.shape[0], dilation))
    out_ref[...] = three_pass((high[...], low[...]), moved, 1, 0)


def heads_grad_kernel(
    row_ref, input_ref, first_ref, second_ref, direct_ref, out_ref, image_ref, framed, high, low
):
    tap = pl.program_id(0)

    @pl.when(tap == 0)
    def _():
        lanes = first_ref.shape[2]
        _, double, breadth, part = direct_ref.shape
        lines = double // 2
        image_ref[:, :, :lanes] = first_ref[...]
        image_ref[:, :, lanes:] = second_ref[...]
        for key in range(4):
            rows = pl.ds((row_ref[0] ^ key) * lines, lines)
            image_ref[rows, :, :part] += direct_ref[key, :lines]
            image_ref[rows, :, lanes : lanes + part] += direct_ref[key, lines:]

    conv_grad_kernel(1, input_ref, image_ref, out_ref, framed, high, low)


def source_rows(weight):
    return jnp.concatenate(
        [weight[:, k].reshape(-1, weight.shape[-1]) for k in range(weight.shape[1])], axis=0
    )


def note_kernel(row_ref, image_ref, weight_ref, keep_ref, give_ref, framed, total):
    tap = pl.program_id(0)

    @pl.when(tap == 0)
    def _():
        frame(image_ref, framed, 1)
        total[...] = jnp.zeros_like(total)

    moved = shifted(framed, tap, image_ref.shape[0], 1)
    total[...] += three_pass(halves(moved), halves(source_rows(weight_ref[...])), 1, 0)

    @pl.when(tap == 8)
    def _():
        quarter = keep_ref.shape[1]
        keep_and_give(
            row_ref[0], lambda j: total[pl.ds(j * quarter, quarter), :], keep_ref, give_ref
        )


def note_back_kernel(note_ref, weight_ref, out_ref, framed):
    tap = pl.program_id(0)

    @pl.when(tap == 0)
    def _():
        frame(note_ref, framed, 1)
        out_ref[...] = jnp.zeros_like(out_ref)

    moved = halves(shifted(framed, 8 - tap, note_ref.shape[0], 1))
    out_ref[...] += three_pass(moved, halves(source_rows(weight_ref[...])), 1, 1)


def note_grad_kernel(
    row_ref, input_ref, one, two, three, four, out_ref, image_ref, framed, high, low
):
    tap = pl.program_id(0)

    @pl.when(tap == 0)
    def _():
        lines = one.shape[0]
        for key, block in enumerate((one, two, three, four)):
            image_ref[pl.ds((row_ref[0] ^ key) * lines, lines)] = block[...]
        frame(image_ref, framed, 1)
        high[...], low[...] = halves(jnp.transpose(input_ref[...]))

    moved = halves(shifted(framed, 8 - tap, image_ref.shape[0], 1))
    grad = three_pass((high[...], low[...]), moved, 1, 0)
    runs, _, grain, mid = out_ref.shape
    part = grad.shape[0] // 2
    for k in range(2):
        out_ref[:, k] = grad[k * part : (k + 1) * part].reshape(runs, grain, mid)


def gates_kernel(
    row_ref, pairs_ref, mix_ref, depth_gate_ref, segment_gate_ref, cotangent_ref, scale_ref,
    feat_ref, open_ref, d_note_ref, joined,
):
    _, double, part = pairs_ref.shape
    quarter = double // 2
    for key in range(4):
        joined[:, at_lanes(row_ref[0] ^ key, part)] = pairs_ref[key]
    feat = exact_pick(joined[...], mix_ref[...], 0)
    feat_ref[...] = feat
    for index, gate_ref in enumerate((depth_gate_ref, segment_gate_ref)):
        rows = slice(index * quarter, (index + 1) * quarter)
        gate = three_pass(halves(feat[rows]), halves(gate_ref[...]), 1, 0)
        open_ref[rows] = jax.nn.sigmoid(gate)
    d_note_ref[...] = cotangent_ref[...] * scale_ref[...] * open_ref[:quarter]


def gate_back(row_ref, feat, opened, note, d_stream, d_note, gate_ref, mix_ref, gate_grad_ref, joined):
    d_pre = halves(d_note * note * (1.0 - opened))
    gate_grad_ref[...] = three_pass(halves(jnp.transpose(feat)), d_pre, 1, 0)
    direct = d_stream + three_pass(d_pre, halves(gate_ref[...]), 1, 1)
    joined[...] = exact_pick(direct, mix_ref[...], 1)


def segment_kernel(
    classes, row_ref, mine_ref, got_ref, feat_ref, open_ref, labels_ref, classifier_ref, gate_ref, mix_ref,
    stream_ref, d_note_ref, direct_ref, gate_grad_ref, classifier_grad_ref, joined,
):
    note = mine_ref[...] + got_ref[...]
    feat, opened = feat_ref[...], open_ref[...]
    stream = feat + opened * note
    stream_ref[...] = stream
    weight = halves(classifier_ref[...])
    logits = three_pass(halves(stream), weight, 1, 0)
    lane = lax.broadcasted_iota(jnp.int32, logits.shape, 1)
    real = lane < classes
    top = jnp.max(jnp.where(real, logits, -3e38), axis=1, keepdims=True)
    powers = jnp.where(real, jnp.exp(jnp.where(real, logits - top, 0.0)), 0.0)
    onehot = jnp.where(lane == labels_ref[...], 1.0, 0.0)
    d_logits = powers / jnp.sum(powers, axis=1, keepdims=True) - onehot
    d_stream = three_pass(halves(d_logits), weight, 1, 1)
    d_note = d_stream * opened
    d_note_ref[...] = d_note
    classifier_grad_ref[...] = three_pass(halves(jnp.transpose(stream)), halves(d_logits), 1, 0)
    gate_back(row_ref, feat, opened, note, d_stream, d_note, gate_ref, mix_ref, gate_grad_ref, joined)
    part = direct_ref.shape[2]
    for key in range(4):
        direct_ref[key] = joined[:, at_lanes(row_ref[0] ^ key, part)]


def depth_kernel(
    row_ref, mine_ref, got_ref, feat_ref, open_ref, cotangent_ref, scale_ref, gate_ref, mix_ref, other_ref,
    stream_ref, direct_ref, gate_grad_ref, joined,
):
    note = mine_ref[...] + got_ref[...]
    feat, opened = feat_ref[...], open_ref[...]
    stream_ref[...] = feat + opened * note
    d_stream = cotangent_ref[...] * scale_ref[...]
    gate_back(
        row_ref, feat, opened, note, d_stream, d_stream * opened, gate_ref, mix_ref, gate_grad_ref, joined
    )
    _, double, part = direct_ref.shape
    quarter = double // 2
    for key in range(4):
        direct_ref[key, :quarter] = other_ref[key]
        direct_ref[key, quarter:] = joined[:, at_lanes(row_ref[0] ^ key, part)]


def reduce_back_kernel(
    row_ref, one, two, three, four, input_ref, weight_ref, d_summed_ref, grad_ref, out_ref, joined
):
    part = one.shape[1]
    for key, block in enumerate((one, two, three, four)):
        joined[:, at_lanes(row_ref[0] ^ key, part)] = block[...]
    d_pre = halves(joined[...])
    grad_ref[...] = three_pass(halves(jnp.transpose(input_ref[...])), d_pre, 1, 0)
    out_ref[...] = d_summed_ref[...] + three_pass(d_pre, halves(weight_ref[...]), 1, 1)


def heads_out_kernel(row_ref, one, two, three, four, mix_ref, *rest):
    outs, joined = rest[:-1], rest[-1]
    part = joined.shape[1] // 4
    for index, out_ref in enumerate(outs):
        lanes = slice(index * part, (index + 1) * part)
        for key, block in enumerate((one, two, three, four)):
            joined[:, at_lanes(row_ref[0] ^ key, part)] = block[:, lanes]
        out_ref[...] = exact_pick(joined[...], mix_ref[...], 0)


def spread_kernel(row_ref, array_ref, out_ref):
    low = lax.broadcasted_iota(jnp.int32, (array_ref.shape[0], 128), 1) < 64
    for device in range(4):
        key = row_ref[0] ^ device
        for k in range(out_ref.shape[2] // 128):
            start = 512 * k + 128 * (device // 2)
            even = array_ref[:, start : start + 128]
            odd = array_ref[:, start + 256 : start + 384]
            if device % 2:
                block = jnp.where(low, pltpu.roll(even, 64, 1), odd)
            else:
                block = jnp.where(low, even, pltpu.roll(odd, 64, 1))
            out_ref[key, :, 128 * k : 128 * (k + 1)] = block


def collect_kernel(row_ref, one, two, three, four, out_ref, ordered):
    for key, block in enumerate((one, two, three, four)):
        ordered[row_ref[0] ^ key] = block[...]
    low = lax.broadcasted_iota(jnp.int32, (one.shape[0], 128), 1) < 64
    for k in range(one.shape[1] // 128):
        for pair in range(2):
            first = ordered[2 * pair, :, 128 * k : 128 * (k + 1)]
            second = ordered[2 * pair + 1, :, 128 * k : 128 * (k + 1)]
            start = 512 * k + 128 * pair
            out_ref[:, start : start + 128] = jnp.where(low, first, pltpu.roll(second, 64, 1))
            out_ref[:, start + 256 : start + 384] = jnp.where(low, pltpu.roll(first, 64, 1), second)


def regroup(array, run):
    runs, sources, grain, mid = array.shape
    if grain == run:
        return array
    if run > grain:
        lists = array.reshape(-1, run // grain, sources, grain, mid)
        return jnp.transpose(lists, (0, 2, 1, 3, 4)).reshape(-1, sources, run, mid)
    parts = array.reshape(runs, sources, grain // run, run, mid)
    return jnp.transpose(parts, (0, 2, 1, 3, 4)).reshape(-1, sources, run, mid)


VMEM_LIMIT = 56 * 2**20
SCALAR = pl.BlockSpec(memory_space=pltpu.SMEM)


def kernel_call(body, grid, in_specs, out_specs, out_shape, scratch, flops):
    return pl.pallas_call(
        body,
        grid=grid,
        in_specs=in_specs,
        out_specs=out_specs,
        out_shape=out_shape,
        scratch_shapes=scratch,
        compiler_params=pltpu.CompilerParams(
            dimension_semantics=("arbitrary",) * len(grid), vmem_limit_bytes=VMEM_LIMIT
        ),
        cost_estimate=pl.CostEstimate(flops=3 * flops, bytes_accessed=12 * 2**20, transcendentals=0),
    )


def single_call(body, args, outs, scratch, flops):
    return kernel_call(
        body,
        (1,),
        [SCALAR] + [whole_spec(arg.shape) for arg in args[1:]],
        [whole_spec(out) for out in outs],
        [jax.ShapeDtypeStruct(out, jnp.float32) for out in outs],
        [pltpu.VMEM(shape, jnp.float32) for shape in scratch],
        flops,
    )(*args)


def framed_scratch(image, dilation):
    height, breadth, depth = image
    return pltpu.VMEM((3, height + 2 * dilation, breadth, depth), jnp.float32)


def whole_spec(shape):
    return pl.BlockSpec(shape, lambda *_: (0,) * len(shape))


def struct(shape):
    return jax.ShapeDtypeStruct(shape, jnp.float32)


def tap_rows(rows, cols):
    return pl.BlockSpec((rows, cols), lambda tap: (tap, 0))


def tap_runs(weight_shape, pair=0):
    runs, _, grain, mid = weight_shape
    return pl.BlockSpec((runs // 9, 2, grain, mid), lambda tap: (tap, pair, 0, 0))


def joined_conv(row, blocks, weight, dilation, with_pairs=False):
    height, breadth, part = blocks[0].shape
    image = (height, breadth, 4 * part)
    rows, cols = weight.shape[0] // 9, weight.shape[1]
    shapes = [(height * breadth, cols), image]
    if with_pairs:
        body = heads_kernel
        shapes.append((4, height * breadth // 2, part))
    else:

        def body(*refs):
            joined_conv_kernel(dilation, *refs)

    return kernel_call(
        body,
        (9,),
        [SCALAR] + [whole_spec(blocks[0].shape)] * 4 + [tap_rows(rows, cols)],
        [whole_spec(shape) for shape in shapes],
        [struct(shape) for shape in shapes],
        [framed_scratch(image, dilation)],
        2 * 9 * height * breadth * rows * cols,
    )(row, *blocks, weight)


def conv_back(row, image, weight, dilation, extra=None):
    height, breadth, _ = image.shape
    rows, cols = weight.shape[0] // 9, weight.shape[1]
    pixels = height * breadth
    shape = (2, pixels, rows // 4)

    def body(*refs):
        conv_back_kernel(dilation, *refs)

    extras = [] if extra is None else [extra]
    return kernel_call(
        body,
        (9,),
        [SCALAR, whole_spec(image.shape), tap_rows(rows, cols)]
        + [whole_spec(array.shape) for array in extras],
        [whole_spec(shape)] * 2,
        [struct(shape)] * 2,
        [framed_scratch(image.shape, dilation), pltpu.VMEM((pixels, rows), jnp.float32)],
        2 * 9 * pixels * rows * cols,
    )(row, image, weight, *extras)


def conv_grad(flat_input, image_grad, dilation):
    pixels, depth = flat_input.shape
    cols = image_grad.shape[2]

    def body(*refs):
        conv_grad_kernel(dilation, *refs)

    return kernel_call(
        body,
        (9,),
        [whole_spec(flat_input.shape), whole_spec(image_grad.shape)],
        tap_rows(depth, cols),
        struct((9 * depth, cols)),
        [framed_scratch(image_grad.shape, dilation)]
        + [pltpu.VMEM((depth, pixels), jnp.bfloat16)] * 2,
        2 * 9 * pixels * depth * cols,
    )(flat_input, image_grad)


def heads_grad_of(row, flat_input, first, second, direct):
    pixels, depth = flat_input.shape
    height, breadth, lanes = first.shape
    image = (height, breadth, 2 * lanes)
    return kernel_call(
        heads_grad_kernel,
        (9,),
        [SCALAR] + [whole_spec(array.shape) for array in (flat_input, first, second, direct)],
        [tap_rows(depth, 2 * lanes), whole_spec(image)],
        [struct((9 * depth, 2 * lanes)), struct(image)],
        [framed_scratch(image, 1)] + [pltpu.VMEM((depth, pixels), jnp.bfloat16)] * 2,
        2 * 9 * pixels * depth * 2 * lanes,
    )(row, flat_input, first, second, direct)


def note_forward(row, image, pair, weight):
    height, breadth, depth = image.shape
    depth = depth // 2
    mid = weight.shape[3]
    pixels = height * breadth
    shape = (2, pixels // 4, mid)
    return kernel_call(
        note_kernel,
        (9,),
        [
            SCALAR,
            pl.BlockSpec((height, breadth, depth), lambda tap: (0, 0, pair)),
            tap_runs(weight.shape, pair),
        ],
        [whole_spec(shape)] * 2,
        [struct(shape)] * 2,
        [framed_scratch((height, breadth, depth), 1), pltpu.VMEM((pixels, mid), jnp.float32)],
        2 * 9 * pixels * depth * mid,
    )(row, image, weight)


def note_back(note, pair, weight):
    height, breadth, mid = note.shape
    shape = (height * breadth, weight.shape[0] // 9 * 2 * weight.shape[2])
    return kernel_call(
        note_back_kernel,
        (9,),
        [whole_spec(note.shape), tap_runs(weight.shape, pair)],
        whole_spec(shape),
        struct(shape),
        [framed_scratch(note.shape, 1)],
        2 * 9 * shape[0] * shape[1] * mid,
    )(note, weight)


def note_grad(row, flat_input, pair, blocks, grain):
    pixels, depth = flat_input.shape
    depth = depth // 2
    lines, breadth, mid = blocks[0].shape
    image = (4 * lines, breadth, mid)
    runs = depth // 2 // grain
    grad = (9 * runs, 2, grain, mid)
    return kernel_call(
        note_grad_kernel,
        (9,),
        [SCALAR, pl.BlockSpec((pixels, depth), lambda tap: (0, pair))]
        + [whole_spec(blocks[0].shape)] * 4,
        [tap_runs(grad), whole_spec(image)],
        [struct(grad), struct(image)],
        [framed_scratch(image, 1)] + [pltpu.VMEM((depth, pixels), jnp.bfloat16)] * 2,
        2 * 9 * pixels * depth * mid,
    )(row, flat_input, *blocks)


def silu_grad(values):
    gate_val = jax.nn.sigmoid(values)
    return gate_val * (1.0 + values * (1.0 - gate_val))


def swap_rows(block, mask):
    size = lax.axis_size("rows")
    return lax.ppermute(block, "rows", [(i, i ^ mask) for i in range(size)])


def in_order(blocks, row):
    count = len(blocks)
    if count == 1:
        return blocks
    half = count // 2
    near = in_order(blocks[:half], row)
    far = in_order(blocks[half:], row)
    upper = (row & half) != 0
    first = [jnp.where(upper, f, n) for n, f in zip(near, far)]
    second = [jnp.where(upper, n, f) for n, f in zip(near, far)]
    return first + second


def gather_keyed(block):
    far = swap_rows(block, 2)
    return [block, swap_rows(block, 1), far, swap_rows(far, 1)]


def gather_rows(block, row):
    return in_order(gather_keyed(block), row)


def scatter_end(keep, give):
    got = swap_rows(give, 1)
    other = keep[1] + got[1]
    return keep[0] + got[0], swap_rows(other, 2)


def scatter_rows(blocks, row):
    core, side = row & 1, row >> 1
    pairs = blocks.reshape((2, 2) + blocks.shape[1:])
    keep = lax.dynamic_index_in_dim(pairs, core, 1, keepdims=False)
    got = keep + swap_rows(lax.dynamic_index_in_dim(pairs, 1 - core, 1, keepdims=False), 1)
    mine = lax.dynamic_index_in_dim(got, side, 0, keepdims=False)
    return mine + swap_rows(lax.dynamic_index_in_dim(got, 1 - side, 0, keepdims=False), 2)


def exchange_keyed(blocks):
    return [blocks[0]] + [swap_rows(blocks[mask], mask) for mask in range(1, 4)]


def sum_batch(values, direct=False):
    size = lax.axis_size("batch")
    if size & (size - 1):
        return lax.psum(values, "batch")

    def swap(block, mask):
        return lax.ppermute(block, "batch", [(i, i ^ mask) for i in range(size)])

    if direct and size <= LONGEST_RING:
        return values + sum(swap(values, mask) for mask in range(1, size))
    mask = 1
    while mask < size:
        values = values + swap(values, mask)
        mask *= 2
    return values


class Ring:
    def __init__(self, batch):
        size = lax.axis_size("batch")
        self.batch, self.size = batch, size
        self.order = list(range(0, size, 2)) + [i for i in reversed(range(size)) if i % 2]
        self.place = {b: p for p, b in enumerate(self.order)}
        self.up = [(self.order[p], self.order[(p + 1) % size]) for p in range(size)]
        self.down = [(b, a) for a, b in self.up]
        table = [[self.order[(self.place[b] + k) % size] for k in range(size)] for b in range(size)]
        self.row = jnp.array(table, jnp.int32)[batch]

    def at(self, offset):
        return self.row[offset % self.size]

    def steps(self, longer_up):
        more = self.size // 2
        less = self.size - 1 - more
        return (more, less) if longer_up else (less, more)

    def gather(self, block, longer_up, beside=None, beside_step=0):
        if self.size > LONGEST_RING:
            return lax.all_gather(block, "batch", axis=0, tiled=False), beside
        whole = jnp.zeros((self.size,) + block.shape, block.dtype)
        whole = lax.dynamic_update_index_in_dim(whole, block, self.batch, 0)
        ups, downs = self.steps(longer_up)
        rising = falling = block
        for k in range(1, max(ups, downs) + 1):
            if k == beside_step and beside is not None:
                rising, falling, beside = lax.optimization_barrier((rising, falling, beside))
            if k <= ups:
                rising = lax.ppermute(rising, "batch", self.up)
                whole = lax.dynamic_update_index_in_dim(whole, rising, self.at(-k), 0)
            if k <= downs:
                falling = lax.ppermute(falling, "batch", self.down)
                whole = lax.dynamic_update_index_in_dim(whole, falling, self.at(k), 0)
        return whole, beside

    def scatter(self, blocks, longer_up):
        hops = Hops(self, blocks, longer_up)
        while not hops.done:
            hops.step()
        return hops.result()


class Hops:
    def __init__(self, ring, blocks, longer_up):
        self.ring, self.blocks, self.hop = ring, blocks, 0
        if ring.size > LONGEST_RING:
            self.sums = lax.psum_scatter(blocks, "batch", scatter_dimension=0, tiled=False)
            self.done = True
            return
        self.sums, self.done = None, False
        self.ups, self.downs = ring.steps(longer_up)
        self.rising, self.falling = self.own(self.ups), self.own(-self.downs)

    def own(self, offset):
        return lax.dynamic_index_in_dim(self.blocks, self.ring.at(offset), 0, keepdims=False)

    def step(self, later=None):
        if self.done:
            return later
        k = self.hop
        if k < self.ups:
            self.rising = lax.ppermute(self.rising, "batch", self.ring.up)
        if k < self.downs:
            self.falling = lax.ppermute(self.falling, "batch", self.ring.down)
        if later is not None:
            self.rising, self.falling, later = lax.optimization_barrier(
                (self.rising, self.falling, later)
            )
        if k < self.ups - 1:
            self.rising = self.rising + self.own(self.ups - 1 - k)
        if k < self.downs - 1:
            self.falling = self.falling + self.own(-(self.downs - 1 - k))
        self.hop += 1
        self.done = self.hop == max(self.ups, self.downs)
        return later

    def await_beside(self, array):
        if not self.done:
            self.rising, self.falling, array = lax.optimization_barrier(
                (self.rising, self.falling, array)
            )
        return array

    def result(self):
        return self.sums if self.sums is not None else self.own(0) + self.rising + self.falling


def sums_of(values, others):
    return jnp.stack([jnp.sum(values, axis=0), jnp.sum(values * others, axis=0)])


def norm_forward(values, total, gain, bias, count):
    center = total[0] / count
    inverse = lax.rsqrt(total[1] / count - center * center + EPSILON)
    hat = (values - center) * inverse
    return hat, hat * gain + bias, inverse


def norm_backward(d_out, hat, inverse, gain, count, direct):
    sums = sum_batch(jnp.stack([jnp.sum(d_out * hat, axis=0), jnp.sum(d_out, axis=0)]), direct)
    d_values = inverse * gain * (d_out - sums[1] / count - hat * (sums[0] / count))
    return d_values, sums


def shards(
    features,
    reduce_weight,
    reduce_norm,
    dilate_weight,
    dilate_norm,
    expand_weight,
    expand_norm,
    depth_head,
    segment_head,
    normal_head,
    contour_head,
    depth_message,
    segment_message,
    normal_message,
    contour_message,
    depth_gate,
    segment_gate,
    classifier,
    depth_valid,
    labels,
    block_cotangent,
    depth_cotangent,
):
    row, batch = lax.axis_index("rows"), lax.axis_index("batch")
    nrows, nbatch = lax.axis_size("rows"), lax.axis_size("batch")
    ring = Ring(batch)
    _, local_height, breadth, wide = features.shape
    mid = reduce_weight.shape[1]
    part = mid // nrows
    quarter = local_height * breadth
    height = local_height * nrows
    pixels = quarter * nrows
    count = float(pixels * nbatch)
    factor = count ** (-0.5)
    classes = classifier.shape[1]
    held = dilate_weight.shape[0]
    grain = math.gcd(held, mid) // nrows
    groups = held // (nrows * grain)
    wide_held = wide // nbatch
    wide_part = wide_held // nrows
    mid_held = mid // nbatch

    def row_slice(array, dim):
        size = array.shape[dim] // nrows
        return lax.dynamic_slice_in_dim(array, row * size, size, dim)

    channel = jnp.arange(mid)
    slot = jnp.arange(part)
    mine = (slot // grain) * (nrows * grain) + row * grain + slot % grain
    pick = (channel[:, None] == mine[None, :]).astype(jnp.float32)
    split = jnp.arange(mid)
    natural = ((split % part) // grain) * (nrows * grain) + (split // part) * grain + split % grain
    mix = (natural[:, None] == channel[None, :]).astype(jnp.bfloat16)
    here = row.astype(jnp.int32).reshape(1)

    def to_narrow(array):
        return jnp.concatenate(
            [array[:, i * part : (i + 1) * part] for i in range(nrows)], axis=0
        )

    def from_narrow(array):
        size = array.shape[1] // nrows
        return jnp.concatenate([array[:, i * size : (i + 1) * size] for i in range(nrows)], axis=2)

    tiny_width = max(mid_held, wide_part)

    def tiny(array):
        return jnp.pad(array, ((0, 0), (0, tiny_width - array.shape[1])))

    heads_mine = jnp.concatenate(
        [
            product(head, pick, 1, 0, EXACT)
            for head in (segment_head, normal_head, depth_head, contour_head)
        ],
        axis=1,
    )
    def message_runs(array):
        runs = array.reshape(groups, nrows, grain, mid)
        return lax.dynamic_index_in_dim(runs, row, 1, keepdims=True)

    def message_pair(first, second):
        return jnp.concatenate([message_runs(first), message_runs(second)], axis=1)

    run = grain if grain % 8 == 0 else part
    messages_mine = jnp.concatenate(
        [
            message_pair(depth_message, normal_message),
            message_pair(segment_message, contour_message),
        ],
        axis=1,
    ).reshape(held, mid)
    heads_full = lax.all_gather(heads_mine, "batch", axis=0, tiled=True)
    messages_full = regroup(
        lax.all_gather(messages_mine, "batch", axis=0, tiled=True).reshape(
            nbatch * groups, 4, grain, mid
        ),
        run,
    )

    expand_norm_mine = lax.dynamic_index_in_dim(
        expand_norm.reshape(2, nrows, wide_part), row, 1, keepdims=False
    )
    params = jnp.concatenate([tiny(reduce_norm), tiny(dilate_norm), tiny(expand_norm_mine)], axis=0)
    params = jnp.pad(params, ((0, 2), (0, part - tiny_width)))
    expand_mine = lax.dynamic_index_in_dim(
        expand_weight.reshape(mid_held, nbatch, nrows, wide_part), row, 2, keepdims=False
    ).reshape(mid_held, nbatch * wide_part)
    class_lanes = -(-classes // part) * part

    def packed(pieces):
        spans, start = {}, 0
        for name, piece in pieces.items():
            spans[name] = slice(start, start + piece.shape[0])
            start += piece.shape[0]
        return jnp.concatenate(list(pieces.values()), axis=0), spans

    first_mine, first_spans = packed(
        {
            "reduce": to_narrow(row_slice(reduce_weight, 0)),
            "params": params,
            "dilate": row_slice(dilate_weight, 1),
        }
    )
    spread_by_kernel = wide_part == 64 and part % 128 == 0

    def spread_wide(array):
        if spread_by_kernel:
            (blocks,) = single_call(
                spread_kernel, (here, array), [(nrows, quarter, wide // nrows)], [], 1
            )
            blocks = [blocks[key] for key in range(4)]
        else:
            split_blocks = jnp.transpose(array.reshape(quarter, nbatch, nrows, wide_part), (2, 0, 1, 3))
            split_blocks = split_blocks.reshape(nrows, quarter, nbatch * wide_part)
            blocks = [
                lax.dynamic_index_in_dim(split_blocks, row ^ key, 0, keepdims=False)
                for key in range(4)
            ]
        return jnp.concatenate(in_order(exchange_keyed(blocks), row), axis=0)

    features, _ = lax.optimization_barrier((features, first_mine))
    inputs = spread_wide(features.reshape(quarter, wide))
    first_all, inputs = ring.gather(first_mine, True, inputs, 3)
    reduce_full = from_narrow(first_all[:, first_spans["reduce"]]).reshape(nbatch * wide_part, mid)
    params_all = first_all[:, first_spans["params"]]
    dilate_full = first_all[:, first_spans["dilate"]].reshape(nbatch * held, part)

    def all_params(pair, size):
        return jnp.transpose(params_all[:, pair : pair + 2, :size], (1, 0, 2)).reshape(2, nbatch * size)

    reduce_gain, reduce_bias = row_slice(all_params(0, mid_held), 1)
    dilate_gain, dilate_bias = row_slice(all_params(2, mid_held), 1)
    expand_gain, expand_bias = all_params(4, wide_part)

    def exchange_wide(array):
        blocks = array.reshape(nrows, quarter, nbatch * wide_part)
        return exchange_keyed(
            [lax.dynamic_index_in_dim(blocks, row ^ key, 0, keepdims=False) for key in range(4)]
        )

    def collect_wide(got):
        if spread_by_kernel:
            (out,) = single_call(
                collect_kernel,
                (here, *got),
                [(quarter, wide)],
                [(nrows, quarter, wide // nrows)],
                1,
            )
        else:
            out = jnp.stack(in_order(got, row)).reshape(nrows, quarter, nbatch, wide_part)
            out = jnp.transpose(out, (1, 2, 0, 3))
        return out.reshape(1, local_height, breadth, wide)

    def image_of(array):
        return array.reshape(height, breadth, array.shape[-1])

    valid = depth_valid.astype(jnp.float32).reshape(quarter, 1)
    keep, give = single_call(
        split_product_kernel,
        (here, inputs, reduce_full, jnp.full((1, part), jnp.sum(valid))),
        [(2, pixels + 8, part)] * 2,
        [(pixels, mid)],
        2 * pixels * mid * mid,
    )
    mine_terms, got_terms = scatter_end(keep, give)
    pre_reduce = mine_terms + got_terms
    valid_row = pre_reduce[pixels]
    pre_reduce = pre_reduce[:pixels]
    total_one = sum_batch(jnp.concatenate([sums_of(pre_reduce, pre_reduce), valid_row[None]]))
    scale = valid * (count / total_one[2, 0])
    hat_one, normed_one, inverse_one = norm_forward(
        pre_reduce, total_one, reduce_gain, reduce_bias, count
    )
    pre_dilate, mid_in = joined_conv(
        here, gather_keyed(image_of(jax.nn.silu(normed_one))), dilate_full, 2
    )
    total_two = sum_batch(sums_of(pre_dilate, pre_dilate))
    total_two, heads_full = lax.optimization_barrier((total_two, heads_full))
    hat_two, normed_two, inverse_two = norm_forward(
        pre_dilate, total_two, dilate_gain, dilate_bias, count
    )

    beside = mid // class_lanes
    square_mine, square_spans = packed(
        {
            "depth_gate": depth_gate,
            "segment_gate": segment_gate,
            "expand": expand_mine,
            "classifier": jnp.pad(classifier, ((0, 0), (0, class_lanes - classes)))
            .reshape(beside, mid_held // beside, class_lanes)
            .transpose(1, 0, 2)
            .reshape(mid_held // beside, mid),
        }
    )
    square_mine, inverse_two = lax.optimization_barrier((square_mine, inverse_two))
    feats, mid_out, pairs = joined_conv(
        here, gather_keyed(image_of(jax.nn.silu(normed_two))), heads_full, 1, True
    )
    square_all, feats = ring.gather(square_mine, False, feats, 2)
    depth_gate_w, segment_gate_w, expand_w = [
        square_all[:, square_spans[name]].reshape(mid, mid)
        for name in ("depth_gate", "segment_gate", "expand")
    ]
    classifier_w = (
        square_all[:, square_spans["classifier"]]
        .reshape(nbatch, mid_held // beside, beside, class_lanes)
        .transpose(0, 2, 1, 3)
        .reshape(mid, class_lanes)
    )
    feats_image = image_of(feats)

    pairs_got = jnp.stack(exchange_keyed([pairs[key] for key in range(4)]))
    block_cotangent, _ = lax.optimization_barrier((block_cotangent, feats))
    cotangent = spread_wide(block_cotangent.reshape(quarter, wide))
    pairs_got, cotangent = lax.optimization_barrier((pairs_got, cotangent))
    depth_cotangent = depth_cotangent.reshape(quarter, mid)
    both, one_map = (2 * quarter, mid), (quarter, mid)
    feat_pair, open_pair, d_depth_note = single_call(
        gates_kernel,
        (here, pairs_got, mix, depth_gate_w, segment_gate_w, depth_cotangent, scale),
        [both, both, one_map],
        [both],
        8 * quarter * mid * mid,
    )

    def lines(array):
        return array.reshape(local_height, breadth, mid)

    depth_pair_grad, d_depth_image = note_grad(here, feats, 0, gather_keyed(lines(d_depth_note)), run)
    depth_pair_sums = lax.psum_scatter(
        regroup(depth_pair_grad, grain).reshape(-1, mid), "batch", scatter_dimension=0, tiled=True
    )
    flat_mid_out = mid_out.reshape(pixels, mid)
    pre_expand = product(flat_mid_out, expand_w, 1, 0)
    hat_three, normed_three, inverse_three = norm_forward(
        pre_expand, sum_batch(sums_of(pre_expand, pre_expand)), expand_gain, expand_bias, count
    )
    summed = normed_three + inputs
    block_blocks = exchange_wide(jax.nn.silu(summed))
    d_summed = cotangent * silu_grad(summed)
    d_pre_expand, expand_sums = norm_backward(
        d_summed, hat_three, inverse_three, expand_gain, count, False
    )
    messages_full, block_blocks, _ = lax.optimization_barrier(
        (messages_full, block_blocks, (expand_sums, depth_pair_grad))
    )
    block_out = collect_wide(block_blocks)

    segment_mine, segment_got = scatter_end(*note_forward(here, feats_image, 1, messages_full))

    def segment_body(*refs):
        segment_kernel(classes, *refs)

    segment_stream, d_segment_note, direct_segment, segment_gate_grad, classifier_grad = single_call(
        segment_body,
        (
            here,
            segment_mine,
            segment_got,
            feat_pair[quarter:],
            open_pair[quarter:],
            labels.reshape(quarter, 1),
            classifier_w,
            segment_gate_w,
            mix,
        ),
        [one_map, one_map, (4, quarter, part), (mid, mid), (mid, class_lanes)],
        [one_map],
        8 * quarter * mid * mid,
    )

    segment_pair_grad, d_segment_image = note_grad(
        here, feats, 1, gather_keyed(lines(d_segment_note)), run
    )
    depth_mine, depth_got = scatter_end(*note_forward(here, feats_image, 0, messages_full))
    hops = Hops(ring, regroup(segment_pair_grad, grain).reshape(nbatch, held // 2, mid), True)
    d_depth_image, _ = lax.optimization_barrier((d_depth_image, segment_pair_grad))
    depth_back = note_back(d_depth_image, 0, messages_full)
    d_segment_image, depth_back = hops.step((d_segment_image, depth_back))
    segment_back = note_back(d_segment_image, 1, messages_full)
    depth_stream, direct_both, depth_gate_grad = single_call(
        depth_kernel,
        (
            here,
            depth_mine,
            depth_got,
            feat_pair[:quarter],
            open_pair[:quarter],
            depth_cotangent,
            scale,
            depth_gate_w,
            mix,
            direct_segment,
        ),
        [one_map, (4, 2 * quarter, part), (mid, mid)],
        [one_map],
        8 * quarter * mid * mid,
    )
    direct_got = jnp.stack(exchange_keyed([direct_both[key] for key in range(4)]))
    heads_grad, d_feats = heads_grad_of(
        here,
        hops.step(flat_mid_out),
        image_of(depth_back),
        image_of(segment_back),
        direct_got.reshape(4, 2 * local_height, breadth, part),
    )
    heads_sums = lax.psum_scatter(heads_grad, "batch", scatter_dimension=0, tiled=True)

    expand_grad = product(flat_mid_out, d_pre_expand, 0, 0).reshape(nbatch, mid_held, mid)

    gate_terms = jnp.stack(
        [
            depth_gate_grad,
            segment_gate_grad,
            jnp.pad(classifier_grad, ((0, 0), (0, mid - class_lanes))),
        ]
    )
    gate_rows = mid_held // nrows
    gate_terms = jnp.transpose(gate_terms.reshape(3, nbatch, nrows, gate_rows, mid), (2, 1, 0, 3, 4))
    gate_sums = scatter_rows(gate_terms, row).reshape(nbatch, 3 * gate_rows, mid)

    d_feats = hops.step(d_feats)
    mine_terms, got_terms = scatter_end(
        *conv_back(here, d_feats, heads_full, 1, product(d_pre_expand, expand_w, 1, 1))
    )
    mine_terms, depth_pair_sums = hops.step((mine_terms, depth_pair_sums))
    segment_pair_sums = hops.result()
    d_pre_dilate, dilate_sums = norm_backward(
        (mine_terms + got_terms) * silu_grad(normed_two), hat_two, inverse_two, dilate_gain, count, False
    )
    d_dilate_image = image_of(d_pre_dilate)
    mine_terms, got_terms = scatter_end(*conv_back(here, d_dilate_image, dilate_full, 2))
    d_pre_reduce, reduce_sums = norm_backward(
        (mine_terms + got_terms) * silu_grad(normed_one), hat_one, inverse_one, reduce_gain, count, False
    )
    reduce_grad, features_back = single_call(
        reduce_back_kernel,
        (here, *gather_keyed(d_pre_reduce), inputs, reduce_full, d_summed),
        [(mid, mid), (pixels, mid)],
        [(pixels, mid)],
        4 * pixels * mid * mid,
    )
    dilate_grad = conv_grad(mid_in.reshape(pixels, mid), d_dilate_image, 2).reshape(
        nbatch, held, part
    )
    narrow = held // nrows
    square_grad = jnp.concatenate(
        [
            jnp.concatenate(
                [dilate_grad[:, i * narrow : (i + 1) * narrow] for i in range(nrows)], axis=2
            ),
            expand_grad,
            gate_sums,
        ],
        axis=1,
    )
    square_grad, reduce_sums, depth_pair_sums, segment_pair_sums = lax.optimization_barrier(
        (square_grad, reduce_sums, depth_pair_sums, segment_pair_sums)
    )
    square_hops = Hops(ring, square_grad, False)
    square_hops.step()
    square_hops.step()
    heads_sums = square_hops.await_beside(heads_sums)
    square_hops.step()
    square_hops.step()
    square_sums = square_hops.result()
    reduce_out = ring.scatter(reduce_grad.reshape(nbatch, wide_part, mid), True)
    features_grad = collect_wide(exchange_wide(features_back))

    pair_sums = jnp.concatenate([depth_pair_sums, segment_pair_sums], axis=0) * factor
    pairs_out = jnp.stack(gather_rows(pair_sums, row)).reshape(nrows, 2, groups, 2, grain, mid)
    depth_pair_out, segment_pair_out = pairs_out[:, 0], pairs_out[:, 1]

    def message_out(pair_got, index):
        return jnp.transpose(pair_got[:, :, index], (1, 0, 2, 3)).reshape(held, mid)

    segment_out, normal_out, depth_out, contour_out = single_call(
        heads_out_kernel,
        (here, *gather_keyed(heads_sums * factor), mix),
        [(held, mid)] * 4,
        [(held, mid)],
        8 * held * mid * mid,
    )

    expand_mine_sums = lax.dynamic_slice_in_dim(expand_sums, batch * wide_part, wide_part, 1)
    norm_sums = jnp.concatenate(
        [
            jnp.pad(sums, ((0, 0), (0, mid - sums.shape[1])))
            for sums in (reduce_sums, dilate_sums, expand_mine_sums)
        ],
        axis=0,
    )
    small = jnp.concatenate([square_sums, jnp.pad(norm_sums, ((0, 2), (0, 0)))], axis=0) * factor
    small_got = gather_rows(small, row)
    squares_got = jnp.stack([block[narrow : narrow + mid_held + 3 * gate_rows] for block in small_got])
    dilate_out = jnp.concatenate(
        [
            jnp.concatenate(
                [block[:narrow, i * part : (i + 1) * part] for i in range(nrows)], axis=0
            )
            for block in small_got
        ],
        axis=1,
    )
    expand_out = jnp.transpose(
        squares_got[:, :mid_held].reshape(nrows, mid_held, nbatch, wide_part), (1, 2, 0, 3)
    ).reshape(mid_held, wide)

    def gate_out(index):
        start = mid_held + index * gate_rows
        return squares_got[:, start : start + gate_rows].reshape(mid_held, mid)

    norms_got = [block[-8:] for block in small_got]

    def norm_out(start):
        full = jnp.concatenate([block[start : start + 2, :part] for block in norms_got], axis=1)
        return lax.dynamic_slice_in_dim(full, batch * mid_held, mid_held, 1)

    expand_norm_out = jnp.concatenate([block[4:6, :wide_part] for block in norms_got], axis=1)
    reduce_got = jnp.concatenate(gather_rows(reduce_out * factor, row), axis=0)

    return (
        block_out,
        depth_stream.reshape(1, local_height, breadth, mid),
        segment_stream.reshape(1, local_height, breadth, mid),
        features_grad,
        reduce_got,
        norm_out(0),
        dilate_out,
        norm_out(2),
        expand_out,
        expand_norm_out,
        depth_out,
        segment_out,
        normal_out,
        contour_out,
        message_out(depth_pair_out, 0),
        message_out(segment_pair_out, 0),
        message_out(depth_pair_out, 1),
        message_out(segment_pair_out, 1),
        gate_out(0),
        gate_out(1),
        gate_out(2)[:, :classes],
    )


def solution(mesh):
    pixels = P("batch", "rows", None, None)
    plane = P("batch", "rows", None)
    weight = P("batch", None)
    norm = P(None, "batch")
    in_specs = (
        (pixels, weight, norm, weight, norm, weight, norm) + (weight,) * 11 + (plane, plane, pixels, pixels)
    )
    out_specs = (pixels,) * 4 + (weight, norm) * 3 + (weight,) * 11
    return jax.shard_map(shards, mesh=mesh, in_specs=in_specs, out_specs=out_specs, check_vma=False)
```

```python
import math

import jax
import jax.numpy as jnp
from jax import lax
from jax.experimental import pallas as pl
from jax.experimental.pallas import tpu as pltpu
from jax.sharding import PartitionSpec as P

EPSILON = 1e-05
EXACT = lax.Precision.HIGHEST
FINE = lax.Precision.HIGH
LONGEST_RING = 8
LANES = 128


def product(left, right, left_dim, right_dim, precision=FINE):
    return lax.dot_general(
        left,
        right,
        (((left_dim,), (right_dim,)), ((), ())),
        precision=precision,
        preferred_element_type=jnp.float32,
    )


def halves(values):
    high = values.astype(jnp.bfloat16)
    return high, (values - high.astype(jnp.float32)).astype(jnp.bfloat16)


def three_pass(left, right, left_dim, right_dim):
    dims = (((left_dim,), (right_dim,)), ((), ()))

    def one(a, b):
        return lax.dot_general(a, b, dims, preferred_element_type=jnp.float32)

    return one(left[0], right[0]) + (one(left[0], right[1]) + one(left[1], right[0]))


def frame(image_ref, framed, dilation):
    height, breadth, depth = image_ref.shape
    edge = jnp.zeros((3, dilation, breadth, depth), jnp.float32)
    framed[:, :dilation] = edge
    framed[:, dilation + height :] = edge
    image = image_ref[...]
    side = jnp.zeros((height, dilation, depth), jnp.float32)
    inner = slice(dilation, dilation + height)
    framed[1, inner] = image
    framed[0, inner, dilation:, :] = image[:, : breadth - dilation]
    framed[0, inner, :dilation, :] = side
    framed[2, inner, : breadth - dilation, :] = image[:, dilation:]
    framed[2, inner, breadth - dilation :, :] = side


def shifted(framed, tap, height, dilation):
    block = framed[tap % 3, pl.ds((tap // 3) * dilation, height)]
    return block.reshape(height * block.shape[1], block.shape[2])


def exact_pick(values, choice, choice_dim):
    high = values.astype(jnp.bfloat16)
    rest = values - high.astype(jnp.float32)
    middle = rest.astype(jnp.bfloat16)
    low = (rest - middle.astype(jnp.float32)).astype(jnp.bfloat16)
    dims = (((1,), (choice_dim,)), ((), ()))

    def one(part):
        return lax.dot_general(part, choice, dims, preferred_element_type=jnp.float32)

    return one(high) + (one(middle) + one(low))


def at_lanes(index, size):
    return pl.ds(pl.multiple_of(index * size, size), size)


def keep_and_give(row, load, keep_ref, give_ref):
    core, side = row & 1, row >> 1
    for k in range(2):
        base = (side ^ k) * 2
        keep_ref[k] = load(base + core)
        give_ref[k] = load(base + 1 - core)


def joined_conv_kernel(dilation, row_ref, one, two, three, four, weight_ref, out_ref, image_ref, framed):
    tap = pl.program_id(0)

    @pl.when(tap == 0)
    def _():
        part = one.shape[2]
        for key, block in enumerate((one, two, three, four)):
            image_ref[:, :, at_lanes(row_ref[0] ^ key, part)] = block[...]
        frame(image_ref, framed, dilation)
        out_ref[...] = jnp.zeros_like(out_ref)

    moved = halves(shifted(framed, tap, image_ref.shape[0], dilation))
    out_ref[...] += three_pass(moved, halves(weight_ref[...]), 1, 0)


def heads_kernel(
    row_ref, one, two, three, four, weight_ref, out_ref, image_ref, pairs_ref, framed
):
    joined_conv_kernel(1, row_ref, one, two, three, four, weight_ref, out_ref, image_ref, framed)

    @pl.when(pl.program_id(0) == 8)
    def _():
        _, double, part = pairs_ref.shape
        quarter = double // 2
        for key in range(4):
            rows = pl.ds((row_ref[0] ^ key) * quarter, quarter)
            pairs_ref[key, :quarter] = out_ref[rows, 2 * part : 3 * part]
            pairs_ref[key, quarter:] = out_ref[rows, :part]


def split_product_kernel(row_ref, left_ref, right_ref, extra_ref, keep_ref, give_ref, total):
    total[...] = three_pass(halves(left_ref[...]), halves(right_ref[...]), 1, 0)
    pixels, part = left_ref.shape[0], keep_ref.shape[2]
    keep_and_give(
        row_ref[0],
        lambda j: total[:, at_lanes(j, part)],
        keep_ref.at[:, :pixels],
        give_ref.at[:, :pixels],
    )
    for ref in (keep_ref, give_ref):
        ref[:, pixels:] = jnp.broadcast_to(extra_ref[...], (2, 8, part))


def conv_back_kernel(dilation, row_ref, image_ref, weight_ref, keep_ref, give_ref, framed, total):
    tap = pl.program_id(0)

    @pl.when(tap == 0)
    def _():
        frame(image_ref, framed, dilation)
        total[...] = jnp.zeros_like(total)

    moved = halves(shifted(framed, 8 - tap, image_ref.shape[0], dilation))
    total[...] += three_pass(moved, halves(weight_ref[...]), 1, 1)

    @pl.when(tap == 8)
    def _():
        part = keep_ref.shape[2]
        keep_and_give(row_ref[0], lambda j: total[:, at_lanes(j, part)], keep_ref, give_ref)


def expand_back_kernel(
    row_ref, left_ref, right_ref, keep_in_ref, give_in_ref, keep_ref, give_ref, total
):
    total[...] = three_pass(halves(left_ref[...]), halves(right_ref[...]), 1, 1)
    part = keep_ref.shape[2]
    keep_and_give(row_ref[0], lambda j: total[:, at_lanes(j, part)], keep_ref, give_ref)
    keep_ref[...] += keep_in_ref[...]
    give_ref[...] += give_in_ref[...]


def conv_grad_kernel(dilation, input_ref, grad_ref, out_ref, framed, high, low):
    tap = pl.program_id(0)

    @pl.when(tap == 0)
    def _():
        frame(grad_ref, framed, dilation)
        high[...], low[...] = halves(jnp.transpose(input_ref[...]))

    moved = halves(shifted(framed, 8 - tap, grad_ref.shape[0], dilation))
    out_ref[...] = three_pass((high[...], low[...]), moved, 1, 0)


def heads_grad_kernel(
    row_ref, input_ref, first_ref, second_ref, direct_ref, out_ref, image_ref, framed, high, low
):
    tap = pl.program_id(0)

    @pl.when(tap == 0)
    def _():
        lanes = first_ref.shape[2]
        _, double, breadth, part = direct_ref.shape
        lines = double // 2
        image_ref[:, :, :lanes] = first_ref[...]
        image_ref[:, :, lanes:] = second_ref[...]
        for key in range(4):
            rows = pl.ds((row_ref[0] ^ key) * lines, lines)
            image_ref[rows, :, :part] += direct_ref[key, :lines]
            image_ref[rows, :, lanes : lanes + part] += direct_ref[key, lines:]

    conv_grad_kernel(1, input_ref, image_ref, out_ref, framed, high, low)


def source_rows(weight):
    return jnp.concatenate(
        [weight[:, k].reshape(-1, weight.shape[-1]) for k in range(weight.shape[1])], axis=0
    )


def note_kernel(row_ref, image_ref, weight_ref, keep_ref, give_ref, framed, total):
    tap = pl.program_id(0)

    @pl.when(tap == 0)
    def _():
        frame(image_ref, framed, 1)
        total[...] = jnp.zeros_like(total)

    moved = shifted(framed, tap, image_ref.shape[0], 1)
    total[...] += three_pass(halves(moved), halves(source_rows(weight_ref[...])), 1, 0)

    @pl.when(tap == 8)
    def _():
        quarter = keep_ref.shape[1]
        keep_and_give(
            row_ref[0], lambda j: total[pl.ds(j * quarter, quarter), :], keep_ref, give_ref
        )


def note_back_kernel(note_ref, weight_ref, out_ref, framed):
    tap = pl.program_id(0)

    @pl.when(tap == 0)
    def _():
        frame(note_ref, framed, 1)
        out_ref[...] = jnp.zeros_like(out_ref)

    moved = halves(shifted(framed, 8 - tap, note_ref.shape[0], 1))
    out_ref[...] += three_pass(moved, halves(source_rows(weight_ref[...])), 1, 1)


def note_grad_kernel(row_ref, input_ref, one, two, three, four, *rest):
    out_ref, image_ref, framed, high, low = rest[-5:]
    tap = pl.program_id(0)

    @pl.when(tap == 0)
    def _():
        lines = one.shape[0]
        for key, block in enumerate((one, two, three, four)):
            image_ref[pl.ds((row_ref[0] ^ key) * lines, lines)] = block[...]
        frame(image_ref, framed, 1)
        high[...], low[...] = halves(jnp.transpose(input_ref[...]))

    moved = halves(shifted(framed, 8 - tap, image_ref.shape[0], 1))
    grad = three_pass((high[...], low[...]), moved, 1, 0)
    runs, _, grain, mid = out_ref.shape
    part = grad.shape[0] // 2
    for k in range(2):
        out_ref[:, k] = grad[k * part : (k + 1) * part].reshape(runs, grain, mid)


def gates_kernel(
    row_ref, pairs_ref, mix_ref, depth_gate_ref, segment_gate_ref, cotangent_ref, scale_ref,
    feat_ref, open_ref, d_note_ref, joined,
):
    _, double, part = pairs_ref.shape
    quarter = double // 2
    for key in range(4):
        joined[:, at_lanes(row_ref[0] ^ key, part)] = pairs_ref[key]
    feat = exact_pick(joined[...], mix_ref[...], 0)
    feat_ref[...] = feat
    for index, gate_ref in enumerate((depth_gate_ref, segment_gate_ref)):
        rows = slice(index * quarter, (index + 1) * quarter)
        gate = three_pass(halves(feat[rows]), halves(gate_ref[...]), 1, 0)
        open_ref[rows] = jax.nn.sigmoid(gate)
    d_note_ref[...] = cotangent_ref[...] * scale_ref[...] * open_ref[:quarter]


def gate_back(row_ref, feat, opened, note, d_stream, d_note, gate_ref, mix_ref, gate_grad_ref, joined):
    d_pre = halves(d_note * note * (1.0 - opened))
    gate_grad_ref[...] = three_pass(halves(jnp.transpose(feat)), d_pre, 1, 0)
    direct = d_stream + three_pass(d_pre, halves(gate_ref[...]), 1, 1)
    joined[...] = exact_pick(direct, mix_ref[...], 1)


def segment_kernel(
    classes, row_ref, mine_ref, got_ref, feat_ref, open_ref, labels_ref, classifier_ref, gate_ref, mix_ref,
    stream_ref, d_note_ref, direct_ref, gate_grad_ref, classifier_grad_ref, joined,
):
    note = mine_ref[...] + got_ref[...]
    feat, opened = feat_ref[...], open_ref[...]
    stream = feat + opened * note
    stream_ref[...] = stream
    weight = halves(classifier_ref[...])
    logits = three_pass(halves(stream), weight, 1, 0)
    lane = lax.broadcasted_iota(jnp.int32, logits.shape, 1)
    real = lane < classes
    top = jnp.max(jnp.where(real, logits, -3e38), axis=1, keepdims=True)
    powers = jnp.where(real, jnp.exp(jnp.where(real, logits - top, 0.0)), 0.0)
    onehot = jnp.where(lane == labels_ref[...], 1.0, 0.0)
    d_logits = powers / jnp.sum(powers, axis=1, keepdims=True) - onehot
    d_stream = three_pass(halves(d_logits), weight, 1, 1)
    d_note = d_stream * opened
    d_note_ref[...] = d_note
    classifier_grad_ref[...] = three_pass(halves(jnp.transpose(stream)), halves(d_logits), 1, 0)
    gate_back(row_ref, feat, opened, note, d_stream, d_note, gate_ref, mix_ref, gate_grad_ref, joined)
    part = direct_ref.shape[2]
    for key in range(4):
        direct_ref[key] = joined[:, at_lanes(row_ref[0] ^ key, part)]


def depth_kernel(
    row_ref, mine_ref, got_ref, feat_ref, open_ref, cotangent_ref, scale_ref, gate_ref, mix_ref, other_ref,
    stream_ref, direct_ref, gate_grad_ref, joined,
):
    note = mine_ref[...] + got_ref[...]
    feat, opened = feat_ref[...], open_ref[...]
    stream_ref[...] = feat + opened * note
    d_stream = cotangent_ref[...] * scale_ref[...]
    gate_back(
        row_ref, feat, opened, note, d_stream, d_stream * opened, gate_ref, mix_ref, gate_grad_ref, joined
    )
    _, double, part = direct_ref.shape
    quarter = double // 2
    for key in range(4):
        direct_ref[key, :quarter] = other_ref[key]
        direct_ref[key, quarter:] = joined[:, at_lanes(row_ref[0] ^ key, part)]


def reduce_back_kernel(
    row_ref, one, two, three, four, input_ref, weight_ref, d_summed_ref, grad_ref, out_ref, joined
):
    part = one.shape[1]
    for key, block in enumerate((one, two, three, four)):
        joined[:, at_lanes(row_ref[0] ^ key, part)] = block[...]
    d_pre = halves(joined[...])
    grad_ref[...] = three_pass(halves(jnp.transpose(input_ref[...])), d_pre, 1, 0)
    out_ref[...] = d_summed_ref[...] + three_pass(d_pre, halves(weight_ref[...]), 1, 1)


def heads_out_kernel(row_ref, one, two, three, four, mix_ref, *rest):
    outs, joined = rest[:-1], rest[-1]
    part = joined.shape[1] // 4
    for index, out_ref in enumerate(outs):
        lanes = slice(index * part, (index + 1) * part)
        for key, block in enumerate((one, two, three, four)):
            joined[:, at_lanes(row_ref[0] ^ key, part)] = block[:, lanes]
        out_ref[...] = exact_pick(joined[...], mix_ref[...], 0)


def spread_kernel(row_ref, array_ref, out_ref):
    low = lax.broadcasted_iota(jnp.int32, (array_ref.shape[0], 128), 1) < 64
    for device in range(4):
        key = row_ref[0] ^ device
        for k in range(out_ref.shape[2] // 128):
            start = 512 * k + 128 * (device // 2)
            even = array_ref[:, start : start + 128]
            odd = array_ref[:, start + 256 : start + 384]
            if device % 2:
                block = jnp.where(low, pltpu.roll(even, 64, 1), odd)
            else:
                block = jnp.where(low, even, pltpu.roll(odd, 64, 1))
            out_ref[key, :, 128 * k : 128 * (k + 1)] = block


def collect_kernel(row_ref, one, two, three, four, out_ref, ordered):
    for key, block in enumerate((one, two, three, four)):
        ordered[row_ref[0] ^ key] = block[...]
    low = lax.broadcasted_iota(jnp.int32, (one.shape[0], 128), 1) < 64
    for k in range(one.shape[1] // 128):
        for pair in range(2):
            first = ordered[2 * pair, :, 128 * k : 128 * (k + 1)]
            second = ordered[2 * pair + 1, :, 128 * k : 128 * (k + 1)]
            start = 512 * k + 128 * pair
            out_ref[:, start : start + 128] = jnp.where(low, first, pltpu.roll(second, 64, 1))
            out_ref[:, start + 256 : start + 384] = jnp.where(low, pltpu.roll(first, 64, 1), second)


def regroup(array, run):
    runs, sources, grain, mid = array.shape
    if grain == run:
        return array
    if run > grain:
        lists = array.reshape(-1, run // grain, sources, grain, mid)
        return jnp.transpose(lists, (0, 2, 1, 3, 4)).reshape(-1, sources, run, mid)
    parts = array.reshape(runs, sources, grain // run, run, mid)
    return jnp.transpose(parts, (0, 2, 1, 3, 4)).reshape(-1, sources, run, mid)


VMEM_LIMIT = 56 * 2**20
SCALAR = pl.BlockSpec(memory_space=pltpu.SMEM)


def kernel_call(body, grid, in_specs, out_specs, out_shape, scratch, flops):
    return pl.pallas_call(
        body,
        grid=grid,
        in_specs=in_specs,
        out_specs=out_specs,
        out_shape=out_shape,
        scratch_shapes=scratch,
        compiler_params=pltpu.CompilerParams(
            dimension_semantics=("arbitrary",) * len(grid), vmem_limit_bytes=VMEM_LIMIT
        ),
        cost_estimate=pl.CostEstimate(flops=3 * flops, bytes_accessed=12 * 2**20, transcendentals=0),
    )


def single_call(body, args, outs, scratch, flops):
    return kernel_call(
        body,
        (1,),
        [SCALAR] + [whole_spec(arg.shape) for arg in args[1:]],
        [whole_spec(out) for out in outs],
        [jax.ShapeDtypeStruct(out, jnp.float32) for out in outs],
        [pltpu.VMEM(shape, jnp.float32) for shape in scratch],
        flops,
    )(*args)


def framed_scratch(image, dilation):
    height, breadth, depth = image
    return pltpu.VMEM((3, height + 2 * dilation, breadth, depth), jnp.float32)


def whole_spec(shape):
    return pl.BlockSpec(shape, lambda *_: (0,) * len(shape))


def struct(shape):
    return jax.ShapeDtypeStruct(shape, jnp.float32)


def tap_rows(rows, cols):
    return pl.BlockSpec((rows, cols), lambda tap: (tap, 0))


def tap_runs(weight_shape):
    return pl.BlockSpec((weight_shape[0] // 9,) + weight_shape[1:], lambda tap: (tap, 0, 0, 0))


def joined_conv(row, blocks, weight, dilation, with_pairs=False):
    height, breadth, part = blocks[0].shape
    image = (height, breadth, 4 * part)
    rows, cols = weight.shape[0] // 9, weight.shape[1]
    shapes = [(height * breadth, cols), image]
    if with_pairs:
        body = heads_kernel
        shapes.append((4, height * breadth // 2, part))
    else:

        def body(*refs):
            joined_conv_kernel(dilation, *refs)

    return kernel_call(
        body,
        (9,),
        [SCALAR] + [whole_spec(blocks[0].shape)] * 4 + [tap_rows(rows, cols)],
        [whole_spec(shape) for shape in shapes],
        [struct(shape) for shape in shapes],
        [framed_scratch(image, dilation)],
        2 * 9 * height * breadth * rows * cols,
    )(row, *blocks, weight)


def conv_back(row, image, weight, dilation):
    height, breadth, _ = image.shape
    rows, cols = weight.shape[0] // 9, weight.shape[1]
    pixels = height * breadth
    shape = (2, pixels, rows // 4)

    def body(*refs):
        conv_back_kernel(dilation, *refs)

    return kernel_call(
        body,
        (9,),
        [SCALAR, whole_spec(image.shape), tap_rows(rows, cols)],
        [whole_spec(shape)] * 2,
        [struct(shape)] * 2,
        [framed_scratch(image.shape, dilation), pltpu.VMEM((pixels, rows), jnp.float32)],
        2 * 9 * pixels * rows * cols,
    )(row, image, weight)


def conv_grad(flat_input, image_grad, dilation):
    pixels, depth = flat_input.shape
    cols = image_grad.shape[2]

    def body(*refs):
        conv_grad_kernel(dilation, *refs)

    return kernel_call(
        body,
        (9,),
        [whole_spec(flat_input.shape), whole_spec(image_grad.shape)],
        tap_rows(depth, cols),
        struct((9 * depth, cols)),
        [framed_scratch(image_grad.shape, dilation)]
        + [pltpu.VMEM((depth, pixels), jnp.bfloat16)] * 2,
        2 * 9 * pixels * depth * cols,
    )(flat_input, image_grad)


def heads_grad_of(row, flat_input, first, second, direct):
    pixels, depth = flat_input.shape
    height, breadth, lanes = first.shape
    image = (height, breadth, 2 * lanes)
    return kernel_call(
        heads_grad_kernel,
        (9,),
        [SCALAR] + [whole_spec(array.shape) for array in (flat_input, first, second, direct)],
        [tap_rows(depth, 2 * lanes), whole_spec(image)],
        [struct((9 * depth, 2 * lanes)), struct(image)],
        [framed_scratch(image, 1)] + [pltpu.VMEM((depth, pixels), jnp.bfloat16)] * 2,
        2 * 9 * pixels * depth * 2 * lanes,
    )(row, flat_input, first, second, direct)


def note_forward(row, image, pair, weight):
    height, breadth, depth = image.shape
    depth = depth // 2
    mid = weight.shape[3]
    pixels = height * breadth
    shape = (2, pixels // 4, mid)
    return kernel_call(
        note_kernel,
        (9,),
        [
            SCALAR,
            pl.BlockSpec((height, breadth, depth), lambda tap: (0, 0, pair)),
            tap_runs(weight.shape),
        ],
        [whole_spec(shape)] * 2,
        [struct(shape)] * 2,
        [framed_scratch((height, breadth, depth), 1), pltpu.VMEM((pixels, mid), jnp.float32)],
        2 * 9 * pixels * depth * mid,
    )(row, image, weight)


def note_back(note, weight):
    height, breadth, mid = note.shape
    shape = (height * breadth, weight.shape[0] // 9 * weight.shape[1] * weight.shape[2])
    return kernel_call(
        note_back_kernel,
        (9,),
        [whole_spec(note.shape), tap_runs(weight.shape)],
        whole_spec(shape),
        struct(shape),
        [framed_scratch(note.shape, 1)],
        2 * 9 * shape[0] * shape[1] * mid,
    )(note, weight)


def note_grad(row, flat_input, pair, blocks, grain, grads=None):
    pixels, depth = flat_input.shape
    depth = depth // 2
    lines, breadth, mid = blocks[0].shape
    image = (4 * lines, breadth, mid)
    runs = depth // 2 // grain
    shape = (9 * runs, 4, grain, mid)
    others = [] if grads is None else [grads]
    return pl.pallas_call(
        note_grad_kernel,
        grid=(9,),
        in_specs=[SCALAR, pl.BlockSpec((pixels, depth), lambda tap: (0, pair))]
        + [whole_spec(blocks[0].shape)] * 4
        + [pl.BlockSpec(memory_space=pl.ANY)] * len(others),
        out_specs=[
            pl.BlockSpec((runs, 2, grain, mid), lambda tap: (tap, pair, 0, 0)),
            whole_spec(image),
        ],
        out_shape=[struct(shape), struct(image)],
        scratch_shapes=[framed_scratch(image, 1)] + [pltpu.VMEM((depth, pixels), jnp.bfloat16)] * 2,
        input_output_aliases={6: 0} if others else {},
        compiler_params=pltpu.CompilerParams(
            dimension_semantics=("arbitrary",), vmem_limit_bytes=VMEM_LIMIT
        ),
        cost_estimate=pl.CostEstimate(
            flops=6 * 9 * pixels * depth * mid, bytes_accessed=12 * 2**20, transcendentals=0
        ),
    )(row, flat_input, *blocks, *others)


def silu_grad(values):
    gate_val = jax.nn.sigmoid(values)
    return gate_val * (1.0 + values * (1.0 - gate_val))


def swap_rows(block, mask):
    size = lax.axis_size("rows")
    return lax.ppermute(block, "rows", [(i, i ^ mask) for i in range(size)])


def in_order(blocks, row):
    count = len(blocks)
    if count == 1:
        return blocks
    half = count // 2
    near = in_order(blocks[:half], row)
    far = in_order(blocks[half:], row)
    upper = (row & half) != 0
    first = [jnp.where(upper, f, n) for n, f in zip(near, far)]
    second = [jnp.where(upper, n, f) for n, f in zip(near, far)]
    return first + second


def gather_keyed(block):
    far = swap_rows(block, 2)
    return [block, swap_rows(block, 1), far, swap_rows(far, 1)]


def gather_rows(block, row):
    return in_order(gather_keyed(block), row)


def scatter_end(keep, give):
    got = swap_rows(give, 1)
    other = keep[1] + got[1]
    return keep[0] + got[0], swap_rows(other, 2)


def scatter_rows(blocks, row):
    core, side = row & 1, row >> 1
    pairs = blocks.reshape((2, 2) + blocks.shape[1:])
    keep = lax.dynamic_index_in_dim(pairs, core, 1, keepdims=False)
    got = keep + swap_rows(lax.dynamic_index_in_dim(pairs, 1 - core, 1, keepdims=False), 1)
    mine = lax.dynamic_index_in_dim(got, side, 0, keepdims=False)
    return mine + swap_rows(lax.dynamic_index_in_dim(got, 1 - side, 0, keepdims=False), 2)


def exchange_keyed(blocks):
    return [blocks[0]] + [swap_rows(blocks[mask], mask) for mask in range(1, 4)]


def sum_batch(values, direct=False):
    size = lax.axis_size("batch")
    if size & (size - 1):
        return lax.psum(values, "batch")

    def swap(block, mask):
        return lax.ppermute(block, "batch", [(i, i ^ mask) for i in range(size)])

    if direct and size <= LONGEST_RING:
        return values + sum(swap(values, mask) for mask in range(1, size))
    mask = 1
    while mask < size:
        values = values + swap(values, mask)
        mask *= 2
    return values


class Ring:
    def __init__(self, batch):
        size = lax.axis_size("batch")
        self.batch, self.size = batch, size
        self.order = list(range(0, size, 2)) + [i for i in reversed(range(size)) if i % 2]
        self.place = {b: p for p, b in enumerate(self.order)}
        self.up = [(self.order[p], self.order[(p + 1) % size]) for p in range(size)]
        self.down = [(b, a) for a, b in self.up]
        table = [[self.order[(self.place[b] + k) % size] for k in range(size)] for b in range(size)]
        self.row = jnp.array(table, jnp.int32)[batch]

    def at(self, offset):
        return self.row[offset % self.size]

    def steps(self, longer_up):
        more = self.size // 2
        less = self.size - 1 - more
        return (more, less) if longer_up else (less, more)

    def gather(self, block, longer_up, beside=None, beside_step=0):
        if self.size > LONGEST_RING:
            return lax.all_gather(block, "batch", axis=0, tiled=False), beside
        whole = jnp.zeros((self.size,) + block.shape, block.dtype)
        whole = lax.dynamic_update_index_in_dim(whole, block, self.batch, 0)
        ups, downs = self.steps(longer_up)
        rising = falling = block
        for k in range(1, max(ups, downs) + 1):
            if k == beside_step and beside is not None:
                rising, falling, beside = lax.optimization_barrier((rising, falling, beside))
            if k <= ups:
                rising = lax.ppermute(rising, "batch", self.up)
                whole = lax.dynamic_update_index_in_dim(whole, rising, self.at(-k), 0)
            if k <= downs:
                falling = lax.ppermute(falling, "batch", self.down)
                whole = lax.dynamic_update_index_in_dim(whole, falling, self.at(k), 0)
        return whole, beside

    def scatter(self, blocks, longer_up):
        hops = Hops(self, blocks, longer_up)
        while not hops.done:
            hops.step()
        return hops.result()


class Hops:
    def __init__(self, ring, blocks, longer_up):
        self.ring, self.blocks, self.hop = ring, blocks, 0
        if ring.size > LONGEST_RING:
            self.sums = lax.psum_scatter(blocks, "batch", scatter_dimension=0, tiled=False)
            self.done = True
            return
        self.sums, self.done = None, False
        self.ups, self.downs = ring.steps(longer_up)
        self.rising, self.falling = self.own(self.ups), self.own(-self.downs)

    def own(self, offset):
        return lax.dynamic_index_in_dim(self.blocks, self.ring.at(offset), 0, keepdims=False)

    def step(self, later=None):
        if self.done:
            return later
        k = self.hop
        if k < self.ups:
            self.rising = lax.ppermute(self.rising, "batch", self.ring.up)
        if k < self.downs:
            self.falling = lax.ppermute(self.falling, "batch", self.ring.down)
        if later is not None:
            self.rising, self.falling, later = lax.optimization_barrier(
                (self.rising, self.falling, later)
            )
        if k < self.ups - 1:
            self.rising = self.rising + self.own(self.ups - 1 - k)
        if k < self.downs - 1:
            self.falling = self.falling + self.own(-(self.downs - 1 - k))
        self.hop += 1
        self.done = self.hop == max(self.ups, self.downs)
        return later

    def result(self):
        while not self.done:
            self.step()
        return self.sums if self.sums is not None else self.own(0) + self.rising + self.falling


def sums_of(values, others):
    return jnp.stack([jnp.sum(values, axis=0), jnp.sum(values * others, axis=0)])


def norm_forward(values, total, gain, bias, count):
    center = total[0] / count
    inverse = lax.rsqrt(total[1] / count - center * center + EPSILON)
    hat = (values - center) * inverse
    return hat, hat * gain + bias, inverse


def norm_backward(d_out, hat, inverse, gain, count, direct):
    sums = sum_batch(jnp.stack([jnp.sum(d_out * hat, axis=0), jnp.sum(d_out, axis=0)]), direct)
    d_values = inverse * gain * (d_out - sums[1] / count - hat * (sums[0] / count))
    return d_values, sums


def shards(
    features,
    reduce_weight,
    reduce_norm,
    dilate_weight,
    dilate_norm,
    expand_weight,
    expand_norm,
    depth_head,
    segment_head,
    normal_head,
    contour_head,
    depth_message,
    segment_message,
    normal_message,
    contour_message,
    depth_gate,
    segment_gate,
    classifier,
    depth_valid,
    labels,
    block_cotangent,
    depth_cotangent,
):
    row, batch = lax.axis_index("rows"), lax.axis_index("batch")
    nrows, nbatch = lax.axis_size("rows"), lax.axis_size("batch")
    ring = Ring(batch)
    _, local_height, breadth, wide = features.shape
    mid = reduce_weight.shape[1]
    part = mid // nrows
    quarter = local_height * breadth
    height = local_height * nrows
    pixels = quarter * nrows
    count = float(pixels * nbatch)
    factor = count ** (-0.5)
    classes = classifier.shape[1]
    held = dilate_weight.shape[0]
    grain = math.gcd(held, mid) // nrows
    groups = held // (nrows * grain)
    wide_held = wide // nbatch
    wide_part = wide_held // nrows
    mid_held = mid // nbatch

    def row_slice(array, dim):
        size = array.shape[dim] // nrows
        return lax.dynamic_slice_in_dim(array, row * size, size, dim)

    channel = jnp.arange(mid)
    slot = jnp.arange(part)
    mine = (slot // grain) * (nrows * grain) + row * grain + slot % grain
    pick = (channel[:, None] == mine[None, :]).astype(jnp.float32)
    split = jnp.arange(mid)
    natural = ((split % part) // grain) * (nrows * grain) + (split // part) * grain + split % grain
    mix = (natural[:, None] == channel[None, :]).astype(jnp.bfloat16)
    here = row.astype(jnp.int32).reshape(1)

    def to_narrow(array):
        return jnp.concatenate(
            [array[:, i * part : (i + 1) * part] for i in range(nrows)], axis=0
        )

    def from_narrow(array):
        size = array.shape[1] // nrows
        return jnp.concatenate([array[:, i * size : (i + 1) * size] for i in range(nrows)], axis=2)

    tiny_width = max(mid_held, wide_part)

    def tiny(array):
        return jnp.pad(array, ((0, 0), (0, tiny_width - array.shape[1])))

    heads_mine = jnp.concatenate(
        [
            product(head, pick, 1, 0, EXACT)
            for head in (segment_head, normal_head, depth_head, contour_head)
        ],
        axis=1,
    )
    heads_full = lax.all_gather(heads_mine, "batch", axis=0, tiled=True)

    def message_runs(array):
        runs = array.reshape(groups, nrows, grain, mid)
        return lax.dynamic_index_in_dim(runs, row, 1, keepdims=True)

    def message_pair(first, second):
        return jnp.concatenate([message_runs(first), message_runs(second)], axis=1)

    run = grain if grain % 8 == 0 else part
    segment_pair_mine = message_pair(segment_message, contour_message).reshape(held // 2, mid)
    depth_pair_mine = message_pair(depth_message, normal_message).reshape(held // 2, mid)
    segment_pair_w, depth_pair_w = [
        regroup(
            lax.all_gather(mine, "batch", axis=0, tiled=True).reshape(
                nbatch * groups, 2, grain, mid
            ),
            run,
        )
        for mine in (segment_pair_mine, depth_pair_mine)
    ]

    expand_norm_mine = lax.dynamic_index_in_dim(
        expand_norm.reshape(2, nrows, wide_part), row, 1, keepdims=False
    )
    params = jnp.concatenate([tiny(reduce_norm), tiny(dilate_norm), tiny(expand_norm_mine)], axis=0)
    params = jnp.pad(params, ((0, 2), (0, part - tiny_width)))
    expand_mine = lax.dynamic_index_in_dim(
        expand_weight.reshape(mid_held, nbatch, nrows, wide_part), row, 2, keepdims=False
    ).reshape(mid_held, nbatch * wide_part)
    class_lanes = -(-classes // part) * part

    def packed(pieces):
        spans, start = {}, 0
        for name, piece in pieces.items():
            spans[name] = slice(start, start + piece.shape[0])
            start += piece.shape[0]
        return jnp.concatenate(list(pieces.values()), axis=0), spans

    first_mine, first_spans = packed(
        {
            "reduce": to_narrow(row_slice(reduce_weight, 0)),
            "params": params,
            "dilate": row_slice(dilate_weight, 1),
        }
    )
    first_all, _ = ring.gather(first_mine, True)
    reduce_full = from_narrow(first_all[:, first_spans["reduce"]]).reshape(nbatch * wide_part, mid)
    params_all = first_all[:, first_spans["params"]]
    dilate_full = first_all[:, first_spans["dilate"]].reshape(nbatch * held, part)

    def all_params(pair, size):
        return jnp.transpose(params_all[:, pair : pair + 2, :size], (1, 0, 2)).reshape(2, nbatch * size)

    reduce_gain, reduce_bias = row_slice(all_params(0, mid_held), 1)
    dilate_gain, dilate_bias = row_slice(all_params(2, mid_held), 1)
    expand_gain, expand_bias = all_params(4, wide_part)

    spread_by_kernel = wide_part == 64 and part % 128 == 0

    def spread_wide(array):
        if spread_by_kernel:
            (blocks,) = single_call(
                spread_kernel, (here, array), [(nrows, quarter, wide // nrows)], [], 1
            )
            blocks = [blocks[key] for key in range(4)]
        else:
            split_blocks = jnp.transpose(array.reshape(quarter, nbatch, nrows, wide_part), (2, 0, 1, 3))
            split_blocks = split_blocks.reshape(nrows, quarter, nbatch * wide_part)
            blocks = [
                lax.dynamic_index_in_dim(split_blocks, row ^ key, 0, keepdims=False)
                for key in range(4)
            ]
        return jnp.concatenate(in_order(exchange_keyed(blocks), row), axis=0)

    def exchange_wide(array):
        blocks = array.reshape(nrows, quarter, nbatch * wide_part)
        return exchange_keyed(
            [lax.dynamic_index_in_dim(blocks, row ^ key, 0, keepdims=False) for key in range(4)]
        )

    def collect_wide(got):
        if spread_by_kernel:
            (out,) = single_call(
                collect_kernel,
                (here, *got),
                [(quarter, wide)],
                [(nrows, quarter, wide // nrows)],
                1,
            )
        else:
            out = jnp.stack(in_order(got, row)).reshape(nrows, quarter, nbatch, wide_part)
            out = jnp.transpose(out, (1, 2, 0, 3))
        return out.reshape(1, local_height, breadth, wide)

    def image_of(array):
        return array.reshape(height, breadth, array.shape[-1])

    features, _ = lax.optimization_barrier((features, (heads_mine, segment_pair_mine, first_mine)))
    inputs = spread_wide(features.reshape(quarter, wide))

    valid = depth_valid.astype(jnp.float32).reshape(quarter, 1)
    keep, give = single_call(
        split_product_kernel,
        (here, inputs, reduce_full, jnp.full((1, part), jnp.sum(valid))),
        [(2, pixels + 8, part)] * 2,
        [(pixels, mid)],
        2 * pixels * mid * mid,
    )
    mine_terms, got_terms = scatter_end(keep, give)
    pre_reduce = mine_terms + got_terms
    valid_row = pre_reduce[pixels]
    pre_reduce = pre_reduce[:pixels]
    total_one = sum_batch(jnp.concatenate([sums_of(pre_reduce, pre_reduce), valid_row[None]]))
    scale = valid * (count / total_one[2, 0])
    hat_one, normed_one, inverse_one = norm_forward(
        pre_reduce, total_one, reduce_gain, reduce_bias, count
    )
    pre_dilate, mid_in = joined_conv(
        here, gather_keyed(image_of(jax.nn.silu(normed_one))), dilate_full, 2
    )
    total_two = sum_batch(sums_of(pre_dilate, pre_dilate))
    total_two, heads_full = lax.optimization_barrier((total_two, heads_full))
    hat_two, normed_two, inverse_two = norm_forward(
        pre_dilate, total_two, dilate_gain, dilate_bias, count
    )

    beside = mid // class_lanes
    square_mine, square_spans = packed(
        {
            "depth_gate": depth_gate,
            "segment_gate": segment_gate,
            "expand": expand_mine,
            "classifier": jnp.pad(classifier, ((0, 0), (0, class_lanes - classes)))
            .reshape(beside, mid_held // beside, class_lanes)
            .transpose(1, 0, 2)
            .reshape(mid_held // beside, mid),
        }
    )
    square_mine, inverse_two = lax.optimization_barrier((square_mine, inverse_two))
    feats, mid_out, pairs = joined_conv(
        here, gather_keyed(image_of(jax.nn.silu(normed_two))), heads_full, 1, True
    )
    square_all, feats = ring.gather(square_mine, False, feats, 2)
    square_all, segment_pair_w = lax.optimization_barrier((square_all, segment_pair_w))
    depth_gate_w, segment_gate_w, expand_w = [
        square_all[:, square_spans[name]].reshape(mid, mid)
        for name in ("depth_gate", "segment_gate", "expand")
    ]
    classifier_w = (
        square_all[:, square_spans["classifier"]]
        .reshape(nbatch, mid_held // beside, beside, class_lanes)
        .transpose(0, 2, 1, 3)
        .reshape(mid, class_lanes)
    )
    feats_image = image_of(feats)

    segment_mine, segment_got = scatter_end(*note_forward(here, feats_image, 1, segment_pair_w))
    pairs_got = jnp.stack(exchange_keyed([pairs[key] for key in range(4)]))
    block_cotangent, _ = lax.optimization_barrier((block_cotangent, feats))
    cotangent = spread_wide(block_cotangent.reshape(quarter, wide))
    pairs_got, segment_mine, cotangent = lax.optimization_barrier((pairs_got, segment_mine, cotangent))
    depth_cotangent = depth_cotangent.reshape(quarter, mid)
    both, one_map = (2 * quarter, mid), (quarter, mid)
    feat_pair, open_pair, d_depth_note = single_call(
        gates_kernel,
        (here, pairs_got, mix, depth_gate_w, segment_gate_w, depth_cotangent, scale),
        [both, both, one_map],
        [both],
        8 * quarter * mid * mid,
    )

    def segment_body(*refs):
        segment_kernel(classes, *refs)

    segment_stream, d_segment_note, direct_segment, segment_gate_grad, classifier_grad = single_call(
        segment_body,
        (
            here,
            segment_mine,
            segment_got,
            feat_pair[quarter:],
            open_pair[quarter:],
            labels.reshape(quarter, 1),
            classifier_w,
            segment_gate_w,
            mix,
        ),
        [one_map, one_map, (4, quarter, part), (mid, mid), (mid, class_lanes)],
        [one_map],
        8 * quarter * mid * mid,
    )

    def lines(array):
        return array.reshape(local_height, breadth, mid)

    d_depth_blocks, d_segment_note = lax.optimization_barrier(
        (gather_keyed(lines(d_depth_note)), d_segment_note)
    )
    message_grads, d_depth_image = note_grad(here, feats, 0, d_depth_blocks, run)
    message_grads, d_segment_image = note_grad(
        here, feats, 1, gather_keyed(lines(d_segment_note)), run, message_grads
    )
    message_sums = lax.psum_scatter(
        regroup(message_grads, grain).reshape(-1, mid), "batch", scatter_dimension=0, tiled=True
    )
    segment_back = note_back(d_segment_image, segment_pair_w)
    depth_mine, depth_got = scatter_end(*note_forward(here, feats_image, 0, depth_pair_w))
    depth_back = note_back(d_depth_image, depth_pair_w)
    depth_stream, direct_both, depth_gate_grad = single_call(
        depth_kernel,
        (
            here,
            depth_mine,
            depth_got,
            feat_pair[:quarter],
            open_pair[:quarter],
            depth_cotangent,
            scale,
            depth_gate_w,
            mix,
            direct_segment,
        ),
        [one_map, (4, 2 * quarter, part), (mid, mid)],
        [one_map],
        8 * quarter * mid * mid,
    )
    direct_got = jnp.stack(exchange_keyed([direct_both[key] for key in range(4)]))
    flat_mid_out = mid_out.reshape(pixels, mid)
    heads_grad, d_feats = heads_grad_of(
        here,
        flat_mid_out,
        image_of(depth_back),
        image_of(segment_back),
        direct_got.reshape(4, 2 * local_height, breadth, part),
    )
    heads_sums = lax.psum_scatter(heads_grad, "batch", scatter_dimension=0, tiled=True)

    pre_expand = product(flat_mid_out, expand_w, 1, 0)
    hat_three, normed_three, inverse_three = norm_forward(
        pre_expand, sum_batch(sums_of(pre_expand, pre_expand)), expand_gain, expand_bias, count
    )
    summed = normed_three + inputs
    block_blocks = exchange_wide(jax.nn.silu(summed))
    d_summed = cotangent * silu_grad(summed)
    d_pre_expand, expand_sums = norm_backward(
        d_summed, hat_three, inverse_three, expand_gain, count, False
    )

    expand_grad = product(flat_mid_out, d_pre_expand, 0, 0).reshape(nbatch, mid_held, mid)

    gate_terms = jnp.stack(
        [
            depth_gate_grad,
            segment_gate_grad,
            jnp.pad(classifier_grad, ((0, 0), (0, mid - class_lanes))),
        ]
    )
    gate_rows = mid_held // nrows
    gate_terms = jnp.transpose(gate_terms.reshape(3, nbatch, nrows, gate_rows, mid), (2, 1, 0, 3, 4))
    gate_sums = scatter_rows(gate_terms, row).reshape(nbatch, 3 * gate_rows, mid)

    keep, give = conv_back(here, d_feats, heads_full, 1)
    keep, give = single_call(
        expand_back_kernel,
        (here, d_pre_expand, expand_w, keep, give),
        [(2, pixels, part)] * 2,
        [(pixels, mid)],
        2 * pixels * mid * mid,
    )
    mine_terms, got_terms = scatter_end(keep, give)
    mine_terms, block_blocks = lax.optimization_barrier((mine_terms, block_blocks))
    block_out = collect_wide(block_blocks)
    d_pre_dilate, dilate_sums = norm_backward(
        (mine_terms + got_terms) * silu_grad(normed_two), hat_two, inverse_two, dilate_gain, count, False
    )
    d_dilate_image = image_of(d_pre_dilate)
    mine_terms, got_terms = scatter_end(*conv_back(here, d_dilate_image, dilate_full, 2))
    d_pre_reduce, reduce_sums = norm_backward(
        (mine_terms + got_terms) * silu_grad(normed_one), hat_one, inverse_one, reduce_gain, count, False
    )
    d_pre_reduce, message_sums = lax.optimization_barrier((d_pre_reduce, message_sums))
    reduce_grad, features_back = single_call(
        reduce_back_kernel,
        (here, *gather_keyed(d_pre_reduce), inputs, reduce_full, d_summed),
        [(mid, mid), (pixels, mid)],
        [(pixels, mid)],
        4 * pixels * mid * mid,
    )
    dilate_grad = conv_grad(mid_in.reshape(pixels, mid), d_dilate_image, 2).reshape(
        nbatch, held, part
    )
    narrow = held // nrows
    square_grad = jnp.concatenate(
        [
            jnp.concatenate(
                [dilate_grad[:, i * narrow : (i + 1) * narrow] for i in range(nrows)], axis=2
            ),
            expand_grad,
            gate_sums,
            reduce_grad.reshape(nbatch, wide_part, mid),
        ],
        axis=1,
    )
    square_grad, reduce_sums = lax.optimization_barrier((square_grad, reduce_sums))
    hops = Hops(ring, square_grad, False)
    hops.step()
    hops.step()
    message_blocks = hops.step(gather_keyed(message_sums * factor))
    features_blocks = hops.step(exchange_wide(features_back))
    square_sums = hops.result()
    features_grad = collect_wide(features_blocks)

    messages_out = jnp.stack(in_order(message_blocks, row)).reshape(
        nrows, groups, 4, grain, mid
    )

    def message_out(index):
        return jnp.transpose(messages_out[:, :, index], (1, 0, 2, 3)).reshape(held, mid)

    expand_mine_sums = lax.dynamic_slice_in_dim(expand_sums, batch * wide_part, wide_part, 1)
    norm_sums = jnp.concatenate(
        [
            jnp.pad(sums, ((0, 0), (0, mid - sums.shape[1])))
            for sums in (reduce_sums, dilate_sums, expand_mine_sums)
        ],
        axis=0,
    )
    small = jnp.concatenate([square_sums, jnp.pad(norm_sums, ((0, 2), (0, 0)))], axis=0) * factor
    small_blocks = gather_keyed(small)
    heads_sums, small_blocks = lax.optimization_barrier((heads_sums, small_blocks))
    small_got = in_order(small_blocks, row)
    segment_out, normal_out, depth_out, contour_out = single_call(
        heads_out_kernel,
        (here, *gather_keyed(heads_sums * factor), mix),
        [(held, mid)] * 4,
        [(held, mid)],
        8 * held * mid * mid,
    )

    squares_got = jnp.stack([block[narrow : narrow + mid_held + 3 * gate_rows] for block in small_got])
    dilate_out = jnp.concatenate(
        [
            jnp.concatenate(
                [block[:narrow, i * part : (i + 1) * part] for i in range(nrows)], axis=0
            )
            for block in small_got
        ],
        axis=1,
    )
    expand_out = jnp.transpose(
        squares_got[:, :mid_held].reshape(nrows, mid_held, nbatch, wide_part), (1, 2, 0, 3)
    ).reshape(mid_held, wide)

    def gate_out(index):
        start = mid_held + index * gate_rows
        return squares_got[:, start : start + gate_rows].reshape(mid_held, mid)

    norms_got = [block[-8:] for block in small_got]

    def norm_out(start):
        full = jnp.concatenate([block[start : start + 2, :part] for block in norms_got], axis=1)
        return lax.dynamic_slice_in_dim(full, batch * mid_held, mid_held, 1)

    expand_norm_out = jnp.concatenate([block[4:6, :wide_part] for block in norms_got], axis=1)
    reduce_start = narrow + mid_held + 3 * gate_rows
    reduce_got = jnp.concatenate(
        [block[reduce_start : reduce_start + wide_part] for block in small_got], axis=0
    )

    return (
        block_out,
        depth_stream.reshape(1, local_height, breadth, mid),
        segment_stream.reshape(1, local_height, breadth, mid),
        features_grad,
        reduce_got,
        norm_out(0),
        dilate_out,
        norm_out(2),
        expand_out,
        expand_norm_out,
        depth_out,
        segment_out,
        normal_out,
        contour_out,
        message_out(0),
        message_out(2),
        message_out(1),
        message_out(3),
        gate_out(0),
        gate_out(1),
        gate_out(2)[:, :classes],
    )


def solution(mesh):
    pixels = P("batch", "rows", None, None)
    plane = P("batch", "rows", None)
    weight = P("batch", None)
    norm = P(None, "batch")
    in_specs = (
        (pixels, weight, norm, weight, norm, weight, norm) + (weight,) * 11 + (plane, plane, pixels, pixels)
    )
    out_specs = (pixels,) * 4 + (weight, norm) * 3 + (weight,) * 11
    return jax.shard_map(shards, mesh=mesh, in_specs=in_specs, out_specs=out_specs, check_vma=False)
```

```python
import math

import jax
import jax.numpy as jnp
from jax import lax
from jax.experimental import pallas as pl
from jax.experimental.pallas import tpu as pltpu
from jax.sharding import PartitionSpec as P

EPSILON = 1e-05
EXACT = lax.Precision.HIGHEST
FINE = lax.Precision.HIGH
LONGEST_RING = 8
LANES = 128


def product(left, right, left_dim, right_dim, precision=FINE):
    return lax.dot_general(
        left,
        right,
        (((left_dim,), (right_dim,)), ((), ())),
        precision=precision,
        preferred_element_type=jnp.float32,
    )


def halves(values):
    high = values.astype(jnp.bfloat16)
    return high, (values - high.astype(jnp.float32)).astype(jnp.bfloat16)


def three_pass(left, right, left_dim, right_dim):
    dims = (((left_dim,), (right_dim,)), ((), ()))

    def one(a, b):
        return lax.dot_general(a, b, dims, preferred_element_type=jnp.float32)

    return one(left[0], right[0]) + (one(left[0], right[1]) + one(left[1], right[0]))


def frame(image_ref, framed, dilation):
    height, breadth, depth = image_ref.shape
    edge = jnp.zeros((3, dilation, breadth, depth), jnp.float32)
    framed[:, :dilation] = edge
    framed[:, dilation + height :] = edge
    image = image_ref[...]
    side = jnp.zeros((height, dilation, depth), jnp.float32)
    inner = slice(dilation, dilation + height)
    framed[1, inner] = image
    framed[0, inner, dilation:, :] = image[:, : breadth - dilation]
    framed[0, inner, :dilation, :] = side
    framed[2, inner, : breadth - dilation, :] = image[:, dilation:]
    framed[2, inner, breadth - dilation :, :] = side


def shifted(framed, tap, height, dilation):
    block = framed[tap % 3, pl.ds((tap // 3) * dilation, height)]
    return block.reshape(height * block.shape[1], block.shape[2])


def exact_pick(values, choice, choice_dim):
    high = values.astype(jnp.bfloat16)
    rest = values - high.astype(jnp.float32)
    middle = rest.astype(jnp.bfloat16)
    low = (rest - middle.astype(jnp.float32)).astype(jnp.bfloat16)
    dims = (((1,), (choice_dim,)), ((), ()))

    def one(part):
        return lax.dot_general(part, choice, dims, preferred_element_type=jnp.float32)

    return one(high) + (one(middle) + one(low))


def at_lanes(index, size):
    return pl.ds(pl.multiple_of(index * size, size), size)


def keep_and_give(row, load, keep_ref, give_ref):
    core, side = row & 1, row >> 1
    for k in range(2):
        base = (side ^ k) * 2
        keep_ref[k] = load(base + core)
        give_ref[k] = load(base + 1 - core)


def joined_conv_kernel(dilation, row_ref, one, two, three, four, weight_ref, out_ref, image_ref, framed):
    tap = pl.program_id(0)

    @pl.when(tap == 0)
    def _():
        part = one.shape[2]
        for key, block in enumerate((one, two, three, four)):
            image_ref[:, :, at_lanes(row_ref[0] ^ key, part)] = block[...]
        frame(image_ref, framed, dilation)
        out_ref[...] = jnp.zeros_like(out_ref)

    moved = halves(shifted(framed, tap, image_ref.shape[0], dilation))
    out_ref[...] += three_pass(moved, halves(weight_ref[...]), 1, 0)


def heads_kernel(
    row_ref, one, two, three, four, weight_ref, out_ref, image_ref, pairs_ref, framed
):
    joined_conv_kernel(1, row_ref, one, two, three, four, weight_ref, out_ref, image_ref, framed)

    @pl.when(pl.program_id(0) == 8)
    def _():
        _, double, part = pairs_ref.shape
        quarter = double // 2
        for key in range(4):
            rows = pl.ds((row_ref[0] ^ key) * quarter, quarter)
            pairs_ref[key, :quarter] = out_ref[rows, 2 * part : 3 * part]
            pairs_ref[key, quarter:] = out_ref[rows, :part]


def split_product_kernel(row_ref, left_ref, right_ref, extra_ref, keep_ref, give_ref, total):
    total[...] = three_pass(halves(left_ref[...]), halves(right_ref[...]), 1, 0)
    pixels, part = left_ref.shape[0], keep_ref.shape[2]
    keep_and_give(
        row_ref[0],
        lambda j: total[:, at_lanes(j, part)],
        keep_ref.at[:, :pixels],
        give_ref.at[:, :pixels],
    )
    for ref in (keep_ref, give_ref):
        ref[:, pixels:] = jnp.broadcast_to(extra_ref[...], (2, 8, part))


def conv_back_kernel(dilation, row_ref, image_ref, weight_ref, keep_ref, give_ref, framed, total):
    tap = pl.program_id(0)

    @pl.when(tap == 0)
    def _():
        frame(image_ref, framed, dilation)
        total[...] = jnp.zeros_like(total)

    moved = halves(shifted(framed, 8 - tap, image_ref.shape[0], dilation))
    total[...] += three_pass(moved, halves(weight_ref[...]), 1, 1)

    @pl.when(tap == 8)
    def _():
        part = keep_ref.shape[2]
        keep_and_give(row_ref[0], lambda j: total[:, at_lanes(j, part)], keep_ref, give_ref)


def expand_back_kernel(
    row_ref, left_ref, right_ref, keep_in_ref, give_in_ref, keep_ref, give_ref, total
):
    total[...] = three_pass(halves(left_ref[...]), halves(right_ref[...]), 1, 1)
    part = keep_ref.shape[2]
    keep_and_give(row_ref[0], lambda j: total[:, at_lanes(j, part)], keep_ref, give_ref)
    keep_ref[...] += keep_in_ref[...]
    give_ref[...] += give_in_ref[...]


def conv_grad_kernel(dilation, input_ref, grad_ref, out_ref, framed, high, low):
    tap = pl.program_id(0)

    @pl.when(tap == 0)
    def _():
        frame(grad_ref, framed, dilation)
        high[...], low[...] = halves(jnp.transpose(input_ref[...]))

    moved = halves(shifted(framed, 8 - tap, grad_ref.shape[0], dilation))
    out_ref[...] = three_pass((high[...], low[...]), moved, 1, 0)


def heads_grad_kernel(
    row_ref, input_ref, first_ref, second_ref, direct_ref, out_ref, image_ref, framed, high, low
):
    tap = pl.program_id(0)

    @pl.when(tap == 0)
    def _():
        lanes = first_ref.shape[2]
        _, double, breadth, part = direct_ref.shape
        lines = double // 2
        image_ref[:, :, :lanes] = first_ref[...]
        image_ref[:, :, lanes:] = second_ref[...]
        for key in range(4):
            rows = pl.ds((row_ref[0] ^ key) * lines, lines)
            image_ref[rows, :, :part] += direct_ref[key, :lines]
            image_ref[rows, :, lanes : lanes + part] += direct_ref[key, lines:]

    conv_grad_kernel(1, input_ref, image_ref, out_ref, framed, high, low)


def source_rows(weight):
    return jnp.concatenate(
        [weight[:, k].reshape(-1, weight.shape[-1]) for k in range(weight.shape[1])], axis=0
    )


def note_kernel(row_ref, image_ref, weight_ref, keep_ref, give_ref, framed, total):
    tap = pl.program_id(0)

    @pl.when(tap == 0)
    def _():
        frame(image_ref, framed, 1)
        total[...] = jnp.zeros_like(total)

    moved = shifted(framed, tap, image_ref.shape[0], 1)
    total[...] += three_pass(halves(moved), halves(source_rows(weight_ref[...])), 1, 0)

    @pl.when(tap == 8)
    def _():
        quarter = keep_ref.shape[1]
        keep_and_give(
            row_ref[0], lambda j: total[pl.ds(j * quarter, quarter), :], keep_ref, give_ref
        )


def note_back_kernel(note_ref, weight_ref, out_ref, framed):
    tap = pl.program_id(0)

    @pl.when(tap == 0)
    def _():
        frame(note_ref, framed, 1)
        out_ref[...] = jnp.zeros_like(out_ref)

    moved = halves(shifted(framed, 8 - tap, note_ref.shape[0], 1))
    out_ref[...] += three_pass(moved, halves(source_rows(weight_ref[...])), 1, 1)


def note_grad_kernel(row_ref, input_ref, one, two, three, four, *rest):
    out_ref, image_ref, framed, high, low = rest[-5:]
    tap = pl.program_id(0)

    @pl.when(tap == 0)
    def _():
        lines = one.shape[0]
        for key, block in enumerate((one, two, three, four)):
            image_ref[pl.ds((row_ref[0] ^ key) * lines, lines)] = block[...]
        frame(image_ref, framed, 1)
        high[...], low[...] = halves(jnp.transpose(input_ref[...]))

    moved = halves(shifted(framed, 8 - tap, image_ref.shape[0], 1))
    grad = three_pass((high[...], low[...]), moved, 1, 0)
    runs, _, grain, mid = out_ref.shape
    part = grad.shape[0] // 2
    for k in range(2):
        out_ref[:, k] = grad[k * part : (k + 1) * part].reshape(runs, grain, mid)


def gates_kernel(
    row_ref, pairs_ref, mix_ref, depth_gate_ref, segment_gate_ref, cotangent_ref, scale_ref,
    feat_ref, open_ref, d_note_ref, joined,
):
    _, double, part = pairs_ref.shape
    quarter = double // 2
    for key in range(4):
        joined[:, at_lanes(row_ref[0] ^ key, part)] = pairs_ref[key]
    feat = exact_pick(joined[...], mix_ref[...], 0)
    feat_ref[...] = feat
    for index, gate_ref in enumerate((depth_gate_ref, segment_gate_ref)):
        rows = slice(index * quarter, (index + 1) * quarter)
        gate = three_pass(halves(feat[rows]), halves(gate_ref[...]), 1, 0)
        open_ref[rows] = jax.nn.sigmoid(gate)
    d_note_ref[...] = cotangent_ref[...] * scale_ref[...] * open_ref[:quarter]


def gate_back(row_ref, feat, opened, note, d_stream, d_note, gate_ref, mix_ref, gate_grad_ref, joined):
    d_pre = halves(d_note * note * (1.0 - opened))
    gate_grad_ref[...] = three_pass(halves(jnp.transpose(feat)), d_pre, 1, 0)
    direct = d_stream + three_pass(d_pre, halves(gate_ref[...]), 1, 1)
    joined[...] = exact_pick(direct, mix_ref[...], 1)


def segment_kernel(
    classes, row_ref, mine_ref, got_ref, feat_ref, open_ref, labels_ref, classifier_ref, gate_ref, mix_ref,
    stream_ref, d_note_ref, direct_ref, gate_grad_ref, classifier_grad_ref, joined,
):
    note = mine_ref[...] + got_ref[...]
    feat, opened = feat_ref[...], open_ref[...]
    stream = feat + opened * note
    stream_ref[...] = stream
    weight = halves(classifier_ref[...])
    logits = three_pass(halves(stream), weight, 1, 0)
    lane = lax.broadcasted_iota(jnp.int32, logits.shape, 1)
    real = lane < classes
    top = jnp.max(jnp.where(real, logits, -3e38), axis=1, keepdims=True)
    powers = jnp.where(real, jnp.exp(jnp.where(real, logits - top, 0.0)), 0.0)
    onehot = jnp.where(lane == labels_ref[...], 1.0, 0.0)
    d_logits = powers / jnp.sum(powers, axis=1, keepdims=True) - onehot
    d_stream = three_pass(halves(d_logits), weight, 1, 1)
    d_note = d_stream * opened
    d_note_ref[...] = d_note
    classifier_grad_ref[...] = three_pass(halves(jnp.transpose(stream)), halves(d_logits), 1, 0)
    gate_back(row_ref, feat, opened, note, d_stream, d_note, gate_ref, mix_ref, gate_grad_ref, joined)
    part = direct_ref.shape[2]
    for key in range(4):
        direct_ref[key] = joined[:, at_lanes(row_ref[0] ^ key, part)]


def depth_kernel(
    row_ref, mine_ref, got_ref, feat_ref, open_ref, cotangent_ref, scale_ref, gate_ref, mix_ref, other_ref,
    stream_ref, direct_ref, gate_grad_ref, joined,
):
    note = mine_ref[...] + got_ref[...]
    feat, opened = feat_ref[...], open_ref[...]
    stream_ref[...] = feat + opened * note
    d_stream = cotangent_ref[...] * scale_ref[...]
    gate_back(
        row_ref, feat, opened, note, d_stream, d_stream * opened, gate_ref, mix_ref, gate_grad_ref, joined
    )
    _, double, part = direct_ref.shape
    quarter = double // 2
    for key in range(4):
        direct_ref[key, :quarter] = other_ref[key]
        direct_ref[key, quarter:] = joined[:, at_lanes(row_ref[0] ^ key, part)]


def reduce_back_kernel(
    row_ref, one, two, three, four, input_ref, weight_ref, d_summed_ref, grad_ref, out_ref, joined
):
    part = one.shape[1]
    for key, block in enumerate((one, two, three, four)):
        joined[:, at_lanes(row_ref[0] ^ key, part)] = block[...]
    d_pre = halves(joined[...])
    grad_ref[...] = three_pass(halves(jnp.transpose(input_ref[...])), d_pre, 1, 0)
    out_ref[...] = d_summed_ref[...] + three_pass(d_pre, halves(weight_ref[...]), 1, 1)


def heads_out_kernel(row_ref, one, two, three, four, mix_ref, *rest):
    outs, joined = rest[:-1], rest[-1]
    part = joined.shape[1] // 4
    for index, out_ref in enumerate(outs):
        lanes = slice(index * part, (index + 1) * part)
        for key, block in enumerate((one, two, three, four)):
            joined[:, at_lanes(row_ref[0] ^ key, part)] = block[:, lanes]
        out_ref[...] = exact_pick(joined[...], mix_ref[...], 0)


def spread_kernel(row_ref, array_ref, out_ref):
    low = lax.broadcasted_iota(jnp.int32, (array_ref.shape[0], 128), 1) < 64
    for device in range(4):
        key = row_ref[0] ^ device
        for k in range(out_ref.shape[2] // 128):
            start = 512 * k + 128 * (device // 2)
            even = array_ref[:, start : start + 128]
            odd = array_ref[:, start + 256 : start + 384]
            if device % 2:
                block = jnp.where(low, pltpu.roll(even, 64, 1), odd)
            else:
                block = jnp.where(low, even, pltpu.roll(odd, 64, 1))
            out_ref[key, :, 128 * k : 128 * (k + 1)] = block


def collect_kernel(row_ref, one, two, three, four, out_ref, ordered):
    for key, block in enumerate((one, two, three, four)):
        ordered[row_ref[0] ^ key] = block[...]
    low = lax.broadcasted_iota(jnp.int32, (one.shape[0], 128), 1) < 64
    for k in range(one.shape[1] // 128):
        for pair in range(2):
            first = ordered[2 * pair, :, 128 * k : 128 * (k + 1)]
            second = ordered[2 * pair + 1, :, 128 * k : 128 * (k + 1)]
            start = 512 * k + 128 * pair
            out_ref[:, start : start + 128] = jnp.where(low, first, pltpu.roll(second, 64, 1))
            out_ref[:, start + 256 : start + 384] = jnp.where(low, pltpu.roll(first, 64, 1), second)


def regroup(array, run):
    runs, sources, grain, mid = array.shape
    if grain == run:
        return array
    if run > grain:
        lists = array.reshape(-1, run // grain, sources, grain, mid)
        return jnp.transpose(lists, (0, 2, 1, 3, 4)).reshape(-1, sources, run, mid)
    parts = array.reshape(runs, sources, grain // run, run, mid)
    return jnp.transpose(parts, (0, 2, 1, 3, 4)).reshape(-1, sources, run, mid)


VMEM_LIMIT = 56 * 2**20
SCALAR = pl.BlockSpec(memory_space=pltpu.SMEM)


def kernel_call(body, grid, in_specs, out_specs, out_shape, scratch, flops):
    return pl.pallas_call(
        body,
        grid=grid,
        in_specs=in_specs,
        out_specs=out_specs,
        out_shape=out_shape,
        scratch_shapes=scratch,
        compiler_params=pltpu.CompilerParams(
            dimension_semantics=("arbitrary",) * len(grid), vmem_limit_bytes=VMEM_LIMIT
        ),
        cost_estimate=pl.CostEstimate(flops=3 * flops, bytes_accessed=12 * 2**20, transcendentals=0),
    )


def single_call(body, args, outs, scratch, flops):
    return kernel_call(
        body,
        (1,),
        [SCALAR] + [whole_spec(arg.shape) for arg in args[1:]],
        [whole_spec(out) for out in outs],
        [jax.ShapeDtypeStruct(out, jnp.float32) for out in outs],
        [pltpu.VMEM(shape, jnp.float32) for shape in scratch],
        flops,
    )(*args)


def framed_scratch(image, dilation):
    height, breadth, depth = image
    return pltpu.VMEM((3, height + 2 * dilation, breadth, depth), jnp.float32)


def whole_spec(shape):
    return pl.BlockSpec(shape, lambda *_: (0,) * len(shape))


def struct(shape):
    return jax.ShapeDtypeStruct(shape, jnp.float32)


def tap_rows(rows, cols):
    return pl.BlockSpec((rows, cols), lambda tap: (tap, 0))


def tap_runs(weight_shape):
    return pl.BlockSpec((weight_shape[0] // 9,) + weight_shape[1:], lambda tap: (tap, 0, 0, 0))


def joined_conv(row, blocks, weight, dilation, with_pairs=False):
    height, breadth, part = blocks[0].shape
    image = (height, breadth, 4 * part)
    rows, cols = weight.shape[0] // 9, weight.shape[1]
    shapes = [(height * breadth, cols), image]
    if with_pairs:
        body = heads_kernel
        shapes.append((4, height * breadth // 2, part))
    else:

        def body(*refs):
            joined_conv_kernel(dilation, *refs)

    return kernel_call(
        body,
        (9,),
        [SCALAR] + [whole_spec(blocks[0].shape)] * 4 + [tap_rows(rows, cols)],
        [whole_spec(shape) for shape in shapes],
        [struct(shape) for shape in shapes],
        [framed_scratch(image, dilation)],
        2 * 9 * height * breadth * rows * cols,
    )(row, *blocks, weight)


def conv_back(row, image, weight, dilation):
    height, breadth, _ = image.shape
    rows, cols = weight.shape[0] // 9, weight.shape[1]
    pixels = height * breadth
    shape = (2, pixels, rows // 4)

    def body(*refs):
        conv_back_kernel(dilation, *refs)

    return kernel_call(
        body,
        (9,),
        [SCALAR, whole_spec(image.shape), tap_rows(rows, cols)],
        [whole_spec(shape)] * 2,
        [struct(shape)] * 2,
        [framed_scratch(image.shape, dilation), pltpu.VMEM((pixels, rows), jnp.float32)],
        2 * 9 * pixels * rows * cols,
    )(row, image, weight)


def conv_grad(flat_input, image_grad, dilation):
    pixels, depth = flat_input.shape
    cols = image_grad.shape[2]

    def body(*refs):
        conv_grad_kernel(dilation, *refs)

    return kernel_call(
        body,
        (9,),
        [whole_spec(flat_input.shape), whole_spec(image_grad.shape)],
        tap_rows(depth, cols),
        struct((9 * depth, cols)),
        [framed_scratch(image_grad.shape, dilation)]
        + [pltpu.VMEM((depth, pixels), jnp.bfloat16)] * 2,
        2 * 9 * pixels * depth * cols,
    )(flat_input, image_grad)


def heads_grad_of(row, flat_input, first, second, direct):
    pixels, depth = flat_input.shape
    height, breadth, lanes = first.shape
    image = (height, breadth, 2 * lanes)
    return kernel_call(
        heads_grad_kernel,
        (9,),
        [SCALAR] + [whole_spec(array.shape) for array in (flat_input, first, second, direct)],
        [tap_rows(depth, 2 * lanes), whole_spec(image)],
        [struct((9 * depth, 2 * lanes)), struct(image)],
        [framed_scratch(image, 1)] + [pltpu.VMEM((depth, pixels), jnp.bfloat16)] * 2,
        2 * 9 * pixels * depth * 2 * lanes,
    )(row, flat_input, first, second, direct)


def note_forward(row, image, pair, weight):
    height, breadth, depth = image.shape
    depth = depth // 2
    mid = weight.shape[3]
    pixels = height * breadth
    shape = (2, pixels // 4, mid)
    return kernel_call(
        note_kernel,
        (9,),
        [
            SCALAR,
            pl.BlockSpec((height, breadth, depth), lambda tap: (0, 0, pair)),
            tap_runs(weight.shape),
        ],
        [whole_spec(shape)] * 2,
        [struct(shape)] * 2,
        [framed_scratch((height, breadth, depth), 1), pltpu.VMEM((pixels, mid), jnp.float32)],
        2 * 9 * pixels * depth * mid,
    )(row, image, weight)


def note_back(note, weight):
    height, breadth, mid = note.shape
    shape = (height * breadth, weight.shape[0] // 9 * weight.shape[1] * weight.shape[2])
    return kernel_call(
        note_back_kernel,
        (9,),
        [whole_spec(note.shape), tap_runs(weight.shape)],
        whole_spec(shape),
        struct(shape),
        [framed_scratch(note.shape, 1)],
        2 * 9 * shape[0] * shape[1] * mid,
    )(note, weight)


def note_grad(row, flat_input, pair, blocks, grain, grads=None):
    pixels, depth = flat_input.shape
    depth = depth // 2
    lines, breadth, mid = blocks[0].shape
    image = (4 * lines, breadth, mid)
    runs = depth // 2 // grain
    shape = (9 * runs, 4, grain, mid)
    others = [] if grads is None else [grads]
    return pl.pallas_call(
        note_grad_kernel,
        grid=(9,),
        in_specs=[SCALAR, pl.BlockSpec((pixels, depth), lambda tap: (0, pair))]
        + [whole_spec(blocks[0].shape)] * 4
        + [pl.BlockSpec(memory_space=pl.ANY)] * len(others),
        out_specs=[
            pl.BlockSpec((runs, 2, grain, mid), lambda tap: (tap, pair, 0, 0)),
            whole_spec(image),
        ],
        out_shape=[struct(shape), struct(image)],
        scratch_shapes=[framed_scratch(image, 1)] + [pltpu.VMEM((depth, pixels), jnp.bfloat16)] * 2,
        input_output_aliases={6: 0} if others else {},
        compiler_params=pltpu.CompilerParams(
            dimension_semantics=("arbitrary",), vmem_limit_bytes=VMEM_LIMIT
        ),
        cost_estimate=pl.CostEstimate(
            flops=6 * 9 * pixels * depth * mid, bytes_accessed=12 * 2**20, transcendentals=0
        ),
    )(row, flat_input, *blocks, *others)


def silu_grad(values):
    gate_val = jax.nn.sigmoid(values)
    return gate_val * (1.0 + values * (1.0 - gate_val))


def swap_rows(block, mask):
    size = lax.axis_size("rows")
    return lax.ppermute(block, "rows", [(i, i ^ mask) for i in range(size)])


def in_order(blocks, row):
    count = len(blocks)
    if count == 1:
        return blocks
    half = count // 2
    near = in_order(blocks[:half], row)
    far = in_order(blocks[half:], row)
    upper = (row & half) != 0
    first = [jnp.where(upper, f, n) for n, f in zip(near, far)]
    second = [jnp.where(upper, n, f) for n, f in zip(near, far)]
    return first + second


def gather_keyed(block):
    far = swap_rows(block, 2)
    return [block, swap_rows(block, 1), far, swap_rows(far, 1)]


def gather_rows(block, row):
    return in_order(gather_keyed(block), row)


def scatter_end(keep, give):
    got = swap_rows(give, 1)
    other = keep[1] + got[1]
    return keep[0] + got[0], swap_rows(other, 2)


def scatter_rows(blocks, row):
    core, side = row & 1, row >> 1
    pairs = blocks.reshape((2, 2) + blocks.shape[1:])
    keep = lax.dynamic_index_in_dim(pairs, core, 1, keepdims=False)
    got = keep + swap_rows(lax.dynamic_index_in_dim(pairs, 1 - core, 1, keepdims=False), 1)
    mine = lax.dynamic_index_in_dim(got, side, 0, keepdims=False)
    return mine + swap_rows(lax.dynamic_index_in_dim(got, 1 - side, 0, keepdims=False), 2)


def exchange_keyed(blocks):
    return [blocks[0]] + [swap_rows(blocks[mask], mask) for mask in range(1, 4)]


def sum_batch(values, direct=False):
    size = lax.axis_size("batch")
    if size & (size - 1):
        return lax.psum(values, "batch")

    def swap(block, mask):
        return lax.ppermute(block, "batch", [(i, i ^ mask) for i in range(size)])

    if direct and size <= LONGEST_RING:
        return values + sum(swap(values, mask) for mask in range(1, size))
    mask = 1
    while mask < size:
        values = values + swap(values, mask)
        mask *= 2
    return values


class Ring:
    def __init__(self, batch):
        size = lax.axis_size("batch")
        self.batch, self.size = batch, size
        self.order = list(range(0, size, 2)) + [i for i in reversed(range(size)) if i % 2]
        self.place = {b: p for p, b in enumerate(self.order)}
        self.up = [(self.order[p], self.order[(p + 1) % size]) for p in range(size)]
        self.down = [(b, a) for a, b in self.up]
        table = [[self.order[(self.place[b] + k) % size] for k in range(size)] for b in range(size)]
        self.row = jnp.array(table, jnp.int32)[batch]

    def at(self, offset):
        return self.row[offset % self.size]

    def steps(self, longer_up):
        more = self.size // 2
        less = self.size - 1 - more
        return (more, less) if longer_up else (less, more)

    def gather(self, block, longer_up, beside=None, beside_step=0):
        if self.size > LONGEST_RING:
            return lax.all_gather(block, "batch", axis=0, tiled=False), beside
        whole = jnp.zeros((self.size,) + block.shape, block.dtype)
        whole = lax.dynamic_update_index_in_dim(whole, block, self.batch, 0)
        ups, downs = self.steps(longer_up)
        rising = falling = block
        for k in range(1, max(ups, downs) + 1):
            if k == beside_step and beside is not None:
                rising, falling, beside = lax.optimization_barrier((rising, falling, beside))
            if k <= ups:
                rising = lax.ppermute(rising, "batch", self.up)
                whole = lax.dynamic_update_index_in_dim(whole, rising, self.at(-k), 0)
            if k <= downs:
                falling = lax.ppermute(falling, "batch", self.down)
                whole = lax.dynamic_update_index_in_dim(whole, falling, self.at(k), 0)
        return whole, beside

    def scatter(self, blocks, longer_up):
        hops = Hops(self, blocks, longer_up)
        while not hops.done:
            hops.step()
        return hops.result()


class Hops:
    def __init__(self, ring, blocks, longer_up):
        self.ring, self.blocks, self.hop = ring, blocks, 0
        if ring.size > LONGEST_RING:
            self.sums = lax.psum_scatter(blocks, "batch", scatter_dimension=0, tiled=False)
            self.done = True
            return
        self.sums, self.done = None, False
        self.ups, self.downs = ring.steps(longer_up)
        self.rising, self.falling = self.own(self.ups), self.own(-self.downs)

    def own(self, offset):
        return lax.dynamic_index_in_dim(self.blocks, self.ring.at(offset), 0, keepdims=False)

    def step(self, later=None):
        if self.done:
            return later
        k = self.hop
        if k < self.ups:
            self.rising = lax.ppermute(self.rising, "batch", self.ring.up)
        if k < self.downs:
            self.falling = lax.ppermute(self.falling, "batch", self.ring.down)
        if later is not None:
            self.rising, self.falling, later = lax.optimization_barrier(
                (self.rising, self.falling, later)
            )
        if k < self.ups - 1:
            self.rising = self.rising + self.own(self.ups - 1 - k)
        if k < self.downs - 1:
            self.falling = self.falling + self.own(-(self.downs - 1 - k))
        self.hop += 1
        self.done = self.hop == max(self.ups, self.downs)
        return later

    def result(self):
        while not self.done:
            self.step()
        return self.sums if self.sums is not None else self.own(0) + self.rising + self.falling


def sums_of(values, others):
    return jnp.stack([jnp.sum(values, axis=0), jnp.sum(values * others, axis=0)])


def norm_forward(values, total, gain, bias, count):
    center = total[0] / count
    inverse = lax.rsqrt(total[1] / count - center * center + EPSILON)
    hat = (values - center) * inverse
    return hat, hat * gain + bias, inverse


def norm_backward(d_out, hat, inverse, gain, count, direct):
    sums = sum_batch(jnp.stack([jnp.sum(d_out * hat, axis=0), jnp.sum(d_out, axis=0)]), direct)
    d_values = inverse * gain * (d_out - sums[1] / count - hat * (sums[0] / count))
    return d_values, sums


def shards(
    features,
    reduce_weight,
    reduce_norm,
    dilate_weight,
    dilate_norm,
    expand_weight,
    expand_norm,
    depth_head,
    segment_head,
    normal_head,
    contour_head,
    depth_message,
    segment_message,
    normal_message,
    contour_message,
    depth_gate,
    segment_gate,
    classifier,
    depth_valid,
    labels,
    block_cotangent,
    depth_cotangent,
):
    row, batch = lax.axis_index("rows"), lax.axis_index("batch")
    nrows, nbatch = lax.axis_size("rows"), lax.axis_size("batch")
    ring = Ring(batch)
    _, local_height, breadth, wide = features.shape
    mid = reduce_weight.shape[1]
    part = mid // nrows
    quarter = local_height * breadth
    height = local_height * nrows
    pixels = quarter * nrows
    count = float(pixels * nbatch)
    factor = count ** (-0.5)
    classes = classifier.shape[1]
    held = dilate_weight.shape[0]
    grain = math.gcd(held, mid) // nrows
    groups = held // (nrows * grain)
    wide_held = wide // nbatch
    wide_part = wide_held // nrows
    mid_held = mid // nbatch

    def row_slice(array, dim):
        size = array.shape[dim] // nrows
        return lax.dynamic_slice_in_dim(array, row * size, size, dim)

    channel = jnp.arange(mid)
    slot = jnp.arange(part)
    mine = (slot // grain) * (nrows * grain) + row * grain + slot % grain
    pick = (channel[:, None] == mine[None, :]).astype(jnp.float32)
    split = jnp.arange(mid)
    natural = ((split % part) // grain) * (nrows * grain) + (split // part) * grain + split % grain
    mix = (natural[:, None] == channel[None, :]).astype(jnp.bfloat16)
    here = row.astype(jnp.int32).reshape(1)

    def to_narrow(array):
        return jnp.concatenate(
            [array[:, i * part : (i + 1) * part] for i in range(nrows)], axis=0
        )

    def from_narrow(array):
        size = array.shape[1] // nrows
        return jnp.concatenate([array[:, i * size : (i + 1) * size] for i in range(nrows)], axis=2)

    tiny_width = max(mid_held, wide_part)

    def tiny(array):
        return jnp.pad(array, ((0, 0), (0, tiny_width - array.shape[1])))

    heads_mine = jnp.concatenate(
        [
            product(head, pick, 1, 0, EXACT)
            for head in (segment_head, normal_head, depth_head, contour_head)
        ],
        axis=1,
    )
    heads_full = lax.all_gather(heads_mine, "batch", axis=0, tiled=True)

    def message_runs(array):
        runs = array.reshape(groups, nrows, grain, mid)
        return lax.dynamic_index_in_dim(runs, row, 1, keepdims=True)

    def message_pair(first, second):
        return jnp.concatenate([message_runs(first), message_runs(second)], axis=1)

    run = grain if grain % 8 == 0 else part
    segment_pair_mine = message_pair(segment_message, contour_message).reshape(held // 2, mid)
    depth_pair_mine = message_pair(depth_message, normal_message).reshape(held // 2, mid)
    segment_pair_w, depth_pair_w = [
        regroup(
            lax.all_gather(mine, "batch", axis=0, tiled=True).reshape(
                nbatch * groups, 2, grain, mid
            ),
            run,
        )
        for mine in (segment_pair_mine, depth_pair_mine)
    ]

    expand_norm_mine = lax.dynamic_index_in_dim(
        expand_norm.reshape(2, nrows, wide_part), row, 1, keepdims=False
    )
    params = jnp.concatenate([tiny(reduce_norm), tiny(dilate_norm), tiny(expand_norm_mine)], axis=0)
    params = jnp.pad(params, ((0, 2), (0, part - tiny_width)))
    expand_mine = lax.dynamic_index_in_dim(
        expand_weight.reshape(mid_held, nbatch, nrows, wide_part), row, 2, keepdims=False
    ).reshape(mid_held, nbatch * wide_part)
    class_lanes = -(-classes // part) * part

    def packed(pieces):
        spans, start = {}, 0
        for name, piece in pieces.items():
            spans[name] = slice(start, start + piece.shape[0])
            start += piece.shape[0]
        return jnp.concatenate(list(pieces.values()), axis=0), spans

    first_mine, first_spans = packed(
        {
            "reduce": to_narrow(row_slice(reduce_weight, 0)),
            "params": params,
            "dilate": row_slice(dilate_weight, 1),
        }
    )
    first_all, _ = ring.gather(first_mine, True)
    reduce_full = from_narrow(first_all[:, first_spans["reduce"]]).reshape(nbatch * wide_part, mid)
    params_all = first_all[:, first_spans["params"]]
    dilate_full = first_all[:, first_spans["dilate"]].reshape(nbatch * held, part)

    def all_params(pair, size):
        return jnp.transpose(params_all[:, pair : pair + 2, :size], (1, 0, 2)).reshape(2, nbatch * size)

    reduce_gain, reduce_bias = row_slice(all_params(0, mid_held), 1)
    dilate_gain, dilate_bias = row_slice(all_params(2, mid_held), 1)
    expand_gain, expand_bias = all_params(4, wide_part)

    spread_by_kernel = wide_part == 64 and part % 128 == 0

    def spread_wide(array):
        if spread_by_kernel:
            (blocks,) = single_call(
                spread_kernel, (here, array), [(nrows, quarter, wide // nrows)], [], 1
            )
            blocks = [blocks[key] for key in range(4)]
        else:
            split_blocks = jnp.transpose(array.reshape(quarter, nbatch, nrows, wide_part), (2, 0, 1, 3))
            split_blocks = split_blocks.reshape(nrows, quarter, nbatch * wide_part)
            blocks = [
                lax.dynamic_index_in_dim(split_blocks, row ^ key, 0, keepdims=False)
                for key in range(4)
            ]
        return jnp.concatenate(in_order(exchange_keyed(blocks), row), axis=0)

    def exchange_wide(array):
        blocks = array.reshape(nrows, quarter, nbatch * wide_part)
        return exchange_keyed(
            [lax.dynamic_index_in_dim(blocks, row ^ key, 0, keepdims=False) for key in range(4)]
        )

    def collect_wide(got):
        if spread_by_kernel:
            (out,) = single_call(
                collect_kernel,
                (here, *got),
                [(quarter, wide)],
                [(nrows, quarter, wide // nrows)],
                1,
            )
        else:
            out = jnp.stack(in_order(got, row)).reshape(nrows, quarter, nbatch, wide_part)
            out = jnp.transpose(out, (1, 2, 0, 3))
        return out.reshape(1, local_height, breadth, wide)

    def image_of(array):
        return array.reshape(height, breadth, array.shape[-1])

    features, _ = lax.optimization_barrier((features, (heads_mine, segment_pair_mine, first_mine)))
    inputs = spread_wide(features.reshape(quarter, wide))

    valid = depth_valid.astype(jnp.float32).reshape(quarter, 1)
    keep, give = single_call(
        split_product_kernel,
        (here, inputs, reduce_full, jnp.full((1, part), jnp.sum(valid))),
        [(2, pixels + 8, part)] * 2,
        [(pixels, mid)],
        2 * pixels * mid * mid,
    )
    mine_terms, got_terms = scatter_end(keep, give)
    pre_reduce = mine_terms + got_terms
    valid_row = pre_reduce[pixels]
    pre_reduce = pre_reduce[:pixels]
    total_one = sum_batch(jnp.concatenate([sums_of(pre_reduce, pre_reduce), valid_row[None]]))
    scale = valid * (count / total_one[2, 0])
    hat_one, normed_one, inverse_one = norm_forward(
        pre_reduce, total_one, reduce_gain, reduce_bias, count
    )
    pre_dilate, mid_in = joined_conv(
        here, gather_keyed(image_of(jax.nn.silu(normed_one))), dilate_full, 2
    )
    total_two = sum_batch(sums_of(pre_dilate, pre_dilate))
    total_two, heads_full = lax.optimization_barrier((total_two, heads_full))
    hat_two, normed_two, inverse_two = norm_forward(
        pre_dilate, total_two, dilate_gain, dilate_bias, count
    )

    beside = mid // class_lanes
    square_mine, square_spans = packed(
        {
            "depth_gate": depth_gate,
            "segment_gate": segment_gate,
            "expand": expand_mine,
            "classifier": jnp.pad(classifier, ((0, 0), (0, class_lanes - classes)))
            .reshape(beside, mid_held // beside, class_lanes)
            .transpose(1, 0, 2)
            .reshape(mid_held // beside, mid),
        }
    )
    square_mine, inverse_two = lax.optimization_barrier((square_mine, inverse_two))
    feats, mid_out, pairs = joined_conv(
        here, gather_keyed(image_of(jax.nn.silu(normed_two))), heads_full, 1, True
    )
    square_all, feats = ring.gather(square_mine, False, feats, 2)
    square_all, segment_pair_w = lax.optimization_barrier((square_all, segment_pair_w))
    depth_gate_w, segment_gate_w, expand_w = [
        square_all[:, square_spans[name]].reshape(mid, mid)
        for name in ("depth_gate", "segment_gate", "expand")
    ]
    classifier_w = (
        square_all[:, square_spans["classifier"]]
        .reshape(nbatch, mid_held // beside, beside, class_lanes)
        .transpose(0, 2, 1, 3)
        .reshape(mid, class_lanes)
    )
    feats_image = image_of(feats)

    segment_mine, segment_got = scatter_end(*note_forward(here, feats_image, 1, segment_pair_w))
    pairs_got = jnp.stack(exchange_keyed([pairs[key] for key in range(4)]))
    block_cotangent, _ = lax.optimization_barrier((block_cotangent, feats))
    cotangent = spread_wide(block_cotangent.reshape(quarter, wide))
    pairs_got, segment_mine, cotangent = lax.optimization_barrier((pairs_got, segment_mine, cotangent))
    depth_cotangent = depth_cotangent.reshape(quarter, mid)
    both, one_map = (2 * quarter, mid), (quarter, mid)
    feat_pair, open_pair, d_depth_note = single_call(
        gates_kernel,
        (here, pairs_got, mix, depth_gate_w, segment_gate_w, depth_cotangent, scale),
        [both, both, one_map],
        [both],
        8 * quarter * mid * mid,
    )

    def segment_body(*refs):
        segment_kernel(classes, *refs)

    segment_stream, d_segment_note, direct_segment, segment_gate_grad, classifier_grad = single_call(
        segment_body,
        (
            here,
            segment_mine,
            segment_got,
            feat_pair[quarter:],
            open_pair[quarter:],
            labels.reshape(quarter, 1),
            classifier_w,
            segment_gate_w,
            mix,
        ),
        [one_map, one_map, (4, quarter, part), (mid, mid), (mid, class_lanes)],
        [one_map],
        8 * quarter * mid * mid,
    )

    def lines(array):
        return array.reshape(local_height, breadth, mid)

    d_depth_blocks, d_segment_note = lax.optimization_barrier(
        (gather_keyed(lines(d_depth_note)), d_segment_note)
    )
    message_grads, d_depth_image = note_grad(here, feats, 0, d_depth_blocks, run)
    message_grads, d_segment_image = note_grad(
        here, feats, 1, gather_keyed(lines(d_segment_note)), run, message_grads
    )
    message_sums = lax.psum_scatter(
        regroup(message_grads, grain).reshape(-1, mid), "batch", scatter_dimension=0, tiled=True
    )
    segment_back = note_back(d_segment_image, segment_pair_w)
    depth_mine, depth_got = scatter_end(*note_forward(here, feats_image, 0, depth_pair_w))
    depth_back = note_back(d_depth_image, depth_pair_w)
    depth_stream, direct_both, depth_gate_grad = single_call(
        depth_kernel,
        (
            here,
            depth_mine,
            depth_got,
            feat_pair[:quarter],
            open_pair[:quarter],
            depth_cotangent,
            scale,
            depth_gate_w,
            mix,
            direct_segment,
        ),
        [one_map, (4, 2 * quarter, part), (mid, mid)],
        [one_map],
        8 * quarter * mid * mid,
    )
    direct_got = jnp.stack(exchange_keyed([direct_both[key] for key in range(4)]))
    flat_mid_out = mid_out.reshape(pixels, mid)
    heads_grad, d_feats = heads_grad_of(
        here,
        flat_mid_out,
        image_of(depth_back),
        image_of(segment_back),
        direct_got.reshape(4, 2 * local_height, breadth, part),
    )
    heads_sums = lax.psum_scatter(heads_grad, "batch", scatter_dimension=0, tiled=True)

    pre_expand = product(flat_mid_out, expand_w, 1, 0)
    hat_three, normed_three, inverse_three = norm_forward(
        pre_expand, sum_batch(sums_of(pre_expand, pre_expand)), expand_gain, expand_bias, count
    )
    summed = normed_three + inputs
    block_blocks = exchange_wide(jax.nn.silu(summed))
    d_summed = cotangent * silu_grad(summed)
    d_pre_expand, expand_sums = norm_backward(
        d_summed, hat_three, inverse_three, expand_gain, count, False
    )

    expand_grad = product(flat_mid_out, d_pre_expand, 0, 0).reshape(nbatch, mid_held, mid)

    gate_terms = jnp.stack(
        [
            depth_gate_grad,
            segment_gate_grad,
            jnp.pad(classifier_grad, ((0, 0), (0, mid - class_lanes))),
        ]
    )
    gate_rows = mid_held // nrows
    gate_terms = jnp.transpose(gate_terms.reshape(3, nbatch, nrows, gate_rows, mid), (2, 1, 0, 3, 4))
    gate_sums = scatter_rows(gate_terms, row).reshape(nbatch, 3 * gate_rows, mid)

    keep, give = conv_back(here, d_feats, heads_full, 1)
    keep, give = single_call(
        expand_back_kernel,
        (here, d_pre_expand, expand_w, keep, give),
        [(2, pixels, part)] * 2,
        [(pixels, mid)],
        2 * pixels * mid * mid,
    )
    mine_terms, got_terms = scatter_end(keep, give)
    mine_terms, block_blocks = lax.optimization_barrier((mine_terms, block_blocks))
    block_out = collect_wide(block_blocks)
    d_pre_dilate, dilate_sums = norm_backward(
        (mine_terms + got_terms) * silu_grad(normed_two), hat_two, inverse_two, dilate_gain, count, False
    )
    d_dilate_image = image_of(d_pre_dilate)
    mine_terms, got_terms = scatter_end(*conv_back(here, d_dilate_image, dilate_full, 2))
    d_pre_reduce, reduce_sums = norm_backward(
        (mine_terms + got_terms) * silu_grad(normed_one), hat_one, inverse_one, reduce_gain, count, False
    )
    d_pre_reduce, message_sums = lax.optimization_barrier((d_pre_reduce, message_sums))
    reduce_grad, features_back = single_call(
        reduce_back_kernel,
        (here, *gather_keyed(d_pre_reduce), inputs, reduce_full, d_summed),
        [(mid, mid), (pixels, mid)],
        [(pixels, mid)],
        4 * pixels * mid * mid,
    )
    dilate_grad = conv_grad(mid_in.reshape(pixels, mid), d_dilate_image, 2).reshape(
        nbatch, held, part
    )
    narrow = held // nrows
    square_grad = jnp.concatenate(
        [
            jnp.concatenate(
                [dilate_grad[:, i * narrow : (i + 1) * narrow] for i in range(nrows)], axis=2
            ),
            expand_grad,
            gate_sums,
            reduce_grad.reshape(nbatch, wide_part, mid),
        ],
        axis=1,
    )
    square_grad, reduce_sums = lax.optimization_barrier((square_grad, reduce_sums))
    hops = Hops(ring, square_grad, False)
    hops.step()
    hops.step()
    message_blocks = hops.step(gather_keyed(message_sums * factor))
    features_blocks = hops.step(exchange_wide(features_back))
    square_sums = hops.result()
    features_grad = collect_wide(features_blocks)

    messages_out = jnp.stack(in_order(message_blocks, row)).reshape(
        nrows, groups, 4, grain, mid
    )

    def message_out(index):
        return jnp.transpose(messages_out[:, :, index], (1, 0, 2, 3)).reshape(held, mid)

    expand_mine_sums = lax.dynamic_slice_in_dim(expand_sums, batch * wide_part, wide_part, 1)
    norm_sums = jnp.concatenate(
        [
            jnp.pad(sums, ((0, 0), (0, mid - sums.shape[1])))
            for sums in (reduce_sums, dilate_sums, expand_mine_sums)
        ],
        axis=0,
    )
    small = jnp.concatenate([square_sums, jnp.pad(norm_sums, ((0, 2), (0, 0)))], axis=0) * factor
    small_blocks = gather_keyed(small)
    small_got = in_order(small_blocks, row)
    segment_out, normal_out, depth_out, contour_out = single_call(
        heads_out_kernel,
        (here, *gather_keyed(heads_sums * factor), mix),
        [(held, mid)] * 4,
        [(held, mid)],
        8 * held * mid * mid,
    )

    squares_got = jnp.stack([block[narrow : narrow + mid_held + 3 * gate_rows] for block in small_got])
    dilate_out = jnp.concatenate(
        [
            jnp.concatenate(
                [block[:narrow, i * part : (i + 1) * part] for i in range(nrows)], axis=0
            )
            for block in small_got
        ],
        axis=1,
    )
    expand_out = jnp.transpose(
        squares_got[:, :mid_held].reshape(nrows, mid_held, nbatch, wide_part), (1, 2, 0, 3)
    ).reshape(mid_held, wide)

    def gate_out(index):
        start = mid_held + index * gate_rows
        return squares_got[:, start : start + gate_rows].reshape(mid_held, mid)

    norms_got = [block[-8:] for block in small_got]

    def norm_out(start):
        full = jnp.concatenate([block[start : start + 2, :part] for block in norms_got], axis=1)
        return lax.dynamic_slice_in_dim(full, batch * mid_held, mid_held, 1)

    expand_norm_out = jnp.concatenate([block[4:6, :wide_part] for block in norms_got], axis=1)
    reduce_start = narrow + mid_held + 3 * gate_rows
    reduce_got = jnp.concatenate(
        [block[reduce_start : reduce_start + wide_part] for block in small_got], axis=0
    )

    return (
        block_out,
        depth_stream.reshape(1, local_height, breadth, mid),
        segment_stream.reshape(1, local_height, breadth, mid),
        features_grad,
        reduce_got,
        norm_out(0),
        dilate_out,
        norm_out(2),
        expand_out,
        expand_norm_out,
        depth_out,
        segment_out,
        normal_out,
        contour_out,
        message_out(0),
        message_out(2),
        message_out(1),
        message_out(3),
        gate_out(0),
        gate_out(1),
        gate_out(2)[:, :classes],
    )


def solution(mesh):
    pixels = P("batch", "rows", None, None)
    plane = P("batch", "rows", None)
    weight = P("batch", None)
    norm = P(None, "batch")
    in_specs = (
        (pixels, weight, norm, weight, norm, weight, norm) + (weight,) * 11 + (plane, plane, pixels, pixels)
    )
    out_specs = (pixels,) * 4 + (weight, norm) * 3 + (weight,) * 11
    return jax.shard_map(shards, mesh=mesh, in_specs=in_specs, out_specs=out_specs, check_vma=False)
```
